128 devices in a mesh: wide: 32 (over y, z, core), narrow: 4 (over x).
Axes of the slice: x: 4, y: 4, z: 4, core: 2. Of those that a mesh axis runs over, the one named last changes fastest.
Arguments:
- image: bfloat16 [128, 4096, 512], P('narrow', 'wide'), may hold values from -7 to 7
- third_norm_gain: float32 [512], replicated, may hold values from 0.5 to 1.5
- third_norm_bias: float32 [512], replicated, may hold values from -3 to 3
- third_in_proj: bfloat16 [512, 1536], replicated, may hold values from -3 to 3
- third_in_bias: float32 [1536], replicated, may hold values from -3 to 3
- third_out_proj: bfloat16 [512, 512], replicated, may hold values from -0.25 to 0.25
- third_out_bias: float32 [512], replicated, may hold values from -3 to 3
- window_keep: int32 [8, 256], P('narrow', 'wide'), may hold values 0 or 1
- merge_gain: float32 [2048], replicated, may hold values from 0.5 to 1.5
- merge_bias: float32 [2048], replicated, may hold values from -3 to 3
- merge_weight: bfloat16 [2048, 1024], replicated, may hold values from -0.125 to 0.125
- fourth_norm_gain: float32 [1024], replicated, may hold values from 0.5 to 1.5
- fourth_norm_bias: float32 [1024], replicated, may hold values from -3 to 3
- fourth_in_proj: bfloat16 [1024, 3072], replicated, may hold values from -3 to 3
- fourth_in_bias: float32 [3072], replicated, may hold values from -3 to 3
- fourth_out_proj: bfloat16 [1024, 1024], replicated, may hold values from -0.1875 to 0.1875
- fourth_out_bias: float32 [1024], replicated, may hold values from -3 to 3
- window_route: int32 [4, 128], P('narrow'), may hold values from 0 to 2, as said below
Outputs:
- merged: bfloat16 [64, 2048, 1024], P('narrow', 'wide')
- section_four: bfloat16 [4, 64, 256, 1024], P('narrow', 'wide')
The draws below stay inside these ranges and needn't reach their ends.
Inputs may be any that keep to these rules, and one draw needn't show every extreme that they name: window_route is 0 for a pruned section-4 window, 1 for a kept one computed in its own column group, 2 for a kept one computed by the next column group (the last wrapping to the first); in every row and column group the windows with 1 plus those with 2 in the previous group number at most 2, and exactly 2 in some.
All inputs are finite; a program needn't handle non-finite values. No bound on the sum of `window_keep` on one device may be relied on, other than what follows from the above.
Results may differ from the reference program's by a relative error of at most 0.012.
Values may be sent and summed in bfloat16 or wider, within the bound.
No kernel may reach another device: no remote copies, remote signals or barrier semaphores. Data moves between devices by JAX's collectives and lax.ppermute only.
A program may use at most 192 MiB of HBM per device.

```python
import jax
import jax.numpy as jnp
from jax import lax

D = 512
HEADS_D = 16
E = 1024
HEADS_E = 32
WIN = 16
WIN_COLS = 8
SHIFT = 8
GRID_ROWS = 128
GRID_COLS = 4096
TOP_WINS = 4
SLOTS_DEV = 2
SLOTS = 64
N_WIDE = 32
N_NARROW = 4


def drawn_projection(key, fan_in):
    return jax.random.truncated_normal(key, -6.0, 6.0, (fan_in, 3 * fan_in), jnp.float32) * fan_in ** (-0.5)


def draw_image(key, part):
    key = jax.random.fold_in(key, 1)
    shape = (GRID_ROWS, GRID_COLS, D)
    return jax.random.truncated_normal(key, -6.0, 6.0, shape, jnp.float32).astype(jnp.bfloat16)


def draw_third_in_proj(key, part):
    key = jax.random.fold_in(key, 2)
    return drawn_projection(key, D).astype(jnp.bfloat16)


def draw_fourth_in_proj(key, part):
    key = jax.random.fold_in(key, 3)
    return drawn_projection(key, E).astype(jnp.bfloat16)


def draw_window_route(key, part):
    key = jax.random.fold_in(key, 4)
    column = jnp.arange(N_WIDE)[None, :]
    moves = jax.random.randint(jax.random.fold_in(key, 1), (N_NARROW, N_WIDE), 0, SLOTS_DEV + 1)
    moves = jnp.where(column == 0, SLOTS_DEV, moves)
    arriving = jnp.roll(moves, 1, axis=1)
    shortfall = jax.random.randint(jax.random.fold_in(key, 2), (N_NARROW, N_WIDE), 0, 2)
    shortfall = jnp.where(column == 0, 0, shortfall)
    staying = jnp.maximum(SLOTS_DEV - arriving - shortfall, 0)
    scores = jax.random.randint(jax.random.fold_in(key, 3), (N_NARROW, N_WIDE, TOP_WINS), 0, 1 << 20) * TOP_WINS + jnp.arange(TOP_WINS)
    order = jnp.argsort(scores, axis=-1)
    ranks = jnp.argsort(order, axis=-1)
    classes = jnp.where(ranks < staying[:, :, None], 1, jnp.where(ranks < (staying + moves)[:, :, None], 2, 0))
    return classes.reshape(N_NARROW, N_WIDE * TOP_WINS).astype(jnp.int32)


def touch_ends(values, own_key, smallest, high):
    place = [jax.random.randint(jax.random.fold_in(own_key, axis), (), 0, length) for axis, length in enumerate(values.shape)]
    widest = values.shape.index(max(values.shape))
    beside = place[:widest] + [(place[widest] + 1) % values.shape[widest]] + place[widest + 1:]
    return values.at[tuple(place)].set(smallest).at[tuple(beside)].set(high)


def normal_values(key, shape, scale, limit, held_as=jnp.bfloat16):
    drawn = scale * jax.random.normal(key, shape, jnp.float32)
    return jnp.clip(drawn, min=-limit, max=limit).astype(held_as)


def setup_inputs(seed: int = 0) -> dict:
    key_list = jax.random.split(jax.random.key(seed), 19)
    return {
        "image": draw_image(jax.random.fold_in(key_list[18], 71), 0),
        "third_norm_gain": jnp.clip(1.0 + 0.1 * jax.random.normal(key_list[1], (D,), jnp.float32), 0.5, 1.5),
        "third_norm_bias": normal_values(key_list[2], (D,), 0.5, 3.0, jnp.float32),
        "third_in_proj": draw_third_in_proj(jax.random.fold_in(key_list[18], 71), 0),
        "third_in_bias": normal_values(key_list[4], (3 * D,), 0.5, 3.0, jnp.float32),
        "third_out_proj": normal_values(key_list[5], (D, D), D ** -0.5, 0.25),
        "third_out_bias": normal_values(key_list[6], (D,), 0.5, 3.0, jnp.float32),
        "window_keep": touch_ends((jax.random.randint(key_list[7], (2 * N_NARROW, WIN_COLS * N_WIDE), 0, 3) < 2).astype(jnp.int32), jax.random.fold_in(key_list[7], 1), 0, 1),
        "merge_gain": jnp.clip(1.0 + 0.1 * jax.random.normal(key_list[8], (4 * D,), jnp.float32), 0.5, 1.5),
        "merge_bias": normal_values(key_list[9], (4 * D,), 0.5, 3.0, jnp.float32),
        "merge_weight": normal_values(key_list[10], (4 * D, E), (4 * D) ** -0.5, 0.125),
        "fourth_norm_gain": jnp.clip(1.0 + 0.1 * jax.random.normal(key_list[11], (E,), jnp.float32), 0.5, 1.5),
        "fourth_norm_bias": normal_values(key_list[12], (E,), 0.5, 3.0, jnp.float32),
        "fourth_in_proj": draw_fourth_in_proj(jax.random.fold_in(key_list[18], 71), 0),
        "fourth_in_bias": normal_values(key_list[14], (3 * E,), 0.5, 3.0, jnp.float32),
        "fourth_out_proj": normal_values(key_list[15], (E, E), E ** -0.5, 0.1875),
        "fourth_out_bias": normal_values(key_list[16], (E,), 0.5, 3.0, jnp.float32),
        "window_route": draw_window_route(jax.random.fold_in(key_list[18], 71), 0),
    }


EPSILON = 1e-05

def layer_norm(values, norm_gain, norm_shift):
    values = values.astype(jnp.float32)
    center = lax.optimization_barrier(jnp.mean(values, axis=-1, keepdims=True))
    offsets = values - center
    spread = lax.optimization_barrier(jnp.mean(offsets * offsets, axis=-1, keepdims=True))
    return (offsets * lax.rsqrt(spread + EPSILON) * norm_gain + norm_shift).astype(jnp.bfloat16)

def attention_block(patch_tokens, allowed, norm_gain, norm_shift, in_proj, in_bias, out_proj, out_bias, head_count):
    patch_count, patch_length, feature_width = patch_tokens.shape
    head_size = feature_width // head_count
    normed = layer_norm(patch_tokens, norm_gain, norm_shift)
    packed = jnp.einsum('nld,de->nle', normed.astype(jnp.float32), in_proj.astype(jnp.float32)) + in_bias
    packed = packed.astype(jnp.bfloat16).reshape(patch_count, patch_length, 3, head_count, head_size)
    scores = jnp.einsum('nqhd,nkhd->nhqk', packed[:, :, 0].astype(jnp.float32), packed[:, :, 1].astype(jnp.float32))
    scores = scores * head_size ** (-0.5)
    if allowed is not None:
        scores = jnp.where(allowed[:, None], scores, -1e+30)
    highest = lax.optimization_barrier(jnp.max(scores, axis=-1, keepdims=True))
    weights = jnp.exp(scores - highest)
    weights_low = (weights / lax.optimization_barrier(jnp.sum(weights, axis=-1, keepdims=True))).astype(jnp.bfloat16)
    context = jnp.einsum('nhqk,nkhd->nqhd', weights_low.astype(jnp.float32), packed[:, :, 2].astype(jnp.float32))
    context = context.astype(jnp.bfloat16).reshape(patch_count, patch_length, feature_width)
    output = jnp.einsum('nld,de->nle', context.astype(jnp.float32), out_proj.astype(jnp.float32)) + out_bias
    return (output + patch_tokens.astype(jnp.float32)).astype(jnp.bfloat16)

def to_windows(layout, window):
    height, breadth, features = layout.shape
    blocks = layout.reshape(height // window, window, breadth // window, window, features)
    return blocks.transpose(0, 2, 1, 3, 4).reshape(-1, window * window, features)

def from_windows(patch_tokens, height, breadth, window):
    features = patch_tokens.shape[-1]
    blocks = patch_tokens.reshape(height // window, breadth // window, window, window, features)
    return blocks.transpose(0, 2, 1, 3, 4).reshape(height, breadth, features)

def merged_token_rows(layout, merge_gain, merge_bias, merge_weight):
    grouped = jnp.concatenate([layout[0::2, 0::2], layout[1::2, 0::2], layout[0::2, 1::2], layout[1::2, 1::2]], axis=-1)
    normed = layer_norm(grouped, merge_gain, merge_bias)
    height, breadth, features = normed.shape
    final_output = jnp.dot(normed.reshape(height * breadth, features), merge_weight, preferred_element_type=jnp.float32)
    return final_output.astype(jnp.bfloat16).reshape(height, breadth, -1)

def region_codes(height, breadth, window, margin, row_start, col_start, total_rows, total_cols):
    row_place = row_start + jnp.arange(height, dtype=jnp.int32)
    col_place = col_start + jnp.arange(breadth, dtype=jnp.int32)
    row_code = (row_place >= total_rows - window).astype(jnp.int32) + (row_place >= total_rows - margin).astype(jnp.int32)
    col_code = (col_place >= total_cols - window).astype(jnp.int32) + (col_place >= total_cols - margin).astype(jnp.int32)
    return row_code[:, None] * 3 + col_code[None, :]

def reference(image, third_norm_gain, third_norm_bias, third_in_proj, third_in_bias, third_out_proj, third_out_bias, window_keep, merge_gain, merge_bias, merge_weight, fourth_norm_gain, fourth_norm_bias, fourth_in_proj, fourth_in_bias, fourth_out_proj, fourth_out_bias, window_route):
    rolled = jnp.roll(image, (-SHIFT, -SHIFT), axis=(0, 1))
    region_map = region_codes(GRID_ROWS, GRID_COLS, WIN, SHIFT, 0, 0, GRID_ROWS, GRID_COLS)
    patch_tokens = to_windows(rolled, WIN)
    code_patches = to_windows(region_map[:, :, None], WIN)[:, :, 0]
    allowed = code_patches[:, :, None] == code_patches[:, None, :]

    def section_three(operands):
        return attention_block(operands[0], operands[1], third_norm_gain, third_norm_bias, third_in_proj, third_in_bias, third_out_proj, third_out_bias, HEADS_D)
    attended = lax.map(section_three, (patch_tokens.reshape(-1, WIN_COLS, WIN * WIN, D), allowed.reshape(-1, WIN_COLS, WIN * WIN, WIN * WIN)))
    attended = attended.reshape(patch_tokens.shape)
    keep_flags = window_keep.reshape(-1)[:, None, None] == 1
    shifted_out = from_windows(jnp.where(keep_flags, attended, patch_tokens), GRID_ROWS, GRID_COLS, WIN)
    layer_three = jnp.roll(shifted_out, (SHIFT, SHIFT), axis=(0, 1))
    merged = merged_token_rows(layer_three, merge_gain, merge_bias, merge_weight)
    top_windows = merged.reshape(N_NARROW, WIN, N_WIDE * TOP_WINS, WIN, E).transpose(0, 2, 1, 3, 4)
    top_windows = top_windows.reshape(N_NARROW, N_WIDE, TOP_WINS, WIN * WIN, E)
    classes = window_route.reshape(N_NARROW, N_WIDE, TOP_WINS)
    home_flags = classes == 1
    moved_flags = jnp.roll(classes == 2, 1, axis=1)
    candidates = jnp.concatenate([top_windows, jnp.roll(top_windows, 1, axis=1)], axis=2)
    take_flags = jnp.concatenate([home_flags, moved_flags], axis=2)
    slot_ranks = jnp.cumsum(take_flags.astype(jnp.int32), axis=2) - 1
    filled_slots = lax.optimization_barrier(jnp.sum(take_flags.astype(jnp.int32), axis=2))
    slot_list = []
    for slot_index in range(SLOTS_DEV):
        onehot = take_flags & (slot_ranks == slot_index)
        picked = lax.optimization_barrier(jnp.sum(jnp.where(onehot[:, :, :, None, None], candidates, jnp.zeros_like(candidates)), axis=2))
        slot_list.append(picked.astype(jnp.bfloat16))
    slot_tokens = jnp.stack(slot_list, axis=2).reshape(N_NARROW, SLOTS, WIN * WIN, E)

    def section_four(slot_row):
        return attention_block(slot_row, None, fourth_norm_gain, fourth_norm_bias, fourth_in_proj, fourth_in_bias, fourth_out_proj, fourth_out_bias, HEADS_E)
    finished = lax.map(section_four, slot_tokens)
    occupied = (jnp.arange(SLOTS_DEV, dtype=jnp.int32)[None, None, :] < filled_slots[:, :, None]).reshape(N_NARROW, SLOTS)
    result_four = jnp.where(occupied[:, :, None, None], finished, jnp.zeros_like(finished))
    return (merged, result_four)
```

```python
import functools

import jax
import jax.numpy as jnp
from jax import lax
from jax.experimental import pallas as pl
from jax.experimental.pallas import tpu as pltpu
from jax.sharding import PartitionSpec as P

D = 512
HEADS_D = 16
E = 1024
HEADS_E = 32
WIN = 16
SHIFT = 8
HEAD = 32
PACK = 4
EPSILON = 1e-05
LOG2E = 1.4426950408889634
QSCALE = HEAD ** (-0.5) * LOG2E
BF16 = jnp.bfloat16
F32 = jnp.float32
VMEM_LIMIT = 60 * 2**20


def matmul(a, b):
    return jnp.dot(a, b, preferred_element_type=F32)


def layer_norm(values, gain, bias):
    center = jnp.mean(values, axis=-1, keepdims=True)
    offsets = values - center
    spread = jnp.mean(offsets * offsets, axis=-1, keepdims=True)
    return (offsets * lax.rsqrt(spread + EPSILON) * gain + bias).astype(BF16)


def attend(q, k, v):
    count = q.shape[0]
    lane = lax.broadcasted_iota(jnp.int32, (count, PACK * HEAD), 1)
    stacked = jnp.concatenate(
        [jnp.where((lane >= HEAD * h) & (lane < HEAD * h + HEAD), q, 0) for h in range(PACK)], axis=0
    )
    scores = lax.dot_general(stacked, k, (((1,), (1,)), ((), ())), preferred_element_type=F32)
    weights = jnp.exp2(scores - jnp.max(scores, axis=1, keepdims=True)).astype(BF16)
    sums = matmul(weights, jnp.concatenate([v, jnp.ones_like(v)], axis=1))
    total = sums[:count]
    lane = lax.broadcasted_iota(jnp.int32, total.shape, 1) % (PACK * HEAD)
    for h in range(1, PACK):
        total = jnp.where(lane >= HEAD * h, sums[count * h : count * (h + 1)], total)
    return (total[:, : PACK * HEAD] / total[:, PACK * HEAD :]).astype(BF16)


def attention_three(tokens, count, refs):
    gain, bias, in_proj, in_bias, out_proj, out_bias = refs
    normed = layer_norm(tokens, gain[...], bias[...])
    q = ((matmul(normed[:count], in_proj[:, :D]) + in_bias[:, :D]) * QSCALE).astype(BF16)
    k = (matmul(normed, in_proj[:, D : 2 * D]) + in_bias[:, D : 2 * D]).astype(BF16)
    v = (matmul(normed, in_proj[:, 2 * D :]) + in_bias[:, 2 * D :]).astype(BF16)
    width = PACK * HEAD
    context = jnp.concatenate(
        [attend(q[:, c : c + width], k[:, c : c + width], v[:, c : c + width]) for c in range(0, D, width)],
        axis=1,
    )
    return (matmul(context, out_proj[...]) + out_bias[...] + tokens[:count]).astype(BF16)


def inner_kernel(keep, image, gain, bias, in_proj, in_bias, out_proj, out_bias, out):
    refs = (gain, bias, in_proj, in_bias, out_proj, out_bias)

    @pl.loop(0, 7)
    def _(j):
        start = pl.multiple_of(j * WIN, WIN)
        wide = image[SHIFT : SHIFT + WIN, pl.ds(start, 2 * WIN), :].astype(F32)
        tokens = wide[:, SHIFT : SHIFT + WIN, :].reshape(WIN * WIN, D)

        @pl.when(keep[1, j + 1] == 1)
        def _():
            out[j] = attention_three(tokens, WIN * WIN, refs)

        @pl.when(keep[1, j + 1] != 1)
        def _():
            out[j] = tokens.astype(BF16)


def outer_kernel(
    place,
    keep,
    route,
    image,
    inner,
    rows_above,
    rows_below,
    cols_left,
    cols_right,
    corner_tl,
    corner_tr,
    corner_bl,
    corner_br,
    gain,
    bias,
    in_proj,
    in_bias,
    out_proj,
    out_bias,
    merge_gain,
    merge_bias,
    merge_weight,
    merged,
    outgoing,
    layer,
    above_below,
    sem,
):
    refs = (gain, bias, in_proj, in_bias, out_proj, out_bias)
    copies = [
        pltpu.make_async_copy(rows_above, above_below.at[0], sem.at[0]),
        pltpu.make_async_copy(rows_below, above_below.at[1], sem.at[1]),
    ]
    for copy in copies:
        copy.start()
    narrow, wide = place[0], place[1]
    at_top, at_bottom = narrow == 0, narrow == place[2] - 1
    at_left, at_right = wide == 0, wide == place[3] - 1

    @pl.loop(0, 7)
    def _(j):
        start = pl.multiple_of(j * WIN + SHIFT, SHIFT)
        values = inner[j].astype(F32).reshape(WIN, WIN, D)
        store(layer, slice(SHIFT, SHIFT + WIN), pl.ds(start, WIN), values)

    def finish(kept, tokens, count, rows, cols, shape):
        @pl.when(kept == 1)
        def _():
            store(layer, rows, cols, attention_three(tokens, count, refs).astype(F32).reshape(shape))

        @pl.when(kept != 1)
        def _():
            store(layer, rows, cols, tokens[:count].reshape(shape))

    for side in range(2):
        own = image[SHIFT : SHIFT + WIN, (0, 7 * WIN)[side] : (WIN, 8 * WIN)[side], :].astype(F32)
        own = own[:, SHIFT * side : SHIFT * side + SHIFT]
        other = (cols_left, cols_right)[side][SHIFT : SHIFT + WIN].astype(F32)
        other = other[:, SHIFT * (1 - side) : SHIFT * (1 - side) + SHIFT]
        other = jnp.where((at_left, at_right)[side], own, other)
        tokens = jnp.concatenate([own.reshape(-1, D), other.reshape(-1, D)], axis=0)
        col = 15 * SHIFT * side
        finish(keep[1, 8 * side], tokens, 128, slice(SHIFT, SHIFT + WIN), slice(col, col + SHIFT), (WIN, SHIFT, D))

    for copy in copies:
        copy.wait()

    @pl.loop(0, 14)
    def _(step):
        side = step // 7
        j = step - 7 * side
        row = side * (3 * SHIFT)
        start = pl.multiple_of(j * WIN, WIN)
        own = image[pl.ds(row, SHIFT), pl.ds(start, 2 * WIN), :].astype(F32)[:, SHIFT : SHIFT + WIN]
        other = above_below[side, :, pl.ds(start, 2 * WIN), :].astype(F32)[:, SHIFT : SHIFT + WIN]
        at_edge = jnp.where(side == 0, at_top, at_bottom)
        other = jnp.where(at_edge, own, other)
        tokens = jnp.concatenate([own.reshape(-1, D), other.reshape(-1, D)], axis=0)
        cols = pl.multiple_of(start + SHIFT, SHIFT)
        finish(
            keep[2 * side, j + 1], tokens, 128, pl.ds(row, SHIFT), pl.ds(cols, WIN), (SHIFT, WIN, D)
        )

    for down in range(2):
        for side in range(2):
            base = (0, 7 * WIN)[side]
            near, far = slice(SHIFT * side, SHIFT * side + SHIFT), slice(SHIFT * (1 - side), SHIFT * (1 - side) + SHIFT)
            row = 3 * SHIFT * down
            own = image[row : row + SHIFT, base : base + WIN, :].astype(F32)[:, near]
            across = above_below[down, :, base : base + WIN, :].astype(F32)[:, near]
            beside = (cols_left, cols_right)[side][row : row + SHIFT].astype(F32)[:, far]
            corner = ((corner_tl, corner_tr), (corner_bl, corner_br))[down][side][...].astype(F32)[:, far]
            edge_row, edge_col = (at_top, at_bottom)[down], (at_left, at_right)[side]
            across = jnp.where(edge_row, own, across)
            beside = jnp.where(edge_col, own, beside)
            corner = jnp.where(edge_col, across, jnp.where(edge_row, beside, corner))
            tokens = jnp.concatenate([t.reshape(-1, D) for t in (own, across, beside, corner)], axis=0)
            col = 15 * SHIFT * side
            finish(
                keep[2 * down, 8 * side],
                tokens,
                64,
                slice(row, row + SHIFT),
                slice(col, col + SHIFT),
                (SHIFT, SHIFT, D),
            )

    @pl.loop(0, 4)
    def _(i):
        parts = []
        for odd_col in range(2):
            for odd_row in range(2):
                parts.append(
                    jnp.concatenate(
                        [load_strided(layer, 8 * i + 2 * r + odd_row, odd_col) for r in range(4)], axis=0
                    )
                )
        grouped = jnp.concatenate(parts, axis=1)
        normed = layer_norm(grouped, merge_gain[...], merge_bias[...])
        result = matmul(normed, merge_weight[...]).astype(BF16)
        merged[pl.ds(4 * i, 4)] = result.reshape(4, 64, E)

    found = 0
    chosen = [0, 0]
    for j in range(4):
        moves = route[0, 4 * wide + j] == 2
        for slot in range(2):
            chosen[slot] = jnp.where(moves & (found == slot), j, chosen[slot])
        found = found + moves.astype(jnp.int32)
    for slot in range(2):
        start = pl.multiple_of(chosen[slot] * WIN, WIN)
        outgoing[slot] = merged[:, pl.ds(start, WIN), :].reshape(WIN * WIN, E)


def store(layer, rows, cols, values):
    for c in range(4):
        layer[c, rows, cols, :] = values[:, :, 128 * c : 128 * c + 128]


def load_strided(layer, row, odd_col):
    return jnp.concatenate([layer[c, row, pl.ds(odd_col, 64, stride=2), :] for c in range(4)], axis=1)


def top_kernel(
    place, route, merged, incoming, gain, bias, in_proj, in_bias, out_proj, out_bias, out, tokens_ref, sem
):
    wide, groups = place[1], place[3]
    before = jnp.where(wide == 0, groups - 1, wide - 1)
    homes = 0
    arriving = 0
    chosen = [0, 0]
    for j in range(4):
        stays = route[0, 4 * wide + j] == 1
        for slot in range(2):
            chosen[slot] = jnp.where(stays & (homes == slot), j, chosen[slot])
        homes = homes + stays.astype(jnp.int32)
        arriving = arriving + (route[0, 4 * before + j] == 2).astype(jnp.int32)
    width = PACK * HEAD
    for slot in range(2):
        filled = slot < homes + arriving

        @pl.when(slot < homes)
        def _():
            start = pl.multiple_of(chosen[slot] * WIN, WIN)
            copy = pltpu.make_async_copy(merged.at[:, pl.ds(start, WIN), :], tokens_ref, sem)
            copy.start()
            copy.wait()

        @pl.when((slot >= homes) & filled)
        def _():
            source = jnp.clip(slot - homes, 0, 1)
            tokens_ref[...] = incoming[source].reshape(WIN, WIN, E)

        @pl.when(filled)
        def _():
            tokens = tokens_ref[...].reshape(WIN * WIN, E).astype(F32)
            normed = layer_norm(tokens, gain[...], bias[...])
            context = []
            for c in range(0, E, 2 * width):
                cols = slice(c, c + 2 * width)
                q = ((matmul(normed, in_proj[:, cols]) + in_bias[:, cols]) * QSCALE).astype(BF16)
                cols = slice(E + c, E + c + 2 * width)
                k = (matmul(normed, in_proj[:, cols]) + in_bias[:, cols]).astype(BF16)
                cols = slice(2 * E + c, 2 * E + c + 2 * width)
                v = (matmul(normed, in_proj[:, cols]) + in_bias[:, cols]).astype(BF16)
                for a in (0, width):
                    context.append(attend(q[:, a : a + width], k[:, a : a + width], v[:, a : a + width]))
            result = matmul(jnp.concatenate(context, axis=1), out_proj[...]) + out_bias[...] + tokens
            out[0, slot] = result.astype(BF16)

        @pl.when(jnp.logical_not(filled))
        def _():
            out[0, slot] = jnp.zeros((WIN * WIN, E), BF16)


def in_smem():
    return pl.BlockSpec(memory_space=pltpu.SMEM)


def in_vmem():
    return pl.BlockSpec(memory_space=pltpu.VMEM)


def anywhere():
    return pl.BlockSpec(memory_space=pl.ANY)


def shifted(block, axis, distance):
    count = lax.axis_size(axis)
    return lax.ppermute(block, axis, [((i - distance) % count, i) for i in range(count)])


def shifted_both(block, down, right):
    rows, cols = lax.axis_size("narrow"), lax.axis_size("wide")
    route = [
        (((c - right) % cols) * rows + (r - down) % rows, c * rows + r)
        for c in range(cols)
        for r in range(rows)
    ]
    return lax.ppermute(block, ("wide", "narrow"), route)


def shards(
    image,
    third_norm_gain,
    third_norm_bias,
    third_in_proj,
    third_in_bias,
    third_out_proj,
    third_out_bias,
    window_keep,
    merge_gain,
    merge_bias,
    merge_weight,
    fourth_norm_gain,
    fourth_norm_bias,
    fourth_in_proj,
    fourth_in_bias,
    fourth_out_proj,
    fourth_out_bias,
    window_route,
):
    last = 3 * SHIFT
    edge = 7 * WIN
    rows_above = shifted(image[last:], "narrow", 1)
    rows_below = shifted(image[:SHIFT], "narrow", -1)
    cols_left = shifted(image[:, edge:], "wide", 1)
    cols_right = shifted(image[:, :WIN], "wide", -1)
    corner_tl = shifted_both(image[last:, edge:], 1, 1)
    corner_tr = shifted_both(image[last:, :WIN], 1, -1)
    corner_bl = shifted_both(image[:SHIFT, edge:], -1, 1)
    corner_br = shifted_both(image[:SHIFT, :WIN], -1, -1)
    keep_rows = jnp.concatenate([shifted(window_keep[1:], "narrow", 1), window_keep], axis=0)
    keep = jnp.concatenate([shifted(keep_rows[:, 7:], "wide", 1), keep_rows], axis=1)
    own_keep = jnp.pad(window_keep, ((1, 0), (1, 0)))
    place = jnp.stack(
        [
            lax.axis_index("narrow"),
            lax.axis_index("wide"),
            jnp.int32(lax.axis_size("narrow")),
            jnp.int32(lax.axis_size("wide")),
        ]
    ).astype(jnp.int32)
    params = pltpu.CompilerParams(vmem_limit_bytes=VMEM_LIMIT)
    third = (
        third_norm_gain[None],
        third_norm_bias[None],
        third_in_proj,
        third_in_bias[None],
        third_out_proj,
        third_out_bias[None],
    )
    inner = pl.pallas_call(
        inner_kernel,
        out_shape=jax.ShapeDtypeStruct((7, WIN * WIN, D), BF16),
        in_specs=[in_smem()] + [in_vmem()] * 7,
        out_specs=in_vmem(),
        compiler_params=params,
        cost_estimate=pl.CostEstimate(flops=20_000_000_000, bytes_accessed=8_000_000, transcendentals=0),
        name="inner_windows",
    )(own_keep, image, *third)
    merged, outgoing = pl.pallas_call(
        outer_kernel,
        out_shape=(
            jax.ShapeDtypeStruct((16, 64, E), BF16),
            jax.ShapeDtypeStruct((2, WIN * WIN, E), BF16),
        ),
        in_specs=[in_smem()] * 3 + [in_vmem()] * 2 + [anywhere()] * 2 + [in_vmem()] * 15,
        out_specs=(in_vmem(), in_vmem()),
        scratch_shapes=[
            pltpu.VMEM((4, 32, 128, 128), F32),
            pltpu.VMEM((2, SHIFT, 128, D), BF16),
            pltpu.SemaphoreType.DMA((2,)),
        ],
        compiler_params=params,
        name="outer_windows",
    )(
        place,
        keep,
        window_route,
        image,
        inner,
        rows_above,
        rows_below,
        cols_left,
        cols_right,
        corner_tl,
        corner_tr,
        corner_bl,
        corner_br,
        *third,
        merge_gain[None],
        merge_bias[None],
        merge_weight,
    )
    incoming = shifted(outgoing, "wide", 1)
    section_four = pl.pallas_call(
        top_kernel,
        out_shape=jax.ShapeDtypeStruct((1, 2, WIN * WIN, E), BF16),
        in_specs=[in_smem()] * 2 + [anywhere()] + [in_vmem()] * 7,
        out_specs=in_vmem(),
        scratch_shapes=[pltpu.VMEM((WIN, WIN, E), BF16), pltpu.SemaphoreType.DMA],
        compiler_params=params,
        name="top_windows",
    )(
        place,
        window_route,
        merged,
        incoming,
        fourth_norm_gain[None],
        fourth_norm_bias[None],
        fourth_in_proj,
        fourth_in_bias[None],
        fourth_out_proj,
        fourth_out_bias[None],
    )
    return merged, section_four


def solution(mesh):
    placed = (
        P("narrow", "wide", None),
        P(),
        P(),
        P(),
        P(),
        P(),
        P(),
        P("narrow", "wide"),
        P(),
        P(),
        P(),
        P(),
        P(),
        P(),
        P(),
        P(),
        P(),
        P("narrow", None),
    )
    return jax.shard_map(
        shards,
        mesh=mesh,
        in_specs=placed,
        out_specs=(P("narrow", "wide", None), P("narrow", "wide", None, None)),
        check_vma=False,
    )
```

```python
import jax
import jax.numpy as jnp
from jax import lax
from jax.experimental import pallas as pl
from jax.experimental.pallas import tpu as pltpu
from jax.sharding import PartitionSpec as P

D = 512
HEADS_D = 16
E = 1024
HEADS_E = 32
WIN = 16
SHIFT = 8
HEAD = 32
PACK = 4
EPSILON = 1e-05
LOG2E = 1.4426950408889634
QSCALE = HEAD ** (-0.5) * LOG2E
BF16 = jnp.bfloat16
F32 = jnp.float32


def matmul(a, b):
    return jnp.dot(a, b, preferred_element_type=F32)


def layer_norm(values, gain, bias):
    center = jnp.mean(values, axis=-1, keepdims=True)
    offsets = values - center
    spread = jnp.mean(offsets * offsets, axis=-1, keepdims=True)
    return (offsets * lax.rsqrt(spread + EPSILON) * gain + bias).astype(BF16)


def attend(q, k, v):
    count = q.shape[0]
    lane = lax.broadcasted_iota(jnp.int32, (count, PACK * HEAD), 1)
    stacked = jnp.concatenate(
        [jnp.where((lane >= HEAD * h) & (lane < HEAD * h + HEAD), q, 0) for h in range(PACK)], axis=0
    )
    scores = lax.dot_general(stacked, k, (((1,), (1,)), ((), ())), preferred_element_type=F32)
    weights = jnp.exp2(scores - jnp.max(scores, axis=1, keepdims=True)).astype(BF16)
    sums = matmul(weights, jnp.concatenate([v, jnp.ones_like(v)], axis=1))
    total = sums[:count]
    lane = lax.broadcasted_iota(jnp.int32, total.shape, 1) % (PACK * HEAD)
    for h in range(1, PACK):
        total = jnp.where(lane >= HEAD * h, sums[count * h : count * (h + 1)], total)
    return (total[:, : PACK * HEAD] / total[:, PACK * HEAD :]).astype(BF16)


def attention_three(tokens, count, refs):
    gain, bias, in_proj, in_bias, out_proj, out_bias = refs
    normed = layer_norm(tokens, gain[...], bias[...])
    q = ((matmul(normed[:count], in_proj[:, :D]) + in_bias[:, :D]) * QSCALE).astype(BF16)
    k = (matmul(normed, in_proj[:, D : 2 * D]) + in_bias[:, D : 2 * D]).astype(BF16)
    v = (matmul(normed, in_proj[:, 2 * D :]) + in_bias[:, 2 * D :]).astype(BF16)
    width = PACK * HEAD
    context = jnp.concatenate(
        [attend(q[:, c : c + width], k[:, c : c + width], v[:, c : c + width]) for c in range(0, D, width)],
        axis=1,
    )
    return (matmul(context, out_proj[...]) + out_bias[...] + tokens[:count]).astype(BF16)


def column(j):
    return pl.multiple_of(j * WIN, WIN)


def inner_kernel(keep, image, gain, bias, in_proj, in_bias, out_proj, out_bias, out):
    refs = (gain, bias, in_proj, in_bias, out_proj, out_bias)

    @pl.loop(0, 7)
    def _(j):
        both = image[SHIFT : SHIFT + WIN, pl.ds(column(j), 2 * WIN), :].astype(F32)
        tokens = both[:, SHIFT : SHIFT + WIN, :].reshape(WIN * WIN, D)

        @pl.when(keep[0, j] == 1)
        def _():
            out[j] = attention_three(tokens, WIN * WIN, refs)

        @pl.when(keep[0, j] != 1)
        def _():
            out[j] = tokens.astype(BF16)


def flag_at(flags, lane):
    lanes = lax.broadcasted_iota(jnp.int32, (WIN, 128), 1)
    return jnp.max(jnp.where(lanes == lane, flags[:, :128].astype(F32), 0.0)) > 0.5


def half_kernel(
    keep, image, above, below, gain, bias, in_proj, in_bias, out_proj, out_bias, out, own_rows, far_rows, flags, sem
):
    refs = (gain, bias, in_proj, in_bias, out_proj, out_bias)
    copies = [
        pltpu.make_async_copy(image.at[0:SHIFT], own_rows.at[0], sem.at[0]),
        pltpu.make_async_copy(image.at[3 * SHIFT : 4 * SHIFT], own_rows.at[1], sem.at[1]),
        pltpu.make_async_copy(below, far_rows.at[1], sem.at[2]),
        pltpu.make_async_copy(above.at[1024:1040], flags, sem.at[3]),
    ]
    for r in range(SHIFT):
        copies.append(pltpu.make_async_copy(above.at[128 * r : 128 * r + 128], far_rows.at[0, r], sem.at[4 + r]))
    for copy in copies:
        copy.start()
    for copy in copies:
        copy.wait()
    narrow, rows = lax.axis_index("narrow"), lax.axis_size("narrow")

    @pl.loop(0, 14)
    def _(step):
        side = step // 7
        j = step - 7 * side
        cols = pl.ds(column(j), 2 * WIN)
        own = own_rows[side, :, cols, :].astype(F32)[:, SHIFT : SHIFT + WIN]
        other = far_rows[side, :, cols, :].astype(F32)[:, SHIFT : SHIFT + WIN]
        at_edge = narrow == jnp.where(side == 0, 0, rows - 1)
        other = jnp.where(at_edge, own, other)
        tokens = jnp.concatenate([own.reshape(-1, D), other.reshape(-1, D)], axis=0)
        kept = jnp.where(side == 0, flag_at(flags, j).astype(jnp.int32), keep[1, j]) == 1

        @pl.when(kept)
        def _():
            out[step] = attention_three(tokens, 128, refs)

        @pl.when(jnp.logical_not(kept))
        def _():
            out[step] = tokens[:128].astype(BF16)


def store(layer, rows, cols, values):
    for c in range(4):
        layer[c, rows, cols, :] = values[:, :, 128 * c : 128 * c + 128]


def lay_out(layer, inner, halves):
    @pl.loop(0, 7)
    def _(j):
        cols = pl.ds(pl.multiple_of(j * WIN + SHIFT, SHIFT), WIN)
        store(layer, slice(SHIFT, SHIFT + WIN), cols, inner[j].astype(F32).reshape(WIN, WIN, D))
        store(layer, slice(0, SHIFT), cols, halves[j].astype(F32).reshape(SHIFT, WIN, D))
        store(layer, slice(3 * SHIFT, 4 * SHIFT), cols, halves[7 + j].astype(F32).reshape(SHIFT, WIN, D))


def merge_order(route, first):
    wide = lax.axis_index("wide")
    moves = [(route[0, 4 * wide + j] == 2).astype(jnp.int32) for j in range(4)]
    total = moves[0] + moves[1] + moves[2] + moves[3]
    chosen = [0, 0]
    moved, stayed = 0, 0
    for j in range(4):
        position = jnp.where(moves[j] == 1, moved, total + stayed)
        for slot in range(2):
            chosen[slot] = jnp.where(position == first + slot, j, chosen[slot])
        moved = moved + moves[j]
        stayed = stayed + 1 - moves[j]
    return chosen


def merge_group(layer, group, gain, bias, weight):
    parts = []
    for odd_col in range(2):
        cols = pl.ds(group * 32 + odd_col, WIN, stride=2)
        for odd_row in range(2):
            lanes = [
                jnp.concatenate([layer[c, 2 * r + odd_row, cols, :] for r in range(WIN)], axis=0) for c in range(4)
            ]
            parts.extend(lanes)
    normed = layer_norm(jnp.concatenate(parts, axis=1), gain[...], bias[...])
    return matmul(normed, weight[...]).astype(BF16)


def edge_kernel(
    keep,
    route,
    own_left,
    own_right,
    far_left,
    far_right,
    inner,
    halves,
    gain,
    bias,
    in_proj,
    in_bias,
    out_proj,
    out_bias,
    merge_gain,
    merge_bias,
    merge_weight,
    merged,
    first,
    second,
    sides,
    corners,
    layer,
    results,
    sem,
):
    refs = (gain, bias, in_proj, in_bias, out_proj, out_bias)
    narrow, rows = lax.axis_index("narrow"), lax.axis_size("narrow")
    wide, groups = lax.axis_index("wide"), lax.axis_size("wide")
    lay_out(layer, inner, halves)
    flags = far_left[24]

    def strip(ref, low, high):
        return ref[low // 2 : high // 2].astype(F32).reshape(-1, D)

    def finish(kept, tokens, count, out, slot):
        @pl.when(kept)
        def _():
            out[slot] = attention_three(tokens, count, refs)

        @pl.when(jnp.logical_not(kept))
        def _():
            out[slot] = tokens[:count].astype(BF16)

    for side in range(2):
        near, far = (own_left, own_right)[side], (far_left, far_right)[side]
        edge_col = wide == (0, groups - 1)[side]
        col = slice(15 * SHIFT * side, 15 * SHIFT * side + SHIFT)
        own = strip(near, 16, 32)
        beside = jnp.where(edge_col, own, strip(far, 16, 32))
        kept = flag_at(flags, 1) if side == 0 else keep[0, 7] == 1
        finish(kept, jnp.concatenate([own, beside], axis=0), 128, sides, side)
        store(layer, slice(SHIFT, SHIFT + WIN), col, sides[side].astype(F32).reshape(WIN, SHIFT, D))
        for down in range(2):
            edge_row = narrow == (0, rows - 1)[down]
            mine, beyond = ((8, 0), (32, 40))[down]
            own = strip(near, mine, mine + SHIFT)
            across = jnp.where(edge_row, own, strip(near, beyond, beyond + SHIFT))
            beside = jnp.where(edge_col, own, strip(far, mine, mine + SHIFT))
            corner = strip(far, beyond, beyond + SHIFT)
            corner = jnp.where(edge_col, across, jnp.where(edge_row, beside, corner))
            tokens = jnp.concatenate([own, across, beside, corner], axis=0)
            if side == 0:
                kept = flag_at(flags, 2 * down)
            elif down == 0:
                kept = flag_at(own_right[24], 0)
            else:
                kept = keep[1, 7] == 1
            slot = 2 * down + side
            finish(kept, tokens, 64, corners, slot)
            row = slice(3 * SHIFT * down, 3 * SHIFT * down + SHIFT)
            store(layer, row, col, corners[slot].astype(F32).reshape(SHIFT, SHIFT, D))
    merge_two(route, 0, layer, merge_gain, merge_bias, merge_weight, merged, results, sem, (first, second))


def merge_two(route, start, layer, gain, bias, weight, merged, results, sem, outs):
    copies = []
    for slot, group in enumerate(merge_order(route, start)):
        result = merge_group(layer, group, gain, bias, weight)
        if outs is not None:
            outs[slot][...] = result
        results[slot] = result.reshape(WIN, WIN, E)
        copy = pltpu.make_async_copy(results.at[slot], merged.at[:, pl.ds(column(group), WIN), :], sem.at[slot])
        copy.start()
        copies.append(copy)
    for copy in copies:
        copy.wait()


def rest_kernel(
    route, earlier, inner, halves, sides, corners, gain, bias, weight, merged, layer, results, sem
):
    lay_out(layer, inner, halves)
    for side in range(2):
        col = slice(15 * SHIFT * side, 15 * SHIFT * side + SHIFT)
        store(layer, slice(SHIFT, SHIFT + WIN), col, sides[side].astype(F32).reshape(WIN, SHIFT, D))
        for down in range(2):
            row = slice(3 * SHIFT * down, 3 * SHIFT * down + SHIFT)
            store(layer, row, col, corners[2 * down + side].astype(F32).reshape(SHIFT, SHIFT, D))
    merge_two(route, 2, layer, gain, bias, weight, merged, results, sem, None)


def top_kernel(
    slot, route, merged, incoming, gain, bias, in_proj, in_bias, out_proj, out_bias, *rest
):
    out, tokens_ref, result, sem = rest[-4:]
    wide, groups = lax.axis_index("wide"), lax.axis_size("wide")
    before = jnp.where(wide == 0, groups - 1, wide - 1)
    homes = 0
    arriving = 0
    chosen = 0
    for j in range(4):
        stays = route[0, 4 * wide + j] == 1
        chosen = jnp.where(stays & (homes == slot), j, chosen)
        homes = homes + stays.astype(jnp.int32)
        arriving = arriving + (route[0, 4 * before + j] == 2).astype(jnp.int32)
    width = PACK * HEAD
    filled = slot < homes + arriving

    @pl.when(slot < homes)
    def _():
        copy = pltpu.make_async_copy(merged.at[:, pl.ds(column(chosen), WIN), :], tokens_ref, sem)
        copy.start()
        copy.wait()

    for source in range(slot + 1):

        @pl.when(homes + source == slot)
        def _():
            tokens_ref[...] = incoming[source][...].reshape(WIN, WIN, E)

    @pl.when(filled)
    def _():
        tokens = tokens_ref[...].reshape(WIN * WIN, E).astype(F32)
        normed = layer_norm(tokens, gain[...], bias[...])
        context = []
        for c in range(0, E, 2 * width):
            cols = slice(c, c + 2 * width)
            q = ((matmul(normed, in_proj[:, cols]) + in_bias[:, cols]) * QSCALE).astype(BF16)
            cols = slice(E + c, E + c + 2 * width)
            k = (matmul(normed, in_proj[:, cols]) + in_bias[:, cols]).astype(BF16)
            cols = slice(2 * E + c, 2 * E + c + 2 * width)
            v = (matmul(normed, in_proj[:, cols]) + in_bias[:, cols]).astype(BF16)
            for a in (0, width):
                context.append(attend(q[:, a : a + width], k[:, a : a + width], v[:, a : a + width]))
        value = matmul(jnp.concatenate(context, axis=1), out_proj[...]) + out_bias[...] + tokens
        result[...] = value.astype(BF16)

    @pl.when(jnp.logical_not(filled))
    def _():
        result[...] = jnp.zeros((WIN * WIN, E), BF16)

    copy = pltpu.make_async_copy(result, out.at[0, slot], sem)
    copy.start()
    copy.wait()


def top_first(route, merged, one, *rest):
    top_kernel(0, route, merged, (one,), *rest)


def top_second(route, merged, one, two, gain, bias, in_proj, in_bias, out_proj, out_bias, earlier, *rest):
    top_kernel(1, route, merged, (one, two), gain, bias, in_proj, in_bias, out_proj, out_bias, *rest)


def in_smem():
    return pl.BlockSpec(memory_space=pltpu.SMEM)


def in_vmem():
    return pl.BlockSpec(memory_space=pltpu.VMEM)


def anywhere():
    return pl.BlockSpec(memory_space=pl.ANY)


def shifted(block, axis, distance):
    count = lax.axis_size(axis)
    return lax.ppermute(block, axis, [((i - distance) % count, i) for i in range(count)])


def flag_rows(flags):
    flags = flags.astype(BF16)
    return jnp.broadcast_to(jnp.pad(flags, (0, D - flags.shape[0]))[None], (WIN, D))


def shape(*sizes):
    return jax.ShapeDtypeStruct(sizes, BF16)


def params(mib):
    return pltpu.CompilerParams(vmem_limit_bytes=mib * 2**20)


def cost(us):
    return pl.CostEstimate(flops=us * 10**9, bytes_accessed=4_000_000, transcendentals=0)


def shards(
    image,
    third_norm_gain,
    third_norm_bias,
    third_in_proj,
    third_in_bias,
    third_out_proj,
    third_out_bias,
    window_keep,
    merge_gain,
    merge_bias,
    merge_weight,
    fourth_norm_gain,
    fourth_norm_bias,
    fourth_in_proj,
    fourth_in_bias,
    fourth_out_proj,
    fourth_out_bias,
    window_route,
):
    last = 3 * SHIFT
    send_down = jnp.concatenate([image[last:].reshape(-1, D), flag_rows(window_keep[1])], axis=0)
    above = shifted(send_down, "narrow", 1)
    below = shifted(image[:SHIFT], "narrow", -1)
    third = (
        third_norm_gain[None],
        third_norm_bias[None],
        third_in_proj,
        third_in_bias[None],
        third_out_proj,
        third_out_bias[None],
    )
    inner = pl.pallas_call(
        inner_kernel,
        out_shape=shape(7, WIN * WIN, D),
        in_specs=[in_smem()] + [in_vmem()] * 7,
        out_specs=in_vmem(),
        compiler_params=params(32),
        cost_estimate=cost(18),
        name="inner_windows",
    )(window_keep, image, *third)

    def strip(cols):
        rows = above[:1024].reshape(SHIFT, -1, D)
        whole = jnp.concatenate([rows[:, cols], image[:, cols], below[:, cols]], axis=0)
        return whole.reshape(24, WIN, D)

    own_left = strip(slice(0, SHIFT))
    side_flags = jnp.concatenate([above[1024, 7:8], window_keep[:, 7].astype(BF16)])
    own_right = jnp.concatenate([strip(slice(15 * SHIFT, 16 * SHIFT)), flag_rows(side_flags)[None]], axis=0)
    far_left = shifted(own_right, "wide", 1)
    far_right = shifted(own_left, "wide", -1)
    halves = pl.pallas_call(
        half_kernel,
        out_shape=shape(14, 128, D),
        in_specs=[in_smem()] + [anywhere()] * 3 + [in_vmem()] * 6,
        out_specs=in_vmem(),
        scratch_shapes=[
            pltpu.VMEM((2, SHIFT, 128, D), BF16),
            pltpu.VMEM((2, SHIFT, 128, D), BF16),
            pltpu.VMEM((WIN, D), BF16),
            pltpu.SemaphoreType.DMA((12,)),
        ],
        compiler_params=params(32),
        cost_estimate=cost(18),
        name="half_windows",
    )(window_keep, image, above, below, *third)
    merging = (merge_gain[None], merge_bias[None], merge_weight)
    scratch = [
        pltpu.VMEM((4, 32, 128, 128), F32),
        pltpu.VMEM((2, WIN, WIN, E), BF16),
        pltpu.SemaphoreType.DMA((2,)),
    ]
    merged, first, second, sides, corners = pl.pallas_call(
        edge_kernel,
        out_shape=(
            shape(16, 64, E),
            shape(WIN * WIN, E),
            shape(WIN * WIN, E),
            shape(2, 128, D),
            shape(4, 64, D),
        ),
        in_specs=[in_smem()] * 2 + [in_vmem()] * 15,
        out_specs=(anywhere(),) + (in_vmem(),) * 4,
        scratch_shapes=scratch,
        compiler_params=params(40),
        cost_estimate=cost(10),
        name="edge_windows",
    )(window_keep, window_route, own_left, own_right, far_left, far_right, inner, halves, *third, *merging)
    incoming_first = shifted(first, "wide", 1)
    incoming_second = shifted(second, "wide", 1)
    merged = pl.pallas_call(
        rest_kernel,
        out_shape=shape(16, 64, E),
        in_specs=[in_smem(), anywhere()] + [in_vmem()] * 7,
        out_specs=anywhere(),
        scratch_shapes=scratch,
        input_output_aliases={1: 0},
        compiler_params=params(32),
        cost_estimate=cost(5),
        name="rest_merging",
    )(window_route, merged, inner, halves, sides, corners, *merging)
    fourth = (
        fourth_norm_gain[None],
        fourth_norm_bias[None],
        fourth_in_proj,
        fourth_in_bias[None],
        fourth_out_proj,
        fourth_out_bias[None],
    )
    scratch = [
        pltpu.VMEM((WIN, WIN, E), BF16),
        pltpu.VMEM((WIN * WIN, E), BF16),
        pltpu.SemaphoreType.DMA,
    ]
    slots = pl.pallas_call(
        top_first,
        out_shape=shape(1, 2, WIN * WIN, E),
        in_specs=[in_smem(), anywhere()] + [in_vmem()] * 7,
        out_specs=anywhere(),
        scratch_shapes=scratch,
        compiler_params=params(32),
        cost_estimate=cost(8),
        name="top_first",
    )(window_route, merged, incoming_first, *fourth)
    slots = pl.pallas_call(
        top_second,
        out_shape=shape(1, 2, WIN * WIN, E),
        in_specs=[in_smem(), anywhere()] + [in_vmem()] * 8 + [anywhere()],
        out_specs=anywhere(),
        scratch_shapes=scratch,
        input_output_aliases={10: 0},
        compiler_params=params(32),
        cost_estimate=cost(8),
        name="top_second",
    )(window_route, merged, incoming_first, incoming_second, *fourth, slots)
    return merged, slots


def solution(mesh):
    placed = (
        P("narrow", "wide", None),
        P(),
        P(),
        P(),
        P(),
        P(),
        P(),
        P("narrow", "wide"),
        P(),
        P(),
        P(),
        P(),
        P(),
        P(),
        P(),
        P(),
        P(),
        P("narrow", None),
    )
    return jax.shard_map(
        shards,
        mesh=mesh,
        in_specs=placed,
        out_specs=(P("narrow", "wide", None), P("narrow", "wide", None, None)),
        check_vma=False,
    )
```

```python
import jax
import jax.numpy as jnp
from jax import lax
from jax.experimental import pallas as pl
from jax.experimental.pallas import tpu as pltpu
from jax.sharding import PartitionSpec as P

D = 512
HEADS_D = 16
E = 1024
HEADS_E = 32
WIN = 16
SHIFT = 8
HEAD = 32
PACK = 4
EPSILON = 1e-05
LOG2E = 1.4426950408889634
QSCALE = HEAD ** (-0.5) * LOG2E
BF16 = jnp.bfloat16
F32 = jnp.float32


def matmul(a, b):
    return jnp.dot(a, b, preferred_element_type=F32)


def layer_norm(values, gain, bias):
    center = jnp.mean(values, axis=-1, keepdims=True)
    offsets = values - center
    spread = jnp.mean(offsets * offsets, axis=-1, keepdims=True)
    return (offsets * lax.rsqrt(spread + EPSILON) * gain + bias).astype(BF16)


def attend(q, k, v):
    count = q.shape[0]
    lane = lax.broadcasted_iota(jnp.int32, (count, PACK * HEAD), 1)
    stacked = jnp.concatenate(
        [jnp.where((lane >= HEAD * h) & (lane < HEAD * h + HEAD), q, 0) for h in range(PACK)], axis=0
    )
    scores = lax.dot_general(stacked, k, (((1,), (1,)), ((), ())), preferred_element_type=F32)
    weights = jnp.exp2(scores - jnp.max(scores, axis=1, keepdims=True)).astype(BF16)
    sums = matmul(weights, jnp.concatenate([v, jnp.ones_like(v)], axis=1))
    total = sums[:count]
    lane = lax.broadcasted_iota(jnp.int32, total.shape, 1) % (PACK * HEAD)
    for h in range(1, PACK):
        total = jnp.where(lane >= HEAD * h, sums[count * h : count * (h + 1)], total)
    return (total[:, : PACK * HEAD] / total[:, PACK * HEAD :]).astype(BF16)


def attention_three(tokens, count, refs):
    gain, bias, in_proj, in_bias, out_proj, out_bias = refs
    normed = layer_norm(tokens, gain[...], bias[...])
    q = ((matmul(normed[:count], in_proj[:, :D]) + in_bias[:, :D]) * QSCALE).astype(BF16)
    k = (matmul(normed, in_proj[:, D : 2 * D]) + in_bias[:, D : 2 * D]).astype(BF16)
    v = (matmul(normed, in_proj[:, 2 * D :]) + in_bias[:, 2 * D :]).astype(BF16)
    width = PACK * HEAD
    context = jnp.concatenate(
        [attend(q[:, c : c + width], k[:, c : c + width], v[:, c : c + width]) for c in range(0, D, width)],
        axis=1,
    )
    return (matmul(context, out_proj[...]) + out_bias[...] + tokens[:count]).astype(BF16)


def column(j):
    return pl.multiple_of(j * WIN, WIN)


def pack_kernel(keep, image, down, up, down_rest, up_rest, sem):
    copies = []
    for side, (early, late) in enumerate(((down, down_rest), (up, up_rest))):
        for r in range(SHIFT):
            row = image.at[3 * SHIFT + r if side == 0 else r]
            copies.append((row.at[0:48], early.at[96 * r : 96 * r + 48]))
            copies.append((row.at[80:128], early.at[96 * r + 48 : 96 * r + 96]))
            copies.append((row.at[48:80], late.at[32 * r : 32 * r + 32]))
    copies = [pltpu.make_async_copy(*pair, sem.at[i]) for i, pair in enumerate(copies)]
    for copy in copies:
        copy.start()
    lanes = lax.broadcasted_iota(jnp.int32, (WIN, D), 1)
    flags = jnp.zeros((WIN, D), F32)
    for j in range(8):
        flags = jnp.where(lanes == j, keep[1, j].astype(F32), flags)
    down[768:784] = flags.astype(BF16)
    for copy in copies:
        copy.wait()


def strip_kernel(keep, image, above, below, left, right):
    for side, out in enumerate((left, right)):
        base, start = (0, 7 * WIN)[side], SHIFT * side
        for pair in range(24):
            rows = []
            for r in (2 * pair, 2 * pair + 1):
                if r < SHIFT:
                    block = above[96 * r + (0, 80)[side] : 96 * r + (16, 96)[side]]
                elif r < 5 * SHIFT:
                    block = image[r - SHIFT, base : base + WIN]
                else:
                    q = r - 5 * SHIFT
                    block = below[96 * q + (0, 80)[side] : 96 * q + (16, 96)[side]]
                rows.append(block.astype(F32)[start : start + SHIFT])
            out[pair] = jnp.concatenate(rows, axis=0).astype(BF16)
    lanes = lax.broadcasted_iota(jnp.int32, (WIN, D), 1)
    flags = jnp.where(lanes == 0, flag_at(above[768:784], 7).astype(F32), 0.0)
    for a in range(2):
        flags = jnp.where(lanes == a + 1, keep[a, 7].astype(F32), flags)
    right[24] = flags.astype(BF16)


def inner_kernel(keep, image, gain, bias, in_proj, in_bias, out_proj, out_bias, out):
    refs = (gain, bias, in_proj, in_bias, out_proj, out_bias)

    @pl.loop(0, 7)
    def _(j):
        both = image[SHIFT : SHIFT + WIN, pl.ds(column(j), 2 * WIN), :].astype(F32)
        tokens = both[:, SHIFT : SHIFT + WIN, :].reshape(WIN * WIN, D)

        @pl.when(keep[0, j] == 1)
        def _():
            out[j] = attention_three(tokens, WIN * WIN, refs)

        @pl.when(keep[0, j] != 1)
        def _():
            out[j] = tokens.astype(BF16)


def flag_at(flags, lane):
    lanes = lax.broadcasted_iota(jnp.int32, (WIN, 128), 1)
    return jnp.max(jnp.where(lanes == lane, flags[:, :128].astype(F32), 0.0)) > 0.5


def project(normed, queries, in_proj, in_bias, q_ref, k_ref, v_ref):
    q = (matmul(queries, in_proj[:, :D]) + in_bias[:, :D]) * QSCALE
    q_ref[...] = q.astype(BF16)
    k_ref[...] = (matmul(normed, in_proj[:, D : 2 * D]) + in_bias[:, D : 2 * D]).astype(BF16)
    v_ref[...] = (matmul(normed, in_proj[:, 2 * D :]) + in_bias[:, 2 * D :]).astype(BF16)


def attend_window(first, count, window, q_ref, k_ref, v_ref, context):
    width = PACK * HEAD
    mine, keys = slice(first, first + count), slice(WIN * WIN * window, WIN * WIN * (window + 1))
    for c in range(0, D, width):
        cols = slice(c, c + width)
        context[mine, cols] = attend(q_ref[mine, cols], k_ref[keys, cols], v_ref[keys, cols])


def half_pair(keep, image, j, far, top_kept, refs, out, step, scratch):
    gain, bias, in_proj, in_bias, out_proj, out_bias = refs
    narrow, rows = lax.axis_index("narrow"), lax.axis_size("narrow")
    q_ref, k_ref, v_ref, context = scratch
    tokens = []
    for side in range(2):
        row = 3 * SHIFT * side
        own = image[row : row + SHIFT, pl.ds(column(j), 2 * WIN), :].astype(F32)
        own = own[:, SHIFT : SHIFT + WIN].reshape(-1, D)
        tokens.append((own, jnp.where(narrow == (0, rows - 1)[side], own, far(side))))
    kept = [top_kept, keep[1, j] == 1]

    @pl.when(kept[0] | kept[1])
    def _():
        normed = [[layer_norm(part, gain[...], bias[...]) for part in pair] for pair in tokens]
        queries = jnp.concatenate([normed[0][0], normed[1][0]], axis=0)
        project(jnp.concatenate(normed[0] + normed[1], axis=0), queries, in_proj, in_bias, q_ref, k_ref, v_ref)

    for side in range(2):

        @pl.when(kept[side])
        def _():
            attend_window(128 * side, 128, side, q_ref, k_ref, v_ref, context)

    @pl.when(kept[0] | kept[1])
    def _():
        result = matmul(context[...], out_proj[...]) + out_bias[...]
        for side in range(2):
            own = tokens[side][0]
            new = own + result[128 * side : 128 * side + 128]
            out[step, side] = jnp.where(kept[side], new, own).astype(BF16)

    @pl.when(jnp.logical_not(kept[0] | kept[1]))
    def _():
        for side in range(2):
            out[step, side] = tokens[side][0].astype(BF16)


def gather_rows(ref, pitch, start):
    rows = [ref[pl.ds(pitch * r + start, 2 * WIN), :].astype(F32)[SHIFT : SHIFT + WIN] for r in range(SHIFT)]
    return jnp.concatenate(rows, axis=0)


def half_outer_kernel(
    keep, image, above, below, gain, bias, in_proj, in_bias, out_proj, out_bias, out, *scratch
):
    refs = (gain, bias, in_proj, in_bias, out_proj, out_bias)
    flags = above[768:784]

    @pl.loop(0, 4)
    def _(step):
        late = (step >= 2).astype(jnp.int32)
        j = step + 3 * late
        start = pl.multiple_of((step + late) * WIN, WIN)
        far = lambda side: gather_rows((above, below)[side], 96, start)
        half_pair(keep, image, j, far, flag_at(flags, j), refs, out, step, scratch)


def half_inner_kernel(
    keep, image, above, below, above_rest, below_rest, gain, bias, in_proj, in_bias, out_proj, out_bias, out, *scratch
):
    refs = (gain, bias, in_proj, in_bias, out_proj, out_bias)
    flags = above[768:784]
    rows = scratch[4]
    for side in range(2):
        early, late = (above, below)[side], (above_rest, below_rest)[side]
        for r in range(SHIFT):
            rows[side, 64 * r : 64 * r + 16] = early[96 * r + 32 : 96 * r + 48]
            rows[side, 64 * r + 16 : 64 * r + 48] = late[32 * r : 32 * r + 32]
            rows[side, 64 * r + 48 : 64 * r + 64] = early[96 * r + 48 : 96 * r + 64]

    @pl.loop(0, 3)
    def _(step):
        j = step + 2
        far = lambda side: gather_rows(rows.at[side], 64, column(step))
        half_pair(keep, image, j, far, flag_at(flags, j), refs, out, step, scratch[:4])


def store(layer, rows, cols, values):
    for c in range(4):
        layer[c, rows, cols, :] = values[:, :, 128 * c : 128 * c + 128]


def lay_out(layer, inner, outer_halves, inner_halves):
    @pl.loop(0, 7)
    def _(j):
        cols = pl.ds(pl.multiple_of(j * WIN + SHIFT, SHIFT), WIN)
        store(layer, slice(SHIFT, SHIFT + WIN), cols, inner[j].astype(F32).reshape(WIN, WIN, D))

    for ref, columns in ((outer_halves, (0, 1, 5, 6)), (inner_halves, (2, 3, 4))):
        for step, j in enumerate(columns):
            cols = slice(j * WIN + SHIFT, j * WIN + SHIFT + WIN)
            for side in range(2):
                rows = slice(3 * SHIFT * side, 3 * SHIFT * side + SHIFT)
                store(layer, rows, cols, ref[step, side].astype(F32).reshape(SHIFT, WIN, D))


def lay_out_edges(layer, edges):
    for side in range(2):
        col = slice(15 * SHIFT * side, 15 * SHIFT * side + SHIFT)
        values = edges[128 * side : 128 * side + 128].astype(F32)
        store(layer, slice(SHIFT, SHIFT + WIN), col, values.reshape(WIN, SHIFT, D))
        for down in range(2):
            row = slice(3 * SHIFT * down, 3 * SHIFT * down + SHIFT)
            first = 256 + 64 * (2 * down + side)
            store(layer, row, col, edges[first : first + 64].astype(F32).reshape(SHIFT, SHIFT, D))


def merge_order(route, first):
    wide = lax.axis_index("wide")
    moves = [(route[0, 4 * wide + j] == 2).astype(jnp.int32) for j in range(4)]
    total = moves[0] + moves[1] + moves[2] + moves[3]
    chosen = [0, 0]
    moved, stayed = 0, 0
    for j in range(4):
        position = jnp.where(moves[j] == 1, moved, total + stayed)
        for slot in range(2):
            chosen[slot] = jnp.where(position == first + slot, j, chosen[slot])
        moved = moved + moves[j]
        stayed = stayed + 1 - moves[j]
    return chosen


def merge_two(route, start, layer, gain, bias, weight, merged, results, sem, outs):
    chosen = merge_order(route, start)
    blocks = []
    for group in chosen:
        parts = []
        for odd_col in range(2):
            cols = pl.ds(group * 32 + odd_col, WIN, stride=2)
            for odd_row in range(2):
                for c in range(4):
                    parts.append(
                        jnp.concatenate([layer[c, 2 * r + odd_row, cols, :] for r in range(WIN)], axis=0)
                    )
        blocks.append(layer_norm(jnp.concatenate(parts, axis=1), gain[...], bias[...]))
    result = matmul(jnp.concatenate(blocks, axis=0), weight[...]).astype(BF16)
    copies = []
    for slot, group in enumerate(chosen):
        part = result[256 * slot : 256 * slot + 256]
        if outs is not None:
            outs[slot][...] = part
        results[slot] = part.reshape(WIN, WIN, E)
        copy = pltpu.make_async_copy(results.at[slot], merged.at[:, pl.ds(column(group), WIN), :], sem.at[slot])
        copy.start()
        copies.append(copy)
    for copy in copies:
        copy.wait()


def edge_kernel(
    keep,
    route,
    own_left,
    own_right,
    far_left,
    far_right,
    inner,
    outer_halves,
    inner_halves,
    gain,
    bias,
    in_proj,
    in_bias,
    out_proj,
    out_bias,
    merge_gain,
    merge_bias,
    merge_weight,
    merged,
    first,
    second,
    edges,
    layer,
    results,
    q_ref,
    k_ref,
    v_ref,
    context,
    sem,
):
    narrow, rows = lax.axis_index("narrow"), lax.axis_size("narrow")
    wide, groups = lax.axis_index("wide"), lax.axis_size("wide")
    flags = far_left[24]

    def strip(ref, low, high):
        return ref[low // 2 : high // 2].astype(F32).reshape(-1, D)

    windows = []
    for side in range(2):
        near, far = (own_left, own_right)[side], (far_left, far_right)[side]
        edge_col = wide == (0, groups - 1)[side]
        own = strip(near, 16, 32)
        beside = jnp.where(edge_col, own, strip(far, 16, 32))
        kept = flag_at(flags, 1) if side == 0 else keep[0, 7] == 1
        windows.append((kept, own, [own, beside]))
    for down in range(2):
        for side in range(2):
            near, far = (own_left, own_right)[side], (far_left, far_right)[side]
            edge_col = wide == (0, groups - 1)[side]
            edge_row = narrow == (0, rows - 1)[down]
            mine, beyond = ((8, 0), (32, 40))[down]
            own = strip(near, mine, mine + SHIFT)
            across = jnp.where(edge_row, own, strip(near, beyond, beyond + SHIFT))
            beside = jnp.where(edge_col, own, strip(far, mine, mine + SHIFT))
            corner = strip(far, beyond, beyond + SHIFT)
            corner = jnp.where(edge_col, across, jnp.where(edge_row, beside, corner))
            if side == 0:
                kept = flag_at(flags, 2 * down)
            elif down == 0:
                kept = flag_at(own_right[24], 0)
            else:
                kept = keep[1, 7] == 1
            windows.append((kept, own, [own, across, beside, corner]))
    normed = [[layer_norm(part, gain[...], bias[...]) for part in parts] for _, _, parts in windows]
    queries = jnp.concatenate([parts[0] for parts in normed], axis=0)
    normed = jnp.concatenate([part for parts in normed for part in parts], axis=0)
    project(normed, queries, in_proj, in_bias, q_ref, k_ref, v_ref)
    place = 0
    for window, (kept, own, _) in enumerate(windows):
        count = own.shape[0]

        @pl.when(kept)
        def _():
            attend_window(place, count, window, q_ref, k_ref, v_ref, context)

        place += count
    result = matmul(context[...], out_proj[...]) + out_bias[...]
    place = 0
    for kept, own, _ in windows:
        mine = slice(place, place + own.shape[0])
        edges[mine] = jnp.where(kept, own + result[mine], own).astype(BF16)
        place += own.shape[0]
    lay_out(layer, inner, outer_halves, inner_halves)
    lay_out_edges(layer, edges)
    merge_two(route, 0, layer, merge_gain, merge_bias, merge_weight, merged, results, sem, (first, second))


def rest_kernel(
    route, earlier, inner, outer_halves, inner_halves, edges, gain, bias, weight, merged, third, fourth, layer, results, sem
):
    lay_out(layer, inner, outer_halves, inner_halves)
    lay_out_edges(layer, edges)
    merge_two(route, 2, layer, gain, bias, weight, merged, results, sem, (third, fourth))


def top_kernel(slot, route, own, incoming, gain, bias, in_proj, in_bias, out_proj, out_bias, *rest):
    out, tokens_ref, result, sem = rest[-4:]
    wide, groups = lax.axis_index("wide"), lax.axis_size("wide")
    before = jnp.where(wide == 0, groups - 1, wide - 1)
    homes = 0
    arriving = 0
    chosen = 0
    for j in range(4):
        stays = route[0, 4 * wide + j] == 1
        chosen = jnp.where(stays & (homes == slot), j, chosen)
        homes = homes + stays.astype(jnp.int32)
        arriving = arriving + (route[0, 4 * before + j] == 2).astype(jnp.int32)
    order = merge_order(route, 0) + merge_order(route, 2)
    width = PACK * HEAD
    filled = slot < homes + arriving

    for position in range(4):

        @pl.when((slot < homes) & (order[position] == chosen))
        def _():
            tokens_ref[...] = own[position][...]

    for source in range(slot + 1):

        @pl.when(homes + source == slot)
        def _():
            tokens_ref[...] = incoming[source][...]

    @pl.when(filled)
    def _():
        tokens = tokens_ref[...].astype(F32)
        normed = layer_norm(tokens, gain[...], bias[...])
        context = []
        for c in range(0, E, 2 * width):
            cols = slice(c, c + 2 * width)
            q = ((matmul(normed, in_proj[:, cols]) + in_bias[:, cols]) * QSCALE).astype(BF16)
            cols = slice(E + c, E + c + 2 * width)
            k = (matmul(normed, in_proj[:, cols]) + in_bias[:, cols]).astype(BF16)
            cols = slice(2 * E + c, 2 * E + c + 2 * width)
            v = (matmul(normed, in_proj[:, cols]) + in_bias[:, cols]).astype(BF16)
            for a in (0, width):
                context.append(attend(q[:, a : a + width], k[:, a : a + width], v[:, a : a + width]))
        value = matmul(jnp.concatenate(context, axis=1), out_proj[...]) + out_bias[...] + tokens
        result[...] = value.astype(BF16)

    @pl.when(jnp.logical_not(filled))
    def _():
        result[...] = jnp.zeros((WIN * WIN, E), BF16)

    copy = pltpu.make_async_copy(result, out.at[0, slot], sem)
    copy.start()
    copy.wait()


def top_first(route, first, second, third, fourth, one, *rest):
    top_kernel(0, route, (first, second, third, fourth), (one,), *rest)


def top_second(route, first, second, third, fourth, one, two, *rest):
    top_kernel(1, route, (first, second, third, fourth), (one, two), *rest)


def in_smem():
    return pl.BlockSpec(memory_space=pltpu.SMEM)


def in_vmem():
    return pl.BlockSpec(memory_space=pltpu.VMEM)


def in_hbm():
    return pl.BlockSpec(memory_space=pltpu.HBM)


def shifted(block, axis, distance):
    count = lax.axis_size(axis)
    return lax.ppermute(block, axis, [((i - distance) % count, i) for i in range(count)])


def shape(*sizes):
    return jax.ShapeDtypeStruct(sizes, BF16)


def params(mib):
    return pltpu.CompilerParams(vmem_limit_bytes=mib * 2**20)


def cost(us):
    return pl.CostEstimate(flops=us * 10**9, bytes_accessed=4_000_000, transcendentals=0)


def shards(
    image,
    third_norm_gain,
    third_norm_bias,
    third_in_proj,
    third_in_bias,
    third_out_proj,
    third_out_bias,
    window_keep,
    merge_gain,
    merge_bias,
    merge_weight,
    fourth_norm_gain,
    fourth_norm_bias,
    fourth_in_proj,
    fourth_in_bias,
    fourth_out_proj,
    fourth_out_bias,
    window_route,
):
    send_down, send_up, send_down_rest, send_up_rest = pl.pallas_call(
        pack_kernel,
        out_shape=(shape(784, D), shape(768, D), shape(256, D), shape(256, D)),
        in_specs=[in_smem(), in_vmem()],
        out_specs=(in_vmem(),) * 4,
        scratch_shapes=[pltpu.SemaphoreType.DMA((48,))],
        compiler_params=params(16),
        cost_estimate=cost(1),
        name="pack_rows",
    )(window_keep, image)
    above = shifted(send_down, "narrow", 1)
    below = shifted(send_up, "narrow", -1)
    third = (
        third_norm_gain[None],
        third_norm_bias[None],
        third_in_proj,
        third_in_bias[None],
        third_out_proj,
        third_out_bias[None],
    )
    inner = pl.pallas_call(
        inner_kernel,
        out_shape=shape(7, WIN * WIN, D),
        in_specs=[in_smem()] + [in_vmem()] * 7,
        out_specs=in_vmem(),
        compiler_params=params(32),
        cost_estimate=cost(18),
        name="inner_windows",
    )(window_keep, image, *third)

    above, below, send_down_rest, send_up_rest = lax.optimization_barrier(
        (above, below, send_down_rest, send_up_rest)
    )
    own_left, own_right = pl.pallas_call(
        strip_kernel,
        out_shape=(shape(24, WIN, D), shape(25, WIN, D)),
        in_specs=[in_smem()] + [in_vmem()] * 3,
        out_specs=(in_vmem(),) * 2,
        compiler_params=params(16),
        cost_estimate=cost(1),
        name="pack_columns",
    )(window_keep, image, above, below)
    above_rest = shifted(send_down_rest, "narrow", 1)
    below_rest = shifted(send_up_rest, "narrow", -1)
    far_left = shifted(own_right, "wide", 1)
    far_right = shifted(own_left, "wide", -1)
    work = [
        pltpu.VMEM((256, D), BF16),
        pltpu.VMEM((512, D), BF16),
        pltpu.VMEM((512, D), BF16),
        pltpu.VMEM((256, D), BF16),
    ]
    outer_halves = pl.pallas_call(
        half_outer_kernel,
        out_shape=shape(4, 2, 128, D),
        in_specs=[in_smem()] + [in_vmem()] * 9,
        out_specs=in_vmem(),
        scratch_shapes=work,
        compiler_params=params(32),
        cost_estimate=cost(14),
        name="half_windows_outer",
    )(window_keep, image, above, below, *third)
    inner_halves = pl.pallas_call(
        half_inner_kernel,
        out_shape=shape(3, 2, 128, D),
        in_specs=[in_smem()] + [in_vmem()] * 11,
        out_specs=in_vmem(),
        scratch_shapes=work + [pltpu.VMEM((2, 512, D), BF16)],
        compiler_params=params(32),
        cost_estimate=cost(10),
        name="half_windows_inner",
    )(window_keep, image, above, below, above_rest, below_rest, *third)
    merging = (merge_gain[None], merge_bias[None], merge_weight)
    scratch = [
        pltpu.VMEM((4, 32, 128, 128), F32),
        pltpu.VMEM((2, WIN, WIN, E), BF16),
        pltpu.SemaphoreType.DMA((2,)),
    ]
    work = [
        pltpu.VMEM((512, D), BF16),
        pltpu.VMEM((1536, D), BF16),
        pltpu.VMEM((1536, D), BF16),
        pltpu.VMEM((512, D), BF16),
    ]
    attended = (inner, outer_halves, inner_halves)
    merged, first, second, edges = pl.pallas_call(
        edge_kernel,
        out_shape=(shape(16, 64, E), shape(WIN * WIN, E), shape(WIN * WIN, E), shape(512, D)),
        in_specs=[in_smem()] * 2 + [in_vmem()] * 16,
        out_specs=(in_hbm(),) + (in_vmem(),) * 3,
        scratch_shapes=scratch[:2] + work + scratch[2:],
        compiler_params=params(40),
        cost_estimate=cost(12),
        name="edge_windows",
    )(window_keep, window_route, own_left, own_right, far_left, far_right, *attended, *third, *merging)
    incoming_first = shifted(first, "wide", 1)
    incoming_second = shifted(second, "wide", 1)
    merged, third, fourth = pl.pallas_call(
        rest_kernel,
        out_shape=(shape(16, 64, E), shape(WIN * WIN, E), shape(WIN * WIN, E)),
        in_specs=[in_smem(), in_hbm()] + [in_vmem()] * 7,
        out_specs=(in_hbm(), in_vmem(), in_vmem()),
        scratch_shapes=scratch,
        input_output_aliases={1: 0},
        compiler_params=params(32),
        cost_estimate=cost(5),
        name="rest_merging",
    )(window_route, merged, *attended, edges, *merging)
    own = (first, second, third, fourth)
    top = (
        fourth_norm_gain[None],
        fourth_norm_bias[None],
        fourth_in_proj,
        fourth_in_bias[None],
        fourth_out_proj,
        fourth_out_bias[None],
    )
    scratch = [
        pltpu.VMEM((WIN * WIN, E), BF16),
        pltpu.VMEM((WIN * WIN, E), BF16),
        pltpu.SemaphoreType.DMA,
    ]
    slots = pl.pallas_call(
        top_first,
        out_shape=shape(1, 2, WIN * WIN, E),
        in_specs=[in_smem()] + [in_vmem()] * 11,
        out_specs=in_hbm(),
        scratch_shapes=scratch,
        compiler_params=params(32),
        cost_estimate=cost(8),
        name="top_first",
    )(window_route, *own, incoming_first, *top)
    slots = pl.pallas_call(
        top_second,
        out_shape=shape(1, 2, WIN * WIN, E),
        in_specs=[in_smem()] + [in_vmem()] * 12 + [in_hbm()],
        out_specs=in_hbm(),
        scratch_shapes=scratch,
        input_output_aliases={13: 0},
        compiler_params=params(32),
        cost_estimate=cost(8),
        name="top_second",
    )(window_route, *own, incoming_first, incoming_second, *top, slots)
    return merged, slots


def solution(mesh):
    placed = (
        P("narrow", "wide", None),
        P(),
        P(),
        P(),
        P(),
        P(),
        P(),
        P("narrow", "wide"),
        P(),
        P(),
        P(),
        P(),
        P(),
        P(),
        P(),
        P(),
        P(),
        P("narrow", None),
    )
    return jax.shard_map(
        shards,
        mesh=mesh,
        in_specs=placed,
        out_specs=(P("narrow", "wide", None), P("narrow", "wide", None, None)),
        check_vma=False,
    )
```

```python
import jax
import jax.numpy as jnp
from jax import lax
from jax.experimental import pallas as pl
from jax.experimental.pallas import tpu as pltpu
from jax.sharding import PartitionSpec as P

D = 512
HEADS_D = 16
E = 1024
HEADS_E = 32
WIN = 16
SHIFT = 8
HEAD = 32
PACK = 4
EPSILON = 1e-05
LOG2E = 1.4426950408889634
QSCALE = HEAD ** (-0.5) * LOG2E
BF16 = jnp.bfloat16
F32 = jnp.float32


def matmul(a, b):
    return jnp.dot(a, b, preferred_element_type=F32)


def layer_norm(values, gain, bias):
    center = jnp.mean(values, axis=-1, keepdims=True)
    offsets = values - center
    spread = jnp.mean(offsets * offsets, axis=-1, keepdims=True)
    return (offsets * lax.rsqrt(spread + EPSILON) * gain + bias).astype(BF16)


def attend(q, k, v):
    count = q.shape[0]
    lane = lax.broadcasted_iota(jnp.int32, (count, PACK * HEAD), 1)
    stacked = jnp.concatenate(
        [jnp.where((lane >= HEAD * h) & (lane < HEAD * h + HEAD), q, 0) for h in range(PACK)], axis=0
    )
    scores = lax.dot_general(stacked, k, (((1,), (1,)), ((), ())), preferred_element_type=F32)
    weights = jnp.exp2(scores - jnp.max(scores, axis=1, keepdims=True)).astype(BF16)
    sums = matmul(weights, jnp.concatenate([v, jnp.ones_like(v)], axis=1))
    total = sums[:count]
    lane = lax.broadcasted_iota(jnp.int32, total.shape, 1) % (PACK * HEAD)
    for h in range(1, PACK):
        total = jnp.where(lane >= HEAD * h, sums[count * h : count * (h + 1)], total)
    return (total[:, : PACK * HEAD] / total[:, PACK * HEAD :]).astype(BF16)


def attention_three(tokens, count, refs):
    gain, bias, in_proj, in_bias, out_proj, out_bias = refs
    normed = layer_norm(tokens, gain[...], bias[...])
    q = ((matmul(normed[:count], in_proj[:, :D]) + in_bias[:D][None]) * QSCALE).astype(BF16)
    k = (matmul(normed, in_proj[:, D : 2 * D]) + in_bias[D : 2 * D][None]).astype(BF16)
    v = (matmul(normed, in_proj[:, 2 * D :]) + in_bias[2 * D : 3 * D][None]).astype(BF16)
    width = PACK * HEAD
    context = jnp.concatenate(
        [attend(q[:, c : c + width], k[:, c : c + width], v[:, c : c + width]) for c in range(0, D, width)],
        axis=1,
    )
    return (matmul(context, out_proj[...]) + out_bias[...] + tokens[:count]).astype(BF16)


def column(j):
    return pl.multiple_of(j * WIN, WIN)


def strip_kernel(keep, keep_above, image, above, below, left, right):
    for side, out in enumerate((left, right)):
        base, start = (0, 7 * WIN)[side], SHIFT * side
        for pair in range(24):
            rows = []
            for r in (2 * pair, 2 * pair + 1):
                if r < SHIFT:
                    block = above[96 * r + (0, 80)[side] : 96 * r + (16, 96)[side]]
                elif r < 5 * SHIFT:
                    block = image[r - SHIFT, base : base + WIN]
                else:
                    q = r - 5 * SHIFT
                    block = below[96 * q + (0, 80)[side] : 96 * q + (16, 96)[side]]
                rows.append(block.astype(F32)[start : start + SHIFT])
            out[pair] = jnp.concatenate(rows, axis=0).astype(BF16)
    lanes = lax.broadcasted_iota(jnp.int32, (WIN, D), 1)
    flags = jnp.where(lanes == 0, keep_above[1, 7].astype(F32), 0.0)
    for a in range(2):
        flags = jnp.where(lanes == a + 1, keep[a, 7].astype(F32), flags)
    right[24] = flags.astype(BF16)


def inner_kernel(keep, image, gain, bias, in_proj, in_bias, out_proj, out_bias, out):
    refs = (gain, bias, in_proj, in_bias, out_proj, out_bias)

    @pl.loop(0, 7)
    def _(j):
        both = image[SHIFT : SHIFT + WIN, pl.ds(column(j), 2 * WIN), :].astype(F32)
        tokens = both[:, SHIFT : SHIFT + WIN, :].reshape(WIN * WIN, D)

        @pl.when(keep[0, j] == 1)
        def _():
            out[j] = attention_three(tokens, WIN * WIN, refs)

        @pl.when(keep[0, j] != 1)
        def _():
            out[j] = tokens.astype(BF16)


def flag_at(flags, lane):
    lanes = lax.broadcasted_iota(jnp.int32, (WIN, 128), 1)
    return jnp.max(jnp.where(lanes == lane, flags[:, :128].astype(F32), 0.0)) > 0.5


def project(normed, queries, in_proj, in_bias, q_ref, k_ref, v_ref):
    q = (matmul(queries, in_proj[:, :D]) + in_bias[:D][None]) * QSCALE
    q_ref[...] = q.astype(BF16)
    k_ref[...] = (matmul(normed, in_proj[:, D : 2 * D]) + in_bias[D : 2 * D][None]).astype(BF16)
    v_ref[...] = (matmul(normed, in_proj[:, 2 * D :]) + in_bias[2 * D : 3 * D][None]).astype(BF16)


def attend_window(first, count, window, q_ref, k_ref, v_ref, context):
    width = PACK * HEAD
    mine, keys = slice(first, first + count), slice(WIN * WIN * window, WIN * WIN * (window + 1))
    for c in range(0, D, width):
        cols = slice(c, c + width)
        context[mine, cols] = attend(q_ref[mine, cols], k_ref[keys, cols], v_ref[keys, cols])


def half_pair(keep, image, j, far, top_kept, refs, out, step, scratch):
    gain, bias, in_proj, in_bias, out_proj, out_bias = refs
    narrow, rows = lax.axis_index("narrow"), lax.axis_size("narrow")
    q_ref, k_ref, v_ref, context = scratch
    tokens = []
    for side in range(2):
        row = 3 * SHIFT * side
        own = image[row : row + SHIFT, pl.ds(column(j), 2 * WIN), :].astype(F32)
        own = own[:, SHIFT : SHIFT + WIN].reshape(-1, D)
        tokens.append((own, jnp.where(narrow == (0, rows - 1)[side], own, far(side))))
    kept = [top_kept, keep[1, j] == 1]

    @pl.when(kept[0] | kept[1])
    def _():
        normed = [[layer_norm(part, gain[...], bias[...]) for part in pair] for pair in tokens]
        queries = jnp.concatenate([normed[0][0], normed[1][0]], axis=0)
        project(jnp.concatenate(normed[0] + normed[1], axis=0), queries, in_proj, in_bias, q_ref, k_ref, v_ref)

    for side in range(2):

        @pl.when(kept[side])
        def _():
            attend_window(128 * side, 128, side, q_ref, k_ref, v_ref, context)

    @pl.when(kept[0] | kept[1])
    def _():
        result = matmul(context[...], out_proj[...]) + out_bias[...]
        for side in range(2):
            own = tokens[side][0]
            new = own + result[128 * side : 128 * side + 128]
            out[step, side] = jnp.where(kept[side], new, own).astype(BF16)

    @pl.when(jnp.logical_not(kept[0] | kept[1]))
    def _():
        for side in range(2):
            out[step, side] = tokens[side][0].astype(BF16)


def gather_rows(ref, pitch, start):
    rows = [ref[pl.ds(pitch * r + start, 2 * WIN), :].astype(F32)[SHIFT : SHIFT + WIN] for r in range(SHIFT)]
    return jnp.concatenate(rows, axis=0)


def half_outer_kernel(
    keep, keep_above, image, above, below, gain, bias, in_proj, in_bias, out_proj, out_bias, out, *scratch
):
    refs = (gain, bias, in_proj, in_bias, out_proj, out_bias)

    @pl.loop(0, 4)
    def _(step):
        late = (step >= 2).astype(jnp.int32)
        j = step + 3 * late
        start = pl.multiple_of((step + late) * WIN, WIN)
        far = lambda side: gather_rows((above, below)[side], 96, start)
        half_pair(keep, image, j, far, keep_above[1, j] == 1, refs, out, step, scratch)


def half_inner_kernel(
    keep, keep_above, image, above, below, above_rest, below_rest, gain, bias, in_proj, in_bias, out_proj, out_bias, out, *scratch
):
    refs = (gain, bias, in_proj, in_bias, out_proj, out_bias)
    rows = scratch[4]
    for side in range(2):
        early, late = (above, below)[side], (above_rest, below_rest)[side]
        for r in range(SHIFT):
            rows[side, 64 * r : 64 * r + 16] = early[96 * r + 32 : 96 * r + 48]
            rows[side, 64 * r + 16 : 64 * r + 48] = late[32 * r : 32 * r + 32]
            rows[side, 64 * r + 48 : 64 * r + 64] = early[96 * r + 48 : 96 * r + 64]

    @pl.loop(0, 3)
    def _(step):
        j = step + 2
        far = lambda side: gather_rows(rows.at[side], 64, column(step))
        half_pair(keep, image, j, far, keep_above[1, j] == 1, refs, out, step, scratch[:4])


def store(layer, rows, cols, values):
    for c in range(4):
        layer[c, rows, cols, :] = values[:, :, 128 * c : 128 * c + 128]


def lay_out(layer, inner, outer_halves, inner_halves):
    @pl.loop(0, 7)
    def _(j):
        cols = pl.ds(pl.multiple_of(j * WIN + SHIFT, SHIFT), WIN)
        store(layer, slice(SHIFT, SHIFT + WIN), cols, inner[j].astype(F32).reshape(WIN, WIN, D))

    for ref, columns in ((outer_halves, (0, 1, 5, 6)), (inner_halves, (2, 3, 4))):
        for step, j in enumerate(columns):
            cols = slice(j * WIN + SHIFT, j * WIN + SHIFT + WIN)
            for side in range(2):
                rows = slice(3 * SHIFT * side, 3 * SHIFT * side + SHIFT)
                store(layer, rows, cols, ref[step, side].astype(F32).reshape(SHIFT, WIN, D))


def lay_out_edges(layer, edges):
    for side in range(2):
        col = slice(15 * SHIFT * side, 15 * SHIFT * side + SHIFT)
        values = edges[128 * side : 128 * side + 128].astype(F32)
        store(layer, slice(SHIFT, SHIFT + WIN), col, values.reshape(WIN, SHIFT, D))
        for down in range(2):
            row = slice(3 * SHIFT * down, 3 * SHIFT * down + SHIFT)
            first = 256 + 64 * (2 * down + side)
            store(layer, row, col, edges[first : first + 64].astype(F32).reshape(SHIFT, SHIFT, D))


def merge_order(route, first):
    wide = lax.axis_index("wide")
    moves = [(route[0, 4 * wide + j] == 2).astype(jnp.int32) for j in range(4)]
    total = moves[0] + moves[1] + moves[2] + moves[3]
    chosen = [0, 0]
    moved, stayed = 0, 0
    for j in range(4):
        position = jnp.where(moves[j] == 1, moved, total + stayed)
        for slot in range(2):
            chosen[slot] = jnp.where(position == first + slot, j, chosen[slot])
        moved = moved + moves[j]
        stayed = stayed + 1 - moves[j]
    return chosen


def merge_two(route, start, layer, gain, bias, weight, merged, results, sem, outs):
    chosen = merge_order(route, start)
    blocks = []
    for group in chosen:
        parts = []
        for odd_col in range(2):
            cols = pl.ds(group * 32 + odd_col, WIN, stride=2)
            for odd_row in range(2):
                for c in range(4):
                    parts.append(
                        jnp.concatenate([layer[c, 2 * r + odd_row, cols, :] for r in range(WIN)], axis=0)
                    )
        blocks.append(layer_norm(jnp.concatenate(parts, axis=1), gain[...], bias[...]))
    result = matmul(jnp.concatenate(blocks, axis=0), weight[...]).astype(BF16)
    copies = []
    for slot, group in enumerate(chosen):
        part = result[256 * slot : 256 * slot + 256]
        if outs is not None:
            outs[slot][...] = part
        results[slot] = part.reshape(WIN, WIN, E)
        copy = pltpu.make_async_copy(results.at[slot], merged.at[:, pl.ds(column(group), WIN), :], sem.at[slot])
        copy.start()
        copies.append(copy)
    for copy in copies:
        copy.wait()


def edge_kernel(
    keep,
    keep_above,
    route,
    own_left,
    own_right,
    far_left,
    far_right,
    inner,
    outer_halves,
    inner_halves,
    gain,
    bias,
    in_proj,
    in_bias,
    out_proj,
    out_bias,
    merge_gain,
    merge_bias,
    merge_weight,
    merged,
    first,
    second,
    edges,
    layer,
    results,
    q_ref,
    k_ref,
    v_ref,
    context,
    sem,
):
    narrow, rows = lax.axis_index("narrow"), lax.axis_size("narrow")
    wide, groups = lax.axis_index("wide"), lax.axis_size("wide")
    flags = far_left[24]

    def strip(ref, low, high):
        return ref[low // 2 : high // 2].astype(F32).reshape(-1, D)

    windows = []
    for side in range(2):
        near, far = (own_left, own_right)[side], (far_left, far_right)[side]
        edge_col = wide == (0, groups - 1)[side]
        own = strip(near, 16, 32)
        beside = jnp.where(edge_col, own, strip(far, 16, 32))
        kept = flag_at(flags, 1) if side == 0 else keep[0, 7] == 1
        windows.append((kept, own, [own, beside]))
    for down in range(2):
        for side in range(2):
            near, far = (own_left, own_right)[side], (far_left, far_right)[side]
            edge_col = wide == (0, groups - 1)[side]
            edge_row = narrow == (0, rows - 1)[down]
            mine, beyond = ((8, 0), (32, 40))[down]
            own = strip(near, mine, mine + SHIFT)
            across = jnp.where(edge_row, own, strip(near, beyond, beyond + SHIFT))
            beside = jnp.where(edge_col, own, strip(far, mine, mine + SHIFT))
            corner = strip(far, beyond, beyond + SHIFT)
            corner = jnp.where(edge_col, across, jnp.where(edge_row, beside, corner))
            if side == 0:
                kept = flag_at(flags, 2 * down)
            elif down == 0:
                kept = keep_above[1, 7] == 1
            else:
                kept = keep[1, 7] == 1
            windows.append((kept, own, [own, across, beside, corner]))
    normed = [[layer_norm(part, gain[...], bias[...]) for part in parts] for _, _, parts in windows]
    queries = jnp.concatenate([parts[0] for parts in normed], axis=0)
    normed = jnp.concatenate([part for parts in normed for part in parts], axis=0)
    project(normed, queries, in_proj, in_bias, q_ref, k_ref, v_ref)
    place = 0
    for window, (kept, own, _) in enumerate(windows):
        count = own.shape[0]

        @pl.when(kept)
        def _():
            attend_window(place, count, window, q_ref, k_ref, v_ref, context)

        place += count
    result = matmul(context[...], out_proj[...]) + out_bias[...]
    place = 0
    for kept, own, _ in windows:
        mine = slice(place, place + own.shape[0])
        edges[mine] = jnp.where(kept, own + result[mine], own).astype(BF16)
        place += own.shape[0]
    lay_out(layer, inner, outer_halves, inner_halves)
    lay_out_edges(layer, edges)
    merge_two(route, 0, layer, merge_gain, merge_bias, merge_weight, merged, results, sem, (first, second))


def rest_kernel(
    route, earlier, inner, outer_halves, inner_halves, edges, gain, bias, weight, merged, third, fourth, layer, results, sem
):
    lay_out(layer, inner, outer_halves, inner_halves)
    lay_out_edges(layer, edges)
    merge_two(route, 2, layer, gain, bias, weight, merged, results, sem, (third, fourth))


def top_kernel(slot, route, own, incoming, gain, bias, in_proj, in_bias, out_proj, out_bias, *rest):
    out, tokens_ref, result, sem = rest[-4:]
    wide, groups = lax.axis_index("wide"), lax.axis_size("wide")
    before = jnp.where(wide == 0, groups - 1, wide - 1)
    homes = 0
    arriving = 0
    chosen = 0
    for j in range(4):
        stays = route[0, 4 * wide + j] == 1
        chosen = jnp.where(stays & (homes == slot), j, chosen)
        homes = homes + stays.astype(jnp.int32)
        arriving = arriving + (route[0, 4 * before + j] == 2).astype(jnp.int32)
    order = merge_order(route, 0) + merge_order(route, 2)
    width = PACK * HEAD
    filled = slot < homes + arriving

    for position in range(4):

        @pl.when((slot < homes) & (order[position] == chosen))
        def _():
            tokens_ref[...] = own[position][...]

    for source in range(slot + 1):

        @pl.when(homes + source == slot)
        def _():
            tokens_ref[...] = incoming[source][...]

    @pl.when(filled)
    def _():
        tokens = tokens_ref[...].astype(F32)
        normed = layer_norm(tokens, gain[...], bias[...])
        context = []
        for c in range(0, E, 2 * width):
            cols = slice(c, c + 2 * width)
            q = ((matmul(normed, in_proj[:, cols]) + in_bias[cols][None]) * QSCALE).astype(BF16)
            cols = slice(E + c, E + c + 2 * width)
            k = (matmul(normed, in_proj[:, cols]) + in_bias[cols][None]).astype(BF16)
            cols = slice(2 * E + c, 2 * E + c + 2 * width)
            v = (matmul(normed, in_proj[:, cols]) + in_bias[cols][None]).astype(BF16)
            for a in (0, width):
                context.append(attend(q[:, a : a + width], k[:, a : a + width], v[:, a : a + width]))
        value = matmul(jnp.concatenate(context, axis=1), out_proj[...]) + out_bias[...] + tokens
        result[...] = value.astype(BF16)

    @pl.when(jnp.logical_not(filled))
    def _():
        result[...] = jnp.zeros((WIN * WIN, E), BF16)

    copy = pltpu.make_async_copy(result, out.at[0, slot], sem)
    copy.start()
    copy.wait()


def top_first(route, first, second, third, fourth, one, *rest):
    top_kernel(0, route, (first, second, third, fourth), (one,), *rest)


def top_second(route, first, second, third, fourth, one, two, *rest):
    top_kernel(1, route, (first, second, third, fourth), (one, two), *rest)


def in_smem():
    return pl.BlockSpec(memory_space=pltpu.SMEM)


def in_vmem():
    return pl.BlockSpec(memory_space=pltpu.VMEM)


def in_hbm():
    return pl.BlockSpec(memory_space=pltpu.HBM)


def shifted(block, axis, distance):
    count = lax.axis_size(axis)
    return lax.ppermute(block, axis, [((i - distance) % count, i) for i in range(count)])


def shape(*sizes):
    return jax.ShapeDtypeStruct(sizes, BF16)


def params(mib):
    return pltpu.CompilerParams(vmem_limit_bytes=mib * 2**20)


def cost(us):
    return pl.CostEstimate(flops=us * 10**9, bytes_accessed=4_000_000, transcendentals=0)


def shards(
    image,
    third_norm_gain,
    third_norm_bias,
    third_in_proj,
    third_in_bias,
    third_out_proj,
    third_out_bias,
    window_keep,
    merge_gain,
    merge_bias,
    merge_weight,
    fourth_norm_gain,
    fourth_norm_bias,
    fourth_in_proj,
    fourth_in_bias,
    fourth_out_proj,
    fourth_out_bias,
    window_route,
):
    low, high = 3 * WIN, 5 * WIN

    def row_parts(rows):
        early = jnp.concatenate([rows[:, :low], rows[:, high:]], axis=1)
        return early.reshape(-1, D), rows[:, low:high].reshape(-1, D)

    keep_above = shifted(window_keep, "narrow", 1)
    send_down, send_down_rest = row_parts(image[3 * SHIFT :])
    send_up, send_up_rest = row_parts(image[:SHIFT])
    above = shifted(send_down, "narrow", 1)
    below = shifted(send_up, "narrow", -1)
    third = (
        third_norm_gain[None],
        third_norm_bias[None],
        third_in_proj,
        third_in_bias,
        third_out_proj,
        third_out_bias[None],
    )
    inner = pl.pallas_call(
        inner_kernel,
        out_shape=shape(7, WIN * WIN, D),
        in_specs=[in_smem()] + [in_vmem()] * 7,
        out_specs=in_vmem(),
        compiler_params=params(24),
        cost_estimate=cost(18),
        name="inner_windows",
    )(window_keep, image, *third)

    above, below, send_down_rest, send_up_rest = lax.optimization_barrier(
        (above, below, send_down_rest, send_up_rest)
    )
    own_left, own_right = pl.pallas_call(
        strip_kernel,
        out_shape=(shape(24, WIN, D), shape(25, WIN, D)),
        in_specs=[in_smem()] * 2 + [in_vmem()] * 3,
        out_specs=(in_vmem(),) * 2,
        compiler_params=params(12),
        cost_estimate=cost(1),
        name="pack_columns",
    )(window_keep, keep_above, image, above, below)
    above, below, own_left, own_right = lax.optimization_barrier((above, below, own_left, own_right))
    above_rest = shifted(send_down_rest, "narrow", 1)
    below_rest = shifted(send_up_rest, "narrow", -1)
    far_left = shifted(own_right, "wide", 1)
    far_right = shifted(own_left, "wide", -1)
    work = [
        pltpu.VMEM((256, D), BF16),
        pltpu.VMEM((512, D), BF16),
        pltpu.VMEM((512, D), BF16),
        pltpu.VMEM((256, D), BF16),
    ]
    outer_halves = pl.pallas_call(
        half_outer_kernel,
        out_shape=shape(4, 2, 128, D),
        in_specs=[in_smem()] * 2 + [in_vmem()] * 9,
        out_specs=in_vmem(),
        scratch_shapes=work,
        compiler_params=params(24),
        cost_estimate=cost(14),
        name="half_windows_outer",
    )(window_keep, keep_above, image, above, below, *third)
    inner_halves = pl.pallas_call(
        half_inner_kernel,
        out_shape=shape(3, 2, 128, D),
        in_specs=[in_smem()] * 2 + [in_vmem()] * 11,
        out_specs=in_vmem(),
        scratch_shapes=work + [pltpu.VMEM((2, 512, D), BF16)],
        compiler_params=params(24),
        cost_estimate=cost(10),
        name="half_windows_inner",
    )(window_keep, keep_above, image, above, below, above_rest, below_rest, *third)
    merging = (merge_gain[None], merge_bias[None], merge_weight)
    scratch = [
        pltpu.VMEM((4, 32, 128, 128), F32),
        pltpu.VMEM((2, WIN, WIN, E), BF16),
        pltpu.SemaphoreType.DMA((2,)),
    ]
    work = [
        pltpu.VMEM((512, D), BF16),
        pltpu.VMEM((1536, D), BF16),
        pltpu.VMEM((1536, D), BF16),
        pltpu.VMEM((512, D), BF16),
    ]
    attended = (inner, outer_halves, inner_halves)
    merged, first, second, edges = pl.pallas_call(
        edge_kernel,
        out_shape=(shape(16, 64, E), shape(WIN * WIN, E), shape(WIN * WIN, E), shape(512, D)),
        in_specs=[in_smem()] * 3 + [in_vmem()] * 16,
        out_specs=(in_hbm(),) + (in_vmem(),) * 3,
        scratch_shapes=scratch[:2] + work + scratch[2:],
        compiler_params=params(36),
        cost_estimate=cost(12),
        name="edge_windows",
    )(window_keep, keep_above, window_route, own_left, own_right, far_left, far_right, *attended, *third, *merging)
    incoming_first = shifted(first, "wide", 1)
    incoming_second = shifted(second, "wide", 1)
    merged, third, fourth = pl.pallas_call(
        rest_kernel,
        out_shape=(shape(16, 64, E), shape(WIN * WIN, E), shape(WIN * WIN, E)),
        in_specs=[in_smem(), in_hbm()] + [in_vmem()] * 7,
        out_specs=(in_hbm(), in_vmem(), in_vmem()),
        scratch_shapes=scratch,
        input_output_aliases={1: 0},
        compiler_params=params(24),
        cost_estimate=cost(5),
        name="rest_merging",
    )(window_route, merged, *attended, edges, *merging)
    own = (first, second, third, fourth)
    top = (
        fourth_norm_gain[None],
        fourth_norm_bias[None],
        fourth_in_proj,
        fourth_in_bias,
        fourth_out_proj,
        fourth_out_bias[None],
    )
    scratch = [
        pltpu.VMEM((WIN * WIN, E), BF16),
        pltpu.VMEM((WIN * WIN, E), BF16),
        pltpu.SemaphoreType.DMA,
    ]
    slots = pl.pallas_call(
        top_first,
        out_shape=shape(1, 2, WIN * WIN, E),
        in_specs=[in_smem()] + [in_vmem()] * 11,
        out_specs=in_hbm(),
        scratch_shapes=scratch,
        compiler_params=params(24),
        cost_estimate=cost(8),
        name="top_first",
    )(window_route, *own, incoming_first, *top)
    slots = pl.pallas_call(
        top_second,
        out_shape=shape(1, 2, WIN * WIN, E),
        in_specs=[in_smem()] + [in_vmem()] * 12 + [in_hbm()],
        out_specs=in_hbm(),
        scratch_shapes=scratch,
        input_output_aliases={13: 0},
        compiler_params=params(24),
        cost_estimate=cost(8),
        name="top_second",
    )(window_route, *own, incoming_first, incoming_second, *top, slots)
    return merged, slots


def solution(mesh):
    placed = (
        P("narrow", "wide", None),
        P(),
        P(),
        P(),
        P(),
        P(),
        P(),
        P("narrow", "wide"),
        P(),
        P(),
        P(),
        P(),
        P(),
        P(),
        P(),
        P(),
        P(),
        P("narrow", None),
    )
    return jax.shard_map(
        shards,
        mesh=mesh,
        in_specs=placed,
        out_specs=(P("narrow", "wide", None), P("narrow", "wide", None, None)),
        check_vma=False,
    )
```

```python
import jax
import jax.numpy as jnp
from jax import lax
from jax.experimental import pallas as pl
from jax.experimental.pallas import tpu as pltpu
from jax.sharding import PartitionSpec as P

D = 512
HEADS_D = 16
E = 1024
HEADS_E = 32
WIN = 16
SHIFT = 8
HEAD = 32
PACK = 4
EPSILON = 1e-05
LOG2E = 1.4426950408889634
QSCALE = HEAD ** (-0.5) * LOG2E
BF16 = jnp.bfloat16
F32 = jnp.float32


def matmul(a, b):
    return jnp.dot(a, b, preferred_element_type=F32)


def layer_norm(values, gain, bias):
    center = jnp.mean(values, axis=-1, keepdims=True)
    offsets = values - center
    spread = jnp.mean(offsets * offsets, axis=-1, keepdims=True)
    return (offsets * lax.rsqrt(spread + EPSILON) * gain + bias).astype(BF16)


def attend(q, k, v):
    count = q.shape[0]
    lane = lax.broadcasted_iota(jnp.int32, (count, PACK * HEAD), 1)
    stacked = jnp.concatenate(
        [jnp.where((lane >= HEAD * h) & (lane < HEAD * h + HEAD), q, 0) for h in range(PACK)], axis=0
    )
    scores = lax.dot_general(stacked, k, (((1,), (1,)), ((), ())), preferred_element_type=F32)
    weights = jnp.exp2(scores - jnp.max(scores, axis=1, keepdims=True)).astype(BF16)
    sums = matmul(weights, jnp.concatenate([v, jnp.ones_like(v)], axis=1))
    total = sums[:count]
    lane = lax.broadcasted_iota(jnp.int32, total.shape, 1) % (PACK * HEAD)
    for h in range(1, PACK):
        total = jnp.where(lane >= HEAD * h, sums[count * h : count * (h + 1)], total)
    return (total[:, : PACK * HEAD] / total[:, PACK * HEAD :]).astype(BF16)


def attention_three(tokens, count, refs):
    gain, bias, in_proj, in_bias, out_proj, out_bias = refs
    normed = layer_norm(tokens, gain[...], bias[...])
    q = ((matmul(normed[:count], in_proj[:, :D]) + in_bias[:D][None]) * QSCALE).astype(BF16)
    k = (matmul(normed, in_proj[:, D : 2 * D]) + in_bias[D : 2 * D][None]).astype(BF16)
    v = (matmul(normed, in_proj[:, 2 * D :]) + in_bias[2 * D : 3 * D][None]).astype(BF16)
    width = PACK * HEAD
    context = jnp.concatenate(
        [attend(q[:, c : c + width], k[:, c : c + width], v[:, c : c + width]) for c in range(0, D, width)],
        axis=1,
    )
    return (matmul(context, out_proj[...]) + out_bias[...] + tokens[:count]).astype(BF16)


def column(j):
    return pl.multiple_of(j * WIN, WIN)


def strip_kernel(keep, keep_above, image, above, below, left, right):
    for side, out in enumerate((left, right)):
        base, start = (0, 7 * WIN)[side], SHIFT * side
        for pair in range(24):
            rows = []
            for r in (2 * pair, 2 * pair + 1):
                if r < SHIFT:
                    block = above[96 * r + (0, 80)[side] : 96 * r + (16, 96)[side]]
                elif r < 5 * SHIFT:
                    block = image[r - SHIFT, base : base + WIN]
                else:
                    q = r - 5 * SHIFT
                    block = below[96 * q + (0, 80)[side] : 96 * q + (16, 96)[side]]
                rows.append(block.astype(F32)[start : start + SHIFT])
            out[pair] = jnp.concatenate(rows, axis=0).astype(BF16)
    lanes = lax.broadcasted_iota(jnp.int32, (WIN, D), 1)
    flags = jnp.where(lanes == 0, keep_above[1, 7].astype(F32), 0.0)
    for a in range(2):
        flags = jnp.where(lanes == a + 1, keep[a, 7].astype(F32), flags)
    right[24] = flags.astype(BF16)


def inner_kernel(keep, image, gain, bias, in_proj, in_bias, out_proj, out_bias, out):
    refs = (gain, bias, in_proj, in_bias, out_proj, out_bias)

    @pl.loop(0, 7)
    def _(j):
        both = image[SHIFT : SHIFT + WIN, pl.ds(column(j), 2 * WIN), :].astype(F32)
        tokens = both[:, SHIFT : SHIFT + WIN, :].reshape(WIN * WIN, D)

        @pl.when(keep[0, j] == 1)
        def _():
            out[j] = attention_three(tokens, WIN * WIN, refs)

        @pl.when(keep[0, j] != 1)
        def _():
            out[j] = tokens.astype(BF16)


def flag_at(flags, lane):
    lanes = lax.broadcasted_iota(jnp.int32, (WIN, 128), 1)
    return jnp.max(jnp.where(lanes == lane, flags[:, :128].astype(F32), 0.0)) > 0.5


def project(normed, queries, in_proj, in_bias, q_ref, k_ref, v_ref):
    q = (matmul(queries, in_proj[:, :D]) + in_bias[:D][None]) * QSCALE
    q_ref[...] = q.astype(BF16)
    k_ref[...] = (matmul(normed, in_proj[:, D : 2 * D]) + in_bias[D : 2 * D][None]).astype(BF16)
    v_ref[...] = (matmul(normed, in_proj[:, 2 * D :]) + in_bias[2 * D : 3 * D][None]).astype(BF16)


def attend_window(first, count, window, q_ref, k_ref, v_ref, context):
    width = PACK * HEAD
    mine, keys = slice(first, first + count), slice(WIN * WIN * window, WIN * WIN * (window + 1))
    for c in range(0, D, width):
        cols = slice(c, c + width)
        context[mine, cols] = attend(q_ref[mine, cols], k_ref[keys, cols], v_ref[keys, cols])


def half_pair(keep, image, j, far, top_kept, refs, out, step, scratch):
    gain, bias, in_proj, in_bias, out_proj, out_bias = refs
    narrow, rows = lax.axis_index("narrow"), lax.axis_size("narrow")
    q_ref, k_ref, v_ref, context = scratch
    tokens = []
    for side in range(2):
        row = 3 * SHIFT * side
        own = image[row : row + SHIFT, pl.ds(column(j), 2 * WIN), :].astype(F32)
        own = own[:, SHIFT : SHIFT + WIN].reshape(-1, D)
        tokens.append((own, jnp.where(narrow == (0, rows - 1)[side], own, far(side))))
    kept = [top_kept, keep[1, j] == 1]

    @pl.when(kept[0] | kept[1])
    def _():
        normed = [[layer_norm(part, gain[...], bias[...]) for part in pair] for pair in tokens]
        queries = jnp.concatenate([normed[0][0], normed[1][0]], axis=0)
        project(jnp.concatenate(normed[0] + normed[1], axis=0), queries, in_proj, in_bias, q_ref, k_ref, v_ref)

    for side in range(2):

        @pl.when(kept[side])
        def _():
            attend_window(128 * side, 128, side, q_ref, k_ref, v_ref, context)

    @pl.when(kept[0] | kept[1])
    def _():
        result = matmul(context[...], out_proj[...]) + out_bias[...]
        for side in range(2):
            own = tokens[side][0]
            new = own + result[128 * side : 128 * side + 128]
            out[step, side] = jnp.where(kept[side], new, own).astype(BF16)

    @pl.when(jnp.logical_not(kept[0] | kept[1]))
    def _():
        for side in range(2):
            out[step, side] = tokens[side][0].astype(BF16)


def gather_rows(ref, pitch, start):
    rows = [ref[pl.ds(pitch * r + start, 2 * WIN), :].astype(F32)[SHIFT : SHIFT + WIN] for r in range(SHIFT)]
    return jnp.concatenate(rows, axis=0)


def half_outer_kernel(
    keep, keep_above, image, above, below, gain, bias, in_proj, in_bias, out_proj, out_bias, out, *scratch
):
    refs = (gain, bias, in_proj, in_bias, out_proj, out_bias)

    @pl.loop(0, 4)
    def _(step):
        late = (step >= 2).astype(jnp.int32)
        j = step + 3 * late
        start = pl.multiple_of((step + late) * WIN, WIN)
        far = lambda side: gather_rows((above, below)[side], 96, start)
        half_pair(keep, image, j, far, keep_above[1, j] == 1, refs, out, step, scratch)


def half_inner_kernel(
    keep, keep_above, image, above, below, above_rest, below_rest, gain, bias, in_proj, in_bias, out_proj, out_bias, out, *scratch
):
    refs = (gain, bias, in_proj, in_bias, out_proj, out_bias)
    rows = scratch[4]
    for side in range(2):
        early, late = (above, below)[side], (above_rest, below_rest)[side]
        for r in range(SHIFT):
            rows[side, 64 * r : 64 * r + 16] = early[96 * r + 32 : 96 * r + 48]
            rows[side, 64 * r + 16 : 64 * r + 48] = late[32 * r : 32 * r + 32]
            rows[side, 64 * r + 48 : 64 * r + 64] = early[96 * r + 48 : 96 * r + 64]

    @pl.loop(0, 3)
    def _(step):
        j = step + 2
        far = lambda side: gather_rows(rows.at[side], 64, column(step))
        half_pair(keep, image, j, far, keep_above[1, j] == 1, refs, out, step, scratch[:4])


def store(layer, rows, cols, values):
    for c in range(4):
        layer[c, rows, cols, :] = values[:, :, 128 * c : 128 * c + 128]


def lay_out(layer, inner, outer_halves, inner_halves):
    @pl.loop(0, 7)
    def _(j):
        cols = pl.ds(pl.multiple_of(j * WIN + SHIFT, SHIFT), WIN)
        store(layer, slice(SHIFT, SHIFT + WIN), cols, inner[j].astype(F32).reshape(WIN, WIN, D))

    for ref, columns in ((outer_halves, (0, 1, 5, 6)), (inner_halves, (2, 3, 4))):
        for step, j in enumerate(columns):
            cols = slice(j * WIN + SHIFT, j * WIN + SHIFT + WIN)
            for side in range(2):
                rows = slice(3 * SHIFT * side, 3 * SHIFT * side + SHIFT)
                store(layer, rows, cols, ref[step, side].astype(F32).reshape(SHIFT, WIN, D))


def lay_out_edges(layer, edges):
    for side in range(2):
        col = slice(15 * SHIFT * side, 15 * SHIFT * side + SHIFT)
        values = edges[128 * side : 128 * side + 128].astype(F32)
        store(layer, slice(SHIFT, SHIFT + WIN), col, values.reshape(WIN, SHIFT, D))
        for down in range(2):
            row = slice(3 * SHIFT * down, 3 * SHIFT * down + SHIFT)
            first = 256 + 64 * (2 * down + side)
            store(layer, row, col, edges[first : first + 64].astype(F32).reshape(SHIFT, SHIFT, D))


def merge_order(route, first):
    wide = lax.axis_index("wide")
    moves = [(route[0, 4 * wide + j] == 2).astype(jnp.int32) for j in range(4)]
    total = moves[0] + moves[1] + moves[2] + moves[3]
    chosen = [0, 0]
    moved, stayed = 0, 0
    for j in range(4):
        position = jnp.where(moves[j] == 1, moved, total + stayed)
        for slot in range(2):
            chosen[slot] = jnp.where(position == first + slot, j, chosen[slot])
        moved = moved + moves[j]
        stayed = stayed + 1 - moves[j]
    return chosen


def merge_two(route, start, layer, gain, bias, weight, merged, results, sem, outs):
    chosen = merge_order(route, start)
    blocks = []
    for group in chosen:
        parts = []
        for odd_col in range(2):
            cols = pl.ds(group * 32 + odd_col, WIN, stride=2)
            for odd_row in range(2):
                for c in range(4):
                    parts.append(
                        jnp.concatenate([layer[c, 2 * r + odd_row, cols, :] for r in range(WIN)], axis=0)
                    )
        blocks.append(layer_norm(jnp.concatenate(parts, axis=1), gain[...], bias[...]))
    result = matmul(jnp.concatenate(blocks, axis=0), weight[...]).astype(BF16)
    copies = []
    for slot, group in enumerate(chosen):
        part = result[256 * slot : 256 * slot + 256]
        if outs is not None:
            outs[slot][...] = part
        results[slot] = part.reshape(WIN, WIN, E)
        copy = pltpu.make_async_copy(results.at[slot], merged.at[:, pl.ds(column(group), WIN), :], sem.at[slot])
        copy.start()
        copies.append(copy)
    for copy in copies:
        copy.wait()


def edge_kernel(
    keep,
    keep_above,
    route,
    own_left,
    own_right,
    far_left,
    far_right,
    inner,
    outer_halves,
    inner_halves,
    gain,
    bias,
    in_proj,
    in_bias,
    out_proj,
    out_bias,
    merge_gain,
    merge_bias,
    merge_weight,
    merged,
    first,
    second,
    edges,
    layer,
    results,
    q_ref,
    k_ref,
    v_ref,
    context,
    sem,
):
    narrow, rows = lax.axis_index("narrow"), lax.axis_size("narrow")
    wide, groups = lax.axis_index("wide"), lax.axis_size("wide")
    flags = far_left[24]

    def strip(ref, low, high):
        return ref[low // 2 : high // 2].astype(F32).reshape(-1, D)

    windows = []
    for side in range(2):
        near, far = (own_left, own_right)[side], (far_left, far_right)[side]
        edge_col = wide == (0, groups - 1)[side]
        own = strip(near, 16, 32)
        beside = jnp.where(edge_col, own, strip(far, 16, 32))
        kept = flag_at(flags, 1) if side == 0 else keep[0, 7] == 1
        windows.append((kept, own, [own, beside]))
    for down in range(2):
        for side in range(2):
            near, far = (own_left, own_right)[side], (far_left, far_right)[side]
            edge_col = wide == (0, groups - 1)[side]
            edge_row = narrow == (0, rows - 1)[down]
            mine, beyond = ((8, 0), (32, 40))[down]
            own = strip(near, mine, mine + SHIFT)
            across = jnp.where(edge_row, own, strip(near, beyond, beyond + SHIFT))
            beside = jnp.where(edge_col, own, strip(far, mine, mine + SHIFT))
            corner = strip(far, beyond, beyond + SHIFT)
            corner = jnp.where(edge_col, across, jnp.where(edge_row, beside, corner))
            if side == 0:
                kept = flag_at(flags, 2 * down)
            elif down == 0:
                kept = keep_above[1, 7] == 1
            else:
                kept = keep[1, 7] == 1
            windows.append((kept, own, [own, across, beside, corner]))
    normed = [[layer_norm(part, gain[...], bias[...]) for part in parts] for _, _, parts in windows]
    queries = jnp.concatenate([parts[0] for parts in normed], axis=0)
    normed = jnp.concatenate([part for parts in normed for part in parts], axis=0)
    project(normed, queries, in_proj, in_bias, q_ref, k_ref, v_ref)
    place = 0
    for window, (kept, own, _) in enumerate(windows):
        count = own.shape[0]

        @pl.when(kept)
        def _():
            attend_window(place, count, window, q_ref, k_ref, v_ref, context)

        place += count
    result = matmul(context[...], out_proj[...]) + out_bias[...]
    place = 0
    for kept, own, _ in windows:
        mine = slice(place, place + own.shape[0])
        edges[mine] = jnp.where(kept, own + result[mine], own).astype(BF16)
        place += own.shape[0]
    lay_out(layer, inner, outer_halves, inner_halves)
    lay_out_edges(layer, edges)
    merge_two(route, 0, layer, merge_gain, merge_bias, merge_weight, merged, results, sem, (first, second))


def rest_kernel(
    route, earlier, inner, outer_halves, inner_halves, edges, gain, bias, weight, merged, third, fourth, layer, results, sem
):
    lay_out(layer, inner, outer_halves, inner_halves)
    lay_out_edges(layer, edges)
    merge_two(route, 2, layer, gain, bias, weight, merged, results, sem, (third, fourth))


def top_kernel(slot, route, own, incoming, gain, bias, in_proj, in_bias, out_proj, out_bias, *rest):
    out, tokens_ref, result, sem = rest[-4:]
    wide, groups = lax.axis_index("wide"), lax.axis_size("wide")
    before = jnp.where(wide == 0, groups - 1, wide - 1)
    homes = 0
    arriving = 0
    chosen = 0
    for j in range(4):
        stays = route[0, 4 * wide + j] == 1
        chosen = jnp.where(stays & (homes == slot), j, chosen)
        homes = homes + stays.astype(jnp.int32)
        arriving = arriving + (route[0, 4 * before + j] == 2).astype(jnp.int32)
    order = merge_order(route, 0) + merge_order(route, 2)
    width = PACK * HEAD
    filled = slot < homes + arriving

    for position in range(4):

        @pl.when((slot < homes) & (order[position] == chosen))
        def _():
            tokens_ref[...] = own[position][...]

    for source in range(slot + 1):

        @pl.when(homes + source == slot)
        def _():
            tokens_ref[...] = incoming[source][...]

    @pl.when(filled)
    def _():
        tokens = tokens_ref[...].astype(F32)
        normed = layer_norm(tokens, gain[...], bias[...])
        context = []
        for c in range(0, E, 2 * width):
            cols = slice(c, c + 2 * width)
            q = ((matmul(normed, in_proj[:, cols]) + in_bias[cols][None]) * QSCALE).astype(BF16)
            cols = slice(E + c, E + c + 2 * width)
            k = (matmul(normed, in_proj[:, cols]) + in_bias[cols][None]).astype(BF16)
            cols = slice(2 * E + c, 2 * E + c + 2 * width)
            v = (matmul(normed, in_proj[:, cols]) + in_bias[cols][None]).astype(BF16)
            for a in (0, width):
                context.append(attend(q[:, a : a + width], k[:, a : a + width], v[:, a : a + width]))
        value = matmul(jnp.concatenate(context, axis=1), out_proj[...]) + out_bias[...] + tokens
        result[...] = value.astype(BF16)

    @pl.when(jnp.logical_not(filled))
    def _():
        result[...] = jnp.zeros((WIN * WIN, E), BF16)

    copy = pltpu.make_async_copy(result, out.at[0, slot], sem)
    copy.start()
    copy.wait()


def top_first(route, first, second, third, fourth, one, *rest):
    top_kernel(0, route, (first, second, third, fourth), (one,), *rest)


def top_second(route, first, second, third, fourth, one, two, *rest):
    top_kernel(1, route, (first, second, third, fourth), (one, two), *rest)


def in_smem():
    return pl.BlockSpec(memory_space=pltpu.SMEM)


def in_vmem():
    return pl.BlockSpec(memory_space=pltpu.VMEM)


def in_hbm():
    return pl.BlockSpec(memory_space=pltpu.HBM)


def shifted(block, axis, distance):
    count = lax.axis_size(axis)
    return lax.ppermute(block, axis, [((i - distance) % count, i) for i in range(count)])


def shape(*sizes):
    return jax.ShapeDtypeStruct(sizes, BF16)


def params(mib):
    return pltpu.CompilerParams(vmem_limit_bytes=mib * 2**20)


def cost(us):
    return pl.CostEstimate(flops=us * 10**9, bytes_accessed=4_000_000, transcendentals=0)


def shards(
    image,
    third_norm_gain,
    third_norm_bias,
    third_in_proj,
    third_in_bias,
    third_out_proj,
    third_out_bias,
    window_keep,
    merge_gain,
    merge_bias,
    merge_weight,
    fourth_norm_gain,
    fourth_norm_bias,
    fourth_in_proj,
    fourth_in_bias,
    fourth_out_proj,
    fourth_out_bias,
    window_route,
):
    low, high = 3 * WIN, 5 * WIN

    def row_parts(rows):
        early = jnp.concatenate([rows[:, :low], rows[:, high:]], axis=1)
        return early.reshape(-1, D), rows[:, low:high].reshape(-1, D)

    send_down, send_down_rest = row_parts(image[3 * SHIFT :])
    send_up, send_up_rest = row_parts(image[:SHIFT])
    send_down, send_up, flags = lax.optimization_barrier((send_down, send_up, window_keep))
    keep_above = shifted(flags, "narrow", 1)
    above = shifted(send_down, "narrow", 1)
    below = shifted(send_up, "narrow", -1)
    third = (
        third_norm_gain[None],
        third_norm_bias[None],
        third_in_proj,
        third_in_bias,
        third_out_proj,
        third_out_bias[None],
    )
    inner = pl.pallas_call(
        inner_kernel,
        out_shape=shape(7, WIN * WIN, D),
        in_specs=[in_smem()] + [in_vmem()] * 7,
        out_specs=in_vmem(),
        compiler_params=params(24),
        cost_estimate=cost(18),
        name="inner_windows",
    )(window_keep, image, *third)

    above, below, send_down_rest, send_up_rest = lax.optimization_barrier(
        (above, below, send_down_rest, send_up_rest)
    )
    own_left, own_right = pl.pallas_call(
        strip_kernel,
        out_shape=(shape(24, WIN, D), shape(25, WIN, D)),
        in_specs=[in_smem()] * 2 + [in_vmem()] * 3,
        out_specs=(in_vmem(),) * 2,
        compiler_params=params(12),
        cost_estimate=cost(1),
        name="pack_columns",
    )(window_keep, keep_above, image, above, below)
    above, below, own_left, own_right = lax.optimization_barrier((above, below, own_left, own_right))
    above_rest = shifted(send_down_rest, "narrow", 1)
    below_rest = shifted(send_up_rest, "narrow", -1)
    far_left = shifted(own_right, "wide", 1)
    far_right = shifted(own_left, "wide", -1)
    work = [
        pltpu.VMEM((256, D), BF16),
        pltpu.VMEM((512, D), BF16),
        pltpu.VMEM((512, D), BF16),
        pltpu.VMEM((256, D), BF16),
    ]
    outer_halves = pl.pallas_call(
        half_outer_kernel,
        out_shape=shape(4, 2, 128, D),
        in_specs=[in_smem()] * 2 + [in_vmem()] * 9,
        out_specs=in_vmem(),
        scratch_shapes=work,
        compiler_params=params(24),
        cost_estimate=cost(14),
        name="half_windows_outer",
    )(window_keep, keep_above, image, above, below, *third)
    inner_halves = pl.pallas_call(
        half_inner_kernel,
        out_shape=shape(3, 2, 128, D),
        in_specs=[in_smem()] * 2 + [in_vmem()] * 11,
        out_specs=in_vmem(),
        scratch_shapes=work + [pltpu.VMEM((2, 512, D), BF16)],
        compiler_params=params(24),
        cost_estimate=cost(10),
        name="half_windows_inner",
    )(window_keep, keep_above, image, above, below, above_rest, below_rest, *third)
    merging = (merge_gain[None], merge_bias[None], merge_weight)
    scratch = [
        pltpu.VMEM((4, 32, 128, 128), F32),
        pltpu.VMEM((2, WIN, WIN, E), BF16),
        pltpu.SemaphoreType.DMA((2,)),
    ]
    work = [
        pltpu.VMEM((512, D), BF16),
        pltpu.VMEM((1536, D), BF16),
        pltpu.VMEM((1536, D), BF16),
        pltpu.VMEM((512, D), BF16),
    ]
    attended = (inner, outer_halves, inner_halves)
    merged, first, second, edges = pl.pallas_call(
        edge_kernel,
        out_shape=(shape(16, 64, E), shape(WIN * WIN, E), shape(WIN * WIN, E), shape(512, D)),
        in_specs=[in_smem()] * 3 + [in_vmem()] * 16,
        out_specs=(in_hbm(),) + (in_vmem(),) * 3,
        scratch_shapes=scratch[:2] + work + scratch[2:],
        compiler_params=params(36),
        cost_estimate=cost(12),
        name="edge_windows",
    )(window_keep, keep_above, window_route, own_left, own_right, far_left, far_right, *attended, *third, *merging)
    incoming_first = shifted(first, "wide", 1)
    merged, third, fourth = pl.pallas_call(
        rest_kernel,
        out_shape=(shape(16, 64, E), shape(WIN * WIN, E), shape(WIN * WIN, E)),
        in_specs=[in_smem(), in_hbm()] + [in_vmem()] * 7,
        out_specs=(in_hbm(), in_vmem(), in_vmem()),
        scratch_shapes=scratch,
        input_output_aliases={1: 0},
        compiler_params=params(24),
        cost_estimate=cost(5),
        name="rest_merging",
    )(window_route, merged, *attended, edges, *merging)
    own = (first, second, third, fourth)
    behind, incoming_first = lax.optimization_barrier((second, incoming_first))
    incoming_second = shifted(behind, "wide", 1)
    top = (
        fourth_norm_gain[None],
        fourth_norm_bias[None],
        fourth_in_proj,
        fourth_in_bias,
        fourth_out_proj,
        fourth_out_bias[None],
    )
    scratch = [
        pltpu.VMEM((WIN * WIN, E), BF16),
        pltpu.VMEM((WIN * WIN, E), BF16),
        pltpu.SemaphoreType.DMA,
    ]
    slots = pl.pallas_call(
        top_first,
        out_shape=shape(1, 2, WIN * WIN, E),
        in_specs=[in_smem()] + [in_vmem()] * 11,
        out_specs=in_hbm(),
        scratch_shapes=scratch,
        compiler_params=params(24),
        cost_estimate=cost(8),
        name="top_first",
    )(window_route, *own, incoming_first, *top)
    slots = pl.pallas_call(
        top_second,
        out_shape=shape(1, 2, WIN * WIN, E),
        in_specs=[in_smem()] + [in_vmem()] * 12 + [in_hbm()],
        out_specs=in_hbm(),
        scratch_shapes=scratch,
        input_output_aliases={13: 0},
        compiler_params=params(24),
        cost_estimate=cost(8),
        name="top_second",
    )(window_route, *own, incoming_first, incoming_second, *top, slots)
    return merged, slots


def solution(mesh):
    placed = (
        P("narrow", "wide", None),
        P(),
        P(),
        P(),
        P(),
        P(),
        P(),
        P("narrow", "wide"),
        P(),
        P(),
        P(),
        P(),
        P(),
        P(),
        P(),
        P(),
        P(),
        P("narrow", None),
    )
    return jax.shard_map(
        shards,
        mesh=mesh,
        in_specs=placed,
        out_specs=(P("narrow", "wide", None), P("narrow", "wide", None, None)),
        check_vma=False,
    )
```

```python
import jax
import jax.numpy as jnp
from jax import lax
from jax.experimental import pallas as pl
from jax.experimental.pallas import tpu as pltpu
from jax.sharding import PartitionSpec as P

D = 512
HEADS_D = 16
E = 1024
HEADS_E = 32
WIN = 16
SHIFT = 8
HEAD = 32
PACK = 4
EPSILON = 1e-05
LOG2E = 1.4426950408889634
QSCALE = HEAD ** (-0.5) * LOG2E
BF16 = jnp.bfloat16
F32 = jnp.float32


def matmul(a, b):
    return jnp.dot(a, b, preferred_element_type=F32)


def layer_norm(values, gain, bias):
    center = jnp.mean(values, axis=-1, keepdims=True)
    offsets = values - center
    spread = jnp.mean(offsets * offsets, axis=-1, keepdims=True)
    return (offsets * lax.rsqrt(spread + EPSILON) * gain + bias).astype(BF16)


def attend(q, k, v):
    count = q.shape[0]
    lane = lax.broadcasted_iota(jnp.int32, (count, PACK * HEAD), 1)
    stacked = jnp.concatenate(
        [jnp.where((lane >= HEAD * h) & (lane < HEAD * h + HEAD), q, 0) for h in range(PACK)], axis=0
    )
    scores = lax.dot_general(stacked, k, (((1,), (1,)), ((), ())), preferred_element_type=F32)
    weights = jnp.exp2(scores - jnp.max(scores, axis=1, keepdims=True)).astype(BF16)
    sums = matmul(weights, jnp.concatenate([v, jnp.ones_like(v)], axis=1))
    total = sums[:count]
    lane = lax.broadcasted_iota(jnp.int32, total.shape, 1) % (PACK * HEAD)
    for h in range(1, PACK):
        total = jnp.where(lane >= HEAD * h, sums[count * h : count * (h + 1)], total)
    return (total[:, : PACK * HEAD] / total[:, PACK * HEAD :]).astype(BF16)


def attention_three(tokens, count, refs):
    gain, bias, in_proj, in_bias, out_proj, out_bias = refs
    normed = layer_norm(tokens, gain[...], bias[...])
    q = ((matmul(normed[:count], in_proj[:, :D]) + in_bias[:D][None]) * QSCALE).astype(BF16)
    k = (matmul(normed, in_proj[:, D : 2 * D]) + in_bias[D : 2 * D][None]).astype(BF16)
    v = (matmul(normed, in_proj[:, 2 * D :]) + in_bias[2 * D : 3 * D][None]).astype(BF16)
    width = PACK * HEAD
    context = jnp.concatenate(
        [attend(q[:, c : c + width], k[:, c : c + width], v[:, c : c + width]) for c in range(0, D, width)],
        axis=1,
    )
    return (matmul(context, out_proj[...]) + out_bias[...] + tokens[:count]).astype(BF16)


def column(j):
    return pl.multiple_of(j * WIN, WIN)


def merge_order(route, first):
    wide = lax.axis_index("wide")
    moves = [(route[0, 4 * wide + j] == 2).astype(jnp.int32) for j in range(4)]
    total = moves[0] + moves[1] + moves[2] + moves[3]
    chosen = [0, 0]
    moved, stayed = 0, 0
    for j in range(4):
        position = jnp.where(moves[j] == 1, moved, total + stayed)
        for slot in range(2):
            chosen[slot] = jnp.where(position == first + slot, j, chosen[slot])
        moved = moved + moves[j]
        stayed = stayed + 1 - moves[j]
    return chosen


def needed_first(route, j):
    first = merge_order(route, 0)
    return (j % 2 == 1) | (j == 2 * first[0]) | (j == 2 * first[1])


def strip_kernel(keep, keep_above, image, above, below, left, right):
    for side, out in enumerate((left, right)):
        base, start = (0, 7 * WIN)[side], SHIFT * side
        for pair in range(24):
            rows = []
            for r in (2 * pair, 2 * pair + 1):
                if r < SHIFT:
                    block = above[96 * r + (0, 80)[side] : 96 * r + (16, 96)[side]]
                elif r < 5 * SHIFT:
                    block = image[r - SHIFT, base : base + WIN]
                else:
                    q = r - 5 * SHIFT
                    block = below[96 * q + (0, 80)[side] : 96 * q + (16, 96)[side]]
                rows.append(block.astype(F32)[start : start + SHIFT])
            out[pair] = jnp.concatenate(rows, axis=0).astype(BF16)
    lanes = lax.broadcasted_iota(jnp.int32, (WIN, D), 1)
    flags = jnp.where(lanes == 0, keep_above[1, 7].astype(F32), 0.0)
    for a in range(2):
        flags = jnp.where(lanes == a + 1, keep[a, 7].astype(F32), flags)
    right[24] = flags.astype(BF16)


def inner_kernel(keep, image, gain, bias, in_proj, in_bias, out_proj, out_bias, out):
    refs = (gain, bias, in_proj, in_bias, out_proj, out_bias)

    @pl.loop(0, 7)
    def _(j):
        both = image[SHIFT : SHIFT + WIN, pl.ds(column(j), 2 * WIN), :].astype(F32)
        tokens = both[:, SHIFT : SHIFT + WIN, :].reshape(WIN * WIN, D)

        @pl.when(keep[0, j] == 1)
        def _():
            out[j] = attention_three(tokens, WIN * WIN, refs)

        @pl.when(keep[0, j] != 1)
        def _():
            out[j] = tokens.astype(BF16)


def flag_at(flags, lane):
    lanes = lax.broadcasted_iota(jnp.int32, (WIN, 128), 1)
    return jnp.max(jnp.where(lanes == lane, flags[:, :128].astype(F32), 0.0)) > 0.5


def project(normed, queries, in_proj, in_bias, q_ref, k_ref, v_ref):
    q = (matmul(queries, in_proj[:, :D]) + in_bias[:D][None]) * QSCALE
    q_ref[...] = q.astype(BF16)
    k_ref[...] = (matmul(normed, in_proj[:, D : 2 * D]) + in_bias[D : 2 * D][None]).astype(BF16)
    v_ref[...] = (matmul(normed, in_proj[:, 2 * D :]) + in_bias[2 * D : 3 * D][None]).astype(BF16)


def attend_window(first, count, window, q_ref, k_ref, v_ref, context):
    width = PACK * HEAD
    mine, keys = slice(first, first + count), slice(WIN * WIN * window, WIN * WIN * (window + 1))
    for c in range(0, D, width):
        cols = slice(c, c + width)
        context[mine, cols] = attend(q_ref[mine, cols], k_ref[keys, cols], v_ref[keys, cols])


def half_pair(keep, image, j, far, top_kept, refs, out, step, scratch):
    gain, bias, in_proj, in_bias, out_proj, out_bias = refs
    narrow, rows = lax.axis_index("narrow"), lax.axis_size("narrow")
    q_ref, k_ref, v_ref, context = scratch
    tokens = []
    for side in range(2):
        row = 3 * SHIFT * side
        own = image[row : row + SHIFT, pl.ds(column(j), 2 * WIN), :].astype(F32)
        own = own[:, SHIFT : SHIFT + WIN].reshape(-1, D)
        tokens.append((own, jnp.where(narrow == (0, rows - 1)[side], own, far(side))))
    kept = [top_kept, keep[1, j] == 1]

    @pl.when(kept[0] | kept[1])
    def _():
        normed = [[layer_norm(part, gain[...], bias[...]) for part in pair] for pair in tokens]
        queries = jnp.concatenate([normed[0][0], normed[1][0]], axis=0)
        project(jnp.concatenate(normed[0] + normed[1], axis=0), queries, in_proj, in_bias, q_ref, k_ref, v_ref)

    for side in range(2):

        @pl.when(kept[side])
        def _():
            attend_window(128 * side, 128, side, q_ref, k_ref, v_ref, context)

    @pl.when(kept[0] | kept[1])
    def _():
        result = matmul(context[...], out_proj[...]) + out_bias[...]
        for side in range(2):
            own = tokens[side][0]
            new = own + result[128 * side : 128 * side + 128]
            out[step, side] = jnp.where(kept[side], new, own).astype(BF16)

    @pl.when(jnp.logical_not(kept[0] | kept[1]))
    def _():
        for side in range(2):
            out[step, side] = tokens[side][0].astype(BF16)


def gather_rows(ref, pitch, start):
    rows = [ref[pl.ds(pitch * r + start, 2 * WIN), :].astype(F32)[SHIFT : SHIFT + WIN] for r in range(SHIFT)]
    return jnp.concatenate(rows, axis=0)


def half_outer_kernel(
    keep, keep_above, route, image, above, below, gain, bias, in_proj, in_bias, out_proj, out_bias, out, *scratch
):
    refs = (gain, bias, in_proj, in_bias, out_proj, out_bias)

    @pl.loop(0, 4)
    def _(step):
        late = (step >= 2).astype(jnp.int32)
        j = step + 3 * late
        start = pl.multiple_of((step + late) * WIN, WIN)
        far = lambda side: gather_rows((above, below)[side], 96, start)

        @pl.when(needed_first(route, j))
        def _():
            half_pair(keep, image, j, far, keep_above[1, j] == 1, refs, out, step, scratch)


def half_inner_kernel(
    keep, keep_above, route, image, above, below, above_rest, below_rest, gain, bias, in_proj, in_bias, out_proj, out_bias, out, *scratch
):
    refs = (gain, bias, in_proj, in_bias, out_proj, out_bias)
    rows = scratch[4]
    for side in range(2):
        early, late = (above, below)[side], (above_rest, below_rest)[side]
        for r in range(SHIFT):
            rows[side, 64 * r : 64 * r + 16] = early[96 * r + 32 : 96 * r + 48]
            rows[side, 64 * r + 16 : 64 * r + 48] = late[32 * r : 32 * r + 32]
            rows[side, 64 * r + 48 : 64 * r + 64] = early[96 * r + 48 : 96 * r + 64]

    @pl.loop(0, 3)
    def _(step):
        j = step + 2
        far = lambda side: gather_rows(rows.at[side], 64, column(step))

        @pl.when(needed_first(route, j))
        def _():
            half_pair(keep, image, j, far, keep_above[1, j] == 1, refs, out, step, scratch[:4])


def store(layer, rows, cols, values):
    for c in range(4):
        layer[c, rows, cols, :] = values[:, :, 128 * c : 128 * c + 128]


def lay_out(layer, inner, outer_halves, inner_halves):
    @pl.loop(0, 7)
    def _(j):
        cols = pl.ds(pl.multiple_of(j * WIN + SHIFT, SHIFT), WIN)
        store(layer, slice(SHIFT, SHIFT + WIN), cols, inner[j].astype(F32).reshape(WIN, WIN, D))

    for ref, columns in ((outer_halves, (0, 1, 5, 6)), (inner_halves, (2, 3, 4))):
        for step, j in enumerate(columns):
            cols = slice(j * WIN + SHIFT, j * WIN + SHIFT + WIN)
            for side in range(2):
                rows = slice(3 * SHIFT * side, 3 * SHIFT * side + SHIFT)
                store(layer, rows, cols, ref[step, side].astype(F32).reshape(SHIFT, WIN, D))


def lay_out_edges(layer, edges):
    for side in range(2):
        col = slice(15 * SHIFT * side, 15 * SHIFT * side + SHIFT)
        values = edges[128 * side : 128 * side + 128].astype(F32)
        store(layer, slice(SHIFT, SHIFT + WIN), col, values.reshape(WIN, SHIFT, D))
        for down in range(2):
            row = slice(3 * SHIFT * down, 3 * SHIFT * down + SHIFT)
            first = 256 + 64 * (2 * down + side)
            store(layer, row, col, edges[first : first + 64].astype(F32).reshape(SHIFT, SHIFT, D))


def merge_two(route, start, layer, gain, bias, weight, merged, results, sem, outs):
    chosen = merge_order(route, start)
    blocks = []
    for group in chosen:
        parts = []
        for odd_col in range(2):
            cols = pl.ds(group * 32 + odd_col, WIN, stride=2)
            for odd_row in range(2):
                for c in range(4):
                    parts.append(
                        jnp.concatenate([layer[c, 2 * r + odd_row, cols, :] for r in range(WIN)], axis=0)
                    )
        blocks.append(layer_norm(jnp.concatenate(parts, axis=1), gain[...], bias[...]))
    result = matmul(jnp.concatenate(blocks, axis=0), weight[...]).astype(BF16)
    copies = []
    for slot, group in enumerate(chosen):
        part = result[256 * slot : 256 * slot + 256]
        if outs is not None:
            outs[slot][...] = part
        results[slot] = part.reshape(WIN, WIN, E)
        copy = pltpu.make_async_copy(results.at[slot], merged.at[:, pl.ds(column(group), WIN), :], sem.at[slot])
        copy.start()
        copies.append(copy)
    for copy in copies:
        copy.wait()


def edge_kernel(
    keep,
    keep_above,
    route,
    own_left,
    own_right,
    far_left,
    far_right,
    inner,
    outer_halves,
    inner_halves,
    gain,
    bias,
    in_proj,
    in_bias,
    out_proj,
    out_bias,
    merge_gain,
    merge_bias,
    merge_weight,
    merged,
    first,
    second,
    edges,
    layer,
    results,
    q_ref,
    k_ref,
    v_ref,
    context,
    sem,
):
    narrow, rows = lax.axis_index("narrow"), lax.axis_size("narrow")
    wide, groups = lax.axis_index("wide"), lax.axis_size("wide")
    flags = far_left[24]

    def strip(ref, low, high):
        return ref[low // 2 : high // 2].astype(F32).reshape(-1, D)

    windows = []
    for side in range(2):
        near, far = (own_left, own_right)[side], (far_left, far_right)[side]
        edge_col = wide == (0, groups - 1)[side]
        own = strip(near, 16, 32)
        beside = jnp.where(edge_col, own, strip(far, 16, 32))
        kept = flag_at(flags, 1) if side == 0 else keep[0, 7] == 1
        windows.append((kept, own, [own, beside]))
    for down in range(2):
        for side in range(2):
            near, far = (own_left, own_right)[side], (far_left, far_right)[side]
            edge_col = wide == (0, groups - 1)[side]
            edge_row = narrow == (0, rows - 1)[down]
            mine, beyond = ((8, 0), (32, 40))[down]
            own = strip(near, mine, mine + SHIFT)
            across = jnp.where(edge_row, own, strip(near, beyond, beyond + SHIFT))
            beside = jnp.where(edge_col, own, strip(far, mine, mine + SHIFT))
            corner = strip(far, beyond, beyond + SHIFT)
            corner = jnp.where(edge_col, across, jnp.where(edge_row, beside, corner))
            if side == 0:
                kept = flag_at(flags, 2 * down)
            elif down == 0:
                kept = keep_above[1, 7] == 1
            else:
                kept = keep[1, 7] == 1
            windows.append((kept, own, [own, across, beside, corner]))
    normed = [[layer_norm(part, gain[...], bias[...]) for part in parts] for _, _, parts in windows]
    queries = jnp.concatenate([parts[0] for parts in normed], axis=0)
    normed = jnp.concatenate([part for parts in normed for part in parts], axis=0)
    project(normed, queries, in_proj, in_bias, q_ref, k_ref, v_ref)
    place = 0
    for window, (kept, own, _) in enumerate(windows):
        count = own.shape[0]

        @pl.when(kept)
        def _():
            attend_window(place, count, window, q_ref, k_ref, v_ref, context)

        place += count
    result = matmul(context[...], out_proj[...]) + out_bias[...]
    place = 0
    for kept, own, _ in windows:
        mine = slice(place, place + own.shape[0])
        edges[mine] = jnp.where(kept, own + result[mine], own).astype(BF16)
        place += own.shape[0]
    lay_out(layer, inner, outer_halves, inner_halves)
    lay_out_edges(layer, edges)
    merge_two(route, 0, layer, merge_gain, merge_bias, merge_weight, merged, results, sem, (first, second))


def rest_kernel(
    keep,
    keep_above,
    route,
    earlier,
    image,
    above,
    below,
    above_rest,
    below_rest,
    inner,
    outer_halves,
    inner_halves,
    edges,
    gain,
    bias,
    in_proj,
    in_bias,
    out_proj,
    out_bias,
    merge_gain,
    merge_bias,
    merge_weight,
    merged,
    third,
    fourth,
    layer,
    results,
    sem,
    q_ref,
    k_ref,
    v_ref,
    context,
    rows,
    out,
):
    refs = (gain, bias, in_proj, in_bias, out_proj, out_bias)
    for side in range(2):
        early, late = (above, below)[side], (above_rest, below_rest)[side]
        for r in range(SHIFT):
            rows[side, 128 * r : 128 * r + 48] = early[96 * r : 96 * r + 48]
            rows[side, 128 * r + 48 : 128 * r + 80] = late[32 * r : 32 * r + 32]
            rows[side, 128 * r + 80 : 128 * r + 128] = early[96 * r + 48 : 96 * r + 96]
    lay_out(layer, inner, outer_halves, inner_halves)
    lay_out_edges(layer, edges)
    left = merge_order(route, 2)

    @pl.loop(0, 2)
    def _(step):
        j = 2 * jnp.where(step == 0, left[0], left[1])
        far = lambda side: gather_rows(rows.at[side], 128, column(j))
        half_pair(
            keep, image, j, far, keep_above[1, j] == 1, refs, out, step, (q_ref, k_ref, v_ref, context)
        )
        cols = pl.ds(pl.multiple_of(j * WIN + SHIFT, SHIFT), WIN)
        for side in range(2):
            where = slice(3 * SHIFT * side, 3 * SHIFT * side + SHIFT)
            store(layer, where, cols, out[step, side].astype(F32).reshape(SHIFT, WIN, D))

    merge_two(route, 2, layer, merge_gain, merge_bias, merge_weight, merged, results, sem, (third, fourth))


def top_kernel(slot, route, own, incoming, gain, bias, in_proj, in_bias, out_proj, out_bias, *rest):
    out, tokens_ref, result, sem = rest[-4:]
    wide, groups = lax.axis_index("wide"), lax.axis_size("wide")
    before = jnp.where(wide == 0, groups - 1, wide - 1)
    homes = 0
    arriving = 0
    chosen = 0
    for j in range(4):
        stays = route[0, 4 * wide + j] == 1
        chosen = jnp.where(stays & (homes == slot), j, chosen)
        homes = homes + stays.astype(jnp.int32)
        arriving = arriving + (route[0, 4 * before + j] == 2).astype(jnp.int32)
    order = merge_order(route, 0) + merge_order(route, 2)
    width = PACK * HEAD
    filled = slot < homes + arriving

    for position in range(4):

        @pl.when((slot < homes) & (order[position] == chosen))
        def _():
            tokens_ref[...] = own[position][...]

    for source in range(slot + 1):

        @pl.when(homes + source == slot)
        def _():
            tokens_ref[...] = incoming[source][...]

    @pl.when(filled)
    def _():
        tokens = tokens_ref[...].astype(F32)
        normed = layer_norm(tokens, gain[...], bias[...])
        context = []
        for c in range(0, E, 2 * width):
            cols = slice(c, c + 2 * width)
            q = ((matmul(normed, in_proj[:, cols]) + in_bias[cols][None]) * QSCALE).astype(BF16)
            cols = slice(E + c, E + c + 2 * width)
            k = (matmul(normed, in_proj[:, cols]) + in_bias[cols][None]).astype(BF16)
            cols = slice(2 * E + c, 2 * E + c + 2 * width)
            v = (matmul(normed, in_proj[:, cols]) + in_bias[cols][None]).astype(BF16)
            for a in (0, width):
                context.append(attend(q[:, a : a + width], k[:, a : a + width], v[:, a : a + width]))
        value = matmul(jnp.concatenate(context, axis=1), out_proj[...]) + out_bias[...] + tokens
        result[...] = value.astype(BF16)

    @pl.when(jnp.logical_not(filled))
    def _():
        result[...] = jnp.zeros((WIN * WIN, E), BF16)

    copy = pltpu.make_async_copy(result, out.at[0, slot], sem)
    copy.start()
    copy.wait()


def top_first(route, first, second, third, fourth, one, *rest):
    top_kernel(0, route, (first, second, third, fourth), (one,), *rest)


def top_second(route, first, second, third, fourth, one, two, *rest):
    top_kernel(1, route, (first, second, third, fourth), (one, two), *rest)


def in_smem():
    return pl.BlockSpec(memory_space=pltpu.SMEM)


def in_vmem():
    return pl.BlockSpec(memory_space=pltpu.VMEM)


def in_hbm():
    return pl.BlockSpec(memory_space=pltpu.HBM)


def shifted(block, axis, distance):
    count = lax.axis_size(axis)
    return lax.ppermute(block, axis, [((i - distance) % count, i) for i in range(count)])


def shape(*sizes):
    return jax.ShapeDtypeStruct(sizes, BF16)


def params(mib):
    return pltpu.CompilerParams(vmem_limit_bytes=mib * 2**20)


def cost(us):
    return pl.CostEstimate(flops=us * 10**9, bytes_accessed=4_000_000, transcendentals=0)


def shards(
    image,
    third_norm_gain,
    third_norm_bias,
    third_in_proj,
    third_in_bias,
    third_out_proj,
    third_out_bias,
    window_keep,
    merge_gain,
    merge_bias,
    merge_weight,
    fourth_norm_gain,
    fourth_norm_bias,
    fourth_in_proj,
    fourth_in_bias,
    fourth_out_proj,
    fourth_out_bias,
    window_route,
):
    low, high = 3 * WIN, 5 * WIN

    def row_parts(rows):
        early = jnp.concatenate([rows[:, :low], rows[:, high:]], axis=1)
        return early.reshape(-1, D), rows[:, low:high].reshape(-1, D)

    keep_above = shifted(window_keep, "narrow", 1)
    send_down, send_down_rest = row_parts(image[3 * SHIFT :])
    send_up, send_up_rest = row_parts(image[:SHIFT])
    above = shifted(send_down, "narrow", 1)
    below = shifted(send_up, "narrow", -1)
    third = (
        third_norm_gain[None],
        third_norm_bias[None],
        third_in_proj,
        third_in_bias,
        third_out_proj,
        third_out_bias[None],
    )
    inner = pl.pallas_call(
        inner_kernel,
        out_shape=shape(7, WIN * WIN, D),
        in_specs=[in_smem()] + [in_vmem()] * 7,
        out_specs=in_vmem(),
        compiler_params=params(24),
        cost_estimate=cost(18),
        name="inner_windows",
    )(window_keep, image, *third)

    above, below, send_down_rest, send_up_rest = lax.optimization_barrier(
        (above, below, send_down_rest, send_up_rest)
    )
    own_left, own_right = pl.pallas_call(
        strip_kernel,
        out_shape=(shape(24, WIN, D), shape(25, WIN, D)),
        in_specs=[in_smem()] * 2 + [in_vmem()] * 3,
        out_specs=(in_vmem(),) * 2,
        compiler_params=params(12),
        cost_estimate=cost(1),
        name="pack_columns",
    )(window_keep, keep_above, image, above, below)
    above, below, own_left, own_right = lax.optimization_barrier((above, below, own_left, own_right))
    above_rest = shifted(send_down_rest, "narrow", 1)
    below_rest = shifted(send_up_rest, "narrow", -1)
    far_left = shifted(own_right, "wide", 1)
    far_right = shifted(own_left, "wide", -1)
    work = [
        pltpu.VMEM((256, D), BF16),
        pltpu.VMEM((512, D), BF16),
        pltpu.VMEM((512, D), BF16),
        pltpu.VMEM((256, D), BF16),
    ]
    outer_halves = pl.pallas_call(
        half_outer_kernel,
        out_shape=shape(4, 2, 128, D),
        in_specs=[in_smem()] * 3 + [in_vmem()] * 9,
        out_specs=in_vmem(),
        scratch_shapes=work,
        compiler_params=params(24),
        cost_estimate=cost(14),
        name="half_windows_outer",
    )(window_keep, keep_above, window_route, image, above, below, *third)
    inner_halves = pl.pallas_call(
        half_inner_kernel,
        out_shape=shape(3, 2, 128, D),
        in_specs=[in_smem()] * 3 + [in_vmem()] * 11,
        out_specs=in_vmem(),
        scratch_shapes=work + [pltpu.VMEM((2, 512, D), BF16)],
        compiler_params=params(24),
        cost_estimate=cost(10),
        name="half_windows_inner",
    )(window_keep, keep_above, window_route, image, above, below, above_rest, below_rest, *third)
    merging = (merge_gain[None], merge_bias[None], merge_weight)
    scratch = [
        pltpu.VMEM((4, 32, 128, 128), F32),
        pltpu.VMEM((2, WIN, WIN, E), BF16),
        pltpu.SemaphoreType.DMA((2,)),
    ]
    half_work = work
    work = [
        pltpu.VMEM((512, D), BF16),
        pltpu.VMEM((1536, D), BF16),
        pltpu.VMEM((1536, D), BF16),
        pltpu.VMEM((512, D), BF16),
    ]
    attended = (inner, outer_halves, inner_halves)
    merged, first, second, edges = pl.pallas_call(
        edge_kernel,
        out_shape=(shape(16, 64, E), shape(WIN * WIN, E), shape(WIN * WIN, E), shape(512, D)),
        in_specs=[in_smem()] * 3 + [in_vmem()] * 16,
        out_specs=(in_hbm(),) + (in_vmem(),) * 3,
        scratch_shapes=scratch[:2] + work + scratch[2:],
        compiler_params=params(36),
        cost_estimate=cost(12),
        name="edge_windows",
    )(window_keep, keep_above, window_route, own_left, own_right, far_left, far_right, *attended, *third, *merging)
    incoming_first = shifted(first, "wide", 1)
    incoming_second = shifted(second, "wide", 1)
    merged, left_first, left_second = pl.pallas_call(
        rest_kernel,
        out_shape=(shape(16, 64, E), shape(WIN * WIN, E), shape(WIN * WIN, E)),
        in_specs=[in_smem()] * 3 + [in_hbm()] + [in_vmem()] * 18,
        out_specs=(in_hbm(), in_vmem(), in_vmem()),
        scratch_shapes=scratch + half_work + [pltpu.VMEM((2, 1024, D), BF16), pltpu.VMEM((2, 2, 128, D), BF16)],
        input_output_aliases={3: 0},
        compiler_params=params(36),
        cost_estimate=cost(12),
        name="rest_merging",
    )(
        window_keep,
        keep_above,
        window_route,
        merged,
        image,
        above,
        below,
        above_rest,
        below_rest,
        *attended,
        edges,
        *third,
        *merging,
    )
    own = (first, second, left_first, left_second)
    top = (
        fourth_norm_gain[None],
        fourth_norm_bias[None],
        fourth_in_proj,
        fourth_in_bias,
        fourth_out_proj,
        fourth_out_bias[None],
    )
    scratch = [
        pltpu.VMEM((WIN * WIN, E), BF16),
        pltpu.VMEM((WIN * WIN, E), BF16),
        pltpu.SemaphoreType.DMA,
    ]
    slots = pl.pallas_call(
        top_first,
        out_shape=shape(1, 2, WIN * WIN, E),
        in_specs=[in_smem()] + [in_vmem()] * 11,
        out_specs=in_hbm(),
        scratch_shapes=scratch,
        compiler_params=params(24),
        cost_estimate=cost(8),
        name="top_first",
    )(window_route, *own, incoming_first, *top)
    slots = pl.pallas_call(
        top_second,
        out_shape=shape(1, 2, WIN * WIN, E),
        in_specs=[in_smem()] + [in_vmem()] * 12 + [in_hbm()],
        out_specs=in_hbm(),
        scratch_shapes=scratch,
        input_output_aliases={13: 0},
        compiler_params=params(24),
        cost_estimate=cost(8),
        name="top_second",
    )(window_route, *own, incoming_first, incoming_second, *top, slots)
    return merged, slots


def solution(mesh):
    placed = (
        P("narrow", "wide", None),
        P(),
        P(),
        P(),
        P(),
        P(),
        P(),
        P("narrow", "wide"),
        P(),
        P(),
        P(),
        P(),
        P(),
        P(),
        P(),
        P(),
        P(),
        P("narrow", None),
    )
    return jax.shard_map(
        shards,
        mesh=mesh,
        in_specs=placed,
        out_specs=(P("narrow", "wide", None), P("narrow", "wide", None, None)),
        check_vma=False,
    )
```

```python
import jax
import jax.numpy as jnp
from jax import lax
from jax.experimental import pallas as pl
from jax.experimental.pallas import tpu as pltpu
from jax.sharding import PartitionSpec as P

D = 512
HEADS_D = 16
E = 1024
HEADS_E = 32
WIN = 16
SHIFT = 8
HEAD = 32
PACK = 4
EPSILON = 1e-05
LOG2E = 1.4426950408889634
QSCALE = HEAD ** (-0.5) * LOG2E
BF16 = jnp.bfloat16
F32 = jnp.float32


def matmul(a, b):
    return jnp.dot(a, b, preferred_element_type=F32)


def layer_norm(values, gain, bias):
    center = jnp.mean(values, axis=-1, keepdims=True)
    offsets = values - center
    spread = jnp.mean(offsets * offsets, axis=-1, keepdims=True)
    return (offsets * lax.rsqrt(spread + EPSILON) * gain + bias).astype(BF16)


def attend(q, k, v):
    count = q.shape[0]
    lane = lax.broadcasted_iota(jnp.int32, (count, PACK * HEAD), 1)
    stacked = jnp.concatenate(
        [jnp.where((lane >= HEAD * h) & (lane < HEAD * h + HEAD), q, 0) for h in range(PACK)], axis=0
    )
    scores = lax.dot_general(stacked, k, (((1,), (1,)), ((), ())), preferred_element_type=F32)
    weights = jnp.exp2(scores - jnp.max(scores, axis=1, keepdims=True)).astype(BF16)
    sums = matmul(weights, jnp.concatenate([v, jnp.ones_like(v)], axis=1))
    total = sums[:count]
    lane = lax.broadcasted_iota(jnp.int32, total.shape, 1) % (PACK * HEAD)
    for h in range(1, PACK):
        total = jnp.where(lane >= HEAD * h, sums[count * h : count * (h + 1)], total)
    return (total[:, : PACK * HEAD] / total[:, PACK * HEAD :]).astype(BF16)


def attention_three(tokens, count, refs):
    gain, bias, in_proj, in_bias, out_proj, out_bias = refs
    normed = layer_norm(tokens, gain[...], bias[...])
    q = ((matmul(normed[:count], in_proj[:, :D]) + in_bias[:D][None]) * QSCALE).astype(BF16)
    k = (matmul(normed, in_proj[:, D : 2 * D]) + in_bias[D : 2 * D][None]).astype(BF16)
    v = (matmul(normed, in_proj[:, 2 * D :]) + in_bias[2 * D : 3 * D][None]).astype(BF16)
    width = PACK * HEAD
    context = jnp.concatenate(
        [attend(q[:, c : c + width], k[:, c : c + width], v[:, c : c + width]) for c in range(0, D, width)],
        axis=1,
    )
    return (matmul(context, out_proj[...]) + out_bias[...] + tokens[:count]).astype(BF16)


def column(j):
    return pl.multiple_of(j * WIN, WIN)


def merge_order(route, first):
    wide = lax.axis_index("wide")
    moves = [(route[0, 4 * wide + j] == 2).astype(jnp.int32) for j in range(4)]
    total = moves[0] + moves[1] + moves[2] + moves[3]
    chosen = [0, 0]
    moved, stayed = 0, 0
    for j in range(4):
        position = jnp.where(moves[j] == 1, moved, total + stayed)
        for slot in range(2):
            chosen[slot] = jnp.where(position == first + slot, j, chosen[slot])
        moved = moved + moves[j]
        stayed = stayed + 1 - moves[j]
    return chosen


def needed_first(route, j):
    first = merge_order(route, 0)
    return (j % 2 == 1) | (j == 2 * first[0]) | (j == 2 * first[1])


def strip_kernel(keep, keep_above, image, above, below, left, right):
    for side, out in enumerate((left, right)):
        base, start = (0, 7 * WIN)[side], SHIFT * side
        for pair in range(24):
            rows = []
            for r in (2 * pair, 2 * pair + 1):
                if r < SHIFT:
                    block = above[96 * r + (0, 80)[side] : 96 * r + (16, 96)[side]]
                elif r < 5 * SHIFT:
                    block = image[r - SHIFT, base : base + WIN]
                else:
                    q = r - 5 * SHIFT
                    block = below[96 * q + (0, 80)[side] : 96 * q + (16, 96)[side]]
                rows.append(block.astype(F32)[start : start + SHIFT])
            out[pair] = jnp.concatenate(rows, axis=0).astype(BF16)
    lanes = lax.broadcasted_iota(jnp.int32, (WIN, D), 1)
    flags = jnp.where(lanes == 0, keep_above[1, 7].astype(F32), 0.0)
    for a in range(2):
        flags = jnp.where(lanes == a + 1, keep[a, 7].astype(F32), flags)
    right[24] = flags.astype(BF16)


def inner_kernel(keep, image, gain, bias, in_proj, in_bias, out_proj, out_bias, out):
    refs = (gain, bias, in_proj, in_bias, out_proj, out_bias)

    @pl.loop(0, 7)
    def _(j):
        both = image[SHIFT : SHIFT + WIN, pl.ds(column(j), 2 * WIN), :].astype(F32)
        tokens = both[:, SHIFT : SHIFT + WIN, :].reshape(WIN * WIN, D)

        @pl.when(keep[0, j] == 1)
        def _():
            out[j] = attention_three(tokens, WIN * WIN, refs)

        @pl.when(keep[0, j] != 1)
        def _():
            out[j] = tokens.astype(BF16)


def flag_at(flags, lane):
    lanes = lax.broadcasted_iota(jnp.int32, (WIN, 128), 1)
    return jnp.max(jnp.where(lanes == lane, flags[:, :128].astype(F32), 0.0)) > 0.5


def project(normed, queries, in_proj, in_bias, q_ref, k_ref, v_ref):
    q = (matmul(queries, in_proj[:, :D]) + in_bias[:D][None]) * QSCALE
    q_ref[...] = q.astype(BF16)
    k_ref[...] = (matmul(normed, in_proj[:, D : 2 * D]) + in_bias[D : 2 * D][None]).astype(BF16)
    v_ref[...] = (matmul(normed, in_proj[:, 2 * D :]) + in_bias[2 * D : 3 * D][None]).astype(BF16)


def attend_window(first, count, window, q_ref, k_ref, v_ref, context):
    width = PACK * HEAD
    mine, keys = slice(first, first + count), slice(WIN * WIN * window, WIN * WIN * (window + 1))
    for c in range(0, D, width):
        cols = slice(c, c + width)
        context[mine, cols] = attend(q_ref[mine, cols], k_ref[keys, cols], v_ref[keys, cols])


def half_pair(keep, image, j, far, top_kept, refs, out, step, scratch):
    gain, bias, in_proj, in_bias, out_proj, out_bias = refs
    narrow, rows = lax.axis_index("narrow"), lax.axis_size("narrow")
    q_ref, k_ref, v_ref, context = scratch
    tokens = []
    for side in range(2):
        row = 3 * SHIFT * side
        own = image[row : row + SHIFT, pl.ds(column(j), 2 * WIN), :].astype(F32)
        own = own[:, SHIFT : SHIFT + WIN].reshape(-1, D)
        tokens.append((own, jnp.where(narrow == (0, rows - 1)[side], own, far(side))))
    kept = [top_kept, keep[1, j] == 1]

    @pl.when(kept[0] | kept[1])
    def _():
        normed = [[layer_norm(part, gain[...], bias[...]) for part in pair] for pair in tokens]
        queries = jnp.concatenate([normed[0][0], normed[1][0]], axis=0)
        project(jnp.concatenate(normed[0] + normed[1], axis=0), queries, in_proj, in_bias, q_ref, k_ref, v_ref)

    for side in range(2):

        @pl.when(kept[side])
        def _():
            attend_window(128 * side, 128, side, q_ref, k_ref, v_ref, context)

    @pl.when(kept[0] | kept[1])
    def _():
        result = matmul(context[...], out_proj[...]) + out_bias[...]
        for side in range(2):
            own = tokens[side][0]
            new = own + result[128 * side : 128 * side + 128]
            out[step, side] = jnp.where(kept[side], new, own).astype(BF16)

    @pl.when(jnp.logical_not(kept[0] | kept[1]))
    def _():
        for side in range(2):
            out[step, side] = tokens[side][0].astype(BF16)


def gather_rows(ref, pitch, start):
    rows = [ref[pl.ds(pitch * r + start, 2 * WIN), :].astype(F32)[SHIFT : SHIFT + WIN] for r in range(SHIFT)]
    return jnp.concatenate(rows, axis=0)


def half_outer_kernel(
    keep, keep_above, route, image, above, below, gain, bias, in_proj, in_bias, out_proj, out_bias, out, *scratch
):
    refs = (gain, bias, in_proj, in_bias, out_proj, out_bias)

    @pl.loop(0, 4)
    def _(step):
        late = (step >= 2).astype(jnp.int32)
        j = step + 3 * late
        start = pl.multiple_of((step + late) * WIN, WIN)
        far = lambda side: gather_rows((above, below)[side], 96, start)

        @pl.when(needed_first(route, j))
        def _():
            half_pair(keep, image, j, far, keep_above[1, j] == 1, refs, out, step, scratch)


def half_inner_kernel(
    keep, keep_above, route, image, above, below, above_rest, below_rest, gain, bias, in_proj, in_bias, out_proj, out_bias, out, *scratch
):
    refs = (gain, bias, in_proj, in_bias, out_proj, out_bias)
    rows = scratch[4]
    for side in range(2):
        early, late = (above, below)[side], (above_rest, below_rest)[side]
        for r in range(SHIFT):
            rows[side, 64 * r : 64 * r + 16] = early[96 * r + 32 : 96 * r + 48]
            rows[side, 64 * r + 16 : 64 * r + 48] = late[32 * r : 32 * r + 32]
            rows[side, 64 * r + 48 : 64 * r + 64] = early[96 * r + 48 : 96 * r + 64]

    @pl.loop(0, 3)
    def _(step):
        j = step + 2
        far = lambda side: gather_rows(rows.at[side], 64, column(step))

        @pl.when(needed_first(route, j))
        def _():
            half_pair(keep, image, j, far, keep_above[1, j] == 1, refs, out, step, scratch[:4])


def store(layer, rows, cols, values):
    for c in range(4):
        layer[c, rows, cols, :] = values[:, :, 128 * c : 128 * c + 128]


def lay_out(layer, inner, outer_halves, inner_halves):
    @pl.loop(0, 7)
    def _(j):
        cols = pl.ds(pl.multiple_of(j * WIN + SHIFT, SHIFT), WIN)
        store(layer, slice(SHIFT, SHIFT + WIN), cols, inner[j].astype(F32).reshape(WIN, WIN, D))

    for ref, columns in ((outer_halves, (0, 1, 5, 6)), (inner_halves, (2, 3, 4))):
        for step, j in enumerate(columns):
            cols = slice(j * WIN + SHIFT, j * WIN + SHIFT + WIN)
            for side in range(2):
                rows = slice(3 * SHIFT * side, 3 * SHIFT * side + SHIFT)
                store(layer, rows, cols, ref[step, side].astype(F32).reshape(SHIFT, WIN, D))


def lay_out_edges(layer, edges):
    for side in range(2):
        col = slice(15 * SHIFT * side, 15 * SHIFT * side + SHIFT)
        values = edges[128 * side : 128 * side + 128].astype(F32)
        store(layer, slice(SHIFT, SHIFT + WIN), col, values.reshape(WIN, SHIFT, D))
        for down in range(2):
            row = slice(3 * SHIFT * down, 3 * SHIFT * down + SHIFT)
            first = 256 + 64 * (2 * down + side)
            store(layer, row, col, edges[first : first + 64].astype(F32).reshape(SHIFT, SHIFT, D))


def merge_two(route, start, layer, gain, bias, weight, merged, results, sem, outs):
    chosen = merge_order(route, start)
    blocks = []
    for group in chosen:
        parts = []
        for odd_col in range(2):
            cols = pl.ds(group * 32 + odd_col, WIN, stride=2)
            for odd_row in range(2):
                for c in range(4):
                    parts.append(
                        jnp.concatenate([layer[c, 2 * r + odd_row, cols, :] for r in range(WIN)], axis=0)
                    )
        blocks.append(layer_norm(jnp.concatenate(parts, axis=1), gain[...], bias[...]))
    result = matmul(jnp.concatenate(blocks, axis=0), weight[...]).astype(BF16)
    copies = []
    for slot, group in enumerate(chosen):
        part = result[256 * slot : 256 * slot + 256]
        if outs is not None:
            outs[slot][...] = part
        results[slot] = part.reshape(WIN, WIN, E)
        copy = pltpu.make_async_copy(results.at[slot], merged.at[:, pl.ds(column(group), WIN), :], sem.at[slot])
        copy.start()
        copies.append(copy)
    for copy in copies:
        copy.wait()


def edge_kernel(
    keep,
    keep_above,
    route,
    own_left,
    own_right,
    far_left,
    far_right,
    inner,
    outer_halves,
    inner_halves,
    gain,
    bias,
    in_proj,
    in_bias,
    out_proj,
    out_bias,
    merge_gain,
    merge_bias,
    merge_weight,
    merged,
    first,
    second,
    edges,
    layer,
    results,
    q_ref,
    k_ref,
    v_ref,
    context,
    sem,
):
    narrow, rows = lax.axis_index("narrow"), lax.axis_size("narrow")
    wide, groups = lax.axis_index("wide"), lax.axis_size("wide")
    flags = far_left[24]

    def strip(ref, low, high):
        return ref[low // 2 : high // 2].astype(F32).reshape(-1, D)

    windows = []
    for side in range(2):
        near, far = (own_left, own_right)[side], (far_left, far_right)[side]
        edge_col = wide == (0, groups - 1)[side]
        own = strip(near, 16, 32)
        beside = jnp.where(edge_col, own, strip(far, 16, 32))
        kept = flag_at(flags, 1) if side == 0 else keep[0, 7] == 1
        windows.append((kept, own, [own, beside]))
    for down in range(2):
        for side in range(2):
            near, far = (own_left, own_right)[side], (far_left, far_right)[side]
            edge_col = wide == (0, groups - 1)[side]
            edge_row = narrow == (0, rows - 1)[down]
            mine, beyond = ((8, 0), (32, 40))[down]
            own = strip(near, mine, mine + SHIFT)
            across = jnp.where(edge_row, own, strip(near, beyond, beyond + SHIFT))
            beside = jnp.where(edge_col, own, strip(far, mine, mine + SHIFT))
            corner = strip(far, beyond, beyond + SHIFT)
            corner = jnp.where(edge_col, across, jnp.where(edge_row, beside, corner))
            if side == 0:
                kept = flag_at(flags, 2 * down)
            elif down == 0:
                kept = keep_above[1, 7] == 1
            else:
                kept = keep[1, 7] == 1
            windows.append((kept, own, [own, across, beside, corner]))
    normed = [[layer_norm(part, gain[...], bias[...]) for part in parts] for _, _, parts in windows]
    queries = jnp.concatenate([parts[0] for parts in normed], axis=0)
    normed = jnp.concatenate([part for parts in normed for part in parts], axis=0)
    project(normed, queries, in_proj, in_bias, q_ref, k_ref, v_ref)
    place = 0
    for window, (kept, own, _) in enumerate(windows):
        count = own.shape[0]

        @pl.when(kept)
        def _():
            attend_window(place, count, window, q_ref, k_ref, v_ref, context)

        place += count
    result = matmul(context[...], out_proj[...]) + out_bias[...]
    place = 0
    for kept, own, _ in windows:
        mine = slice(place, place + own.shape[0])
        edges[mine] = jnp.where(kept, own + result[mine], own).astype(BF16)
        place += own.shape[0]
    lay_out(layer, inner, outer_halves, inner_halves)
    lay_out_edges(layer, edges)
    merge_two(route, 0, layer, merge_gain, merge_bias, merge_weight, merged, results, sem, (first, second))


def rest_kernel(
    keep,
    keep_above,
    route,
    earlier,
    image,
    above,
    below,
    above_rest,
    below_rest,
    inner,
    outer_halves,
    inner_halves,
    edges,
    gain,
    bias,
    in_proj,
    in_bias,
    out_proj,
    out_bias,
    merge_gain,
    merge_bias,
    merge_weight,
    merged,
    third,
    fourth,
    layer,
    results,
    sem,
    q_ref,
    k_ref,
    v_ref,
    context,
    rows,
    out,
):
    refs = (gain, bias, in_proj, in_bias, out_proj, out_bias)
    for side in range(2):
        early, late = (above, below)[side], (above_rest, below_rest)[side]
        for r in range(SHIFT):
            rows[side, 128 * r : 128 * r + 48] = early[96 * r : 96 * r + 48]
            rows[side, 128 * r + 48 : 128 * r + 80] = late[32 * r : 32 * r + 32]
            rows[side, 128 * r + 80 : 128 * r + 128] = early[96 * r + 48 : 96 * r + 96]
    lay_out(layer, inner, outer_halves, inner_halves)
    lay_out_edges(layer, edges)
    left = merge_order(route, 2)

    @pl.loop(0, 2)
    def _(step):
        j = 2 * jnp.where(step == 0, left[0], left[1])
        far = lambda side: gather_rows(rows.at[side], 128, column(j))
        half_pair(
            keep, image, j, far, keep_above[1, j] == 1, refs, out, step, (q_ref, k_ref, v_ref, context)
        )
        cols = pl.ds(pl.multiple_of(j * WIN + SHIFT, SHIFT), WIN)
        for side in range(2):
            where = slice(3 * SHIFT * side, 3 * SHIFT * side + SHIFT)
            store(layer, where, cols, out[step, side].astype(F32).reshape(SHIFT, WIN, D))

    merge_two(route, 2, layer, merge_gain, merge_bias, merge_weight, merged, results, sem, (third, fourth))


def top_kernel(slot, route, own, incoming, gain, bias, in_proj, in_bias, out_proj, out_bias, *rest):
    out, tokens_ref, result, sem = rest[-4:]
    wide, groups = lax.axis_index("wide"), lax.axis_size("wide")
    before = jnp.where(wide == 0, groups - 1, wide - 1)
    homes = 0
    arriving = 0
    chosen = 0
    for j in range(4):
        stays = route[0, 4 * wide + j] == 1
        chosen = jnp.where(stays & (homes == slot), j, chosen)
        homes = homes + stays.astype(jnp.int32)
        arriving = arriving + (route[0, 4 * before + j] == 2).astype(jnp.int32)
    order = merge_order(route, 0) + merge_order(route, 2)
    width = PACK * HEAD
    filled = slot < homes + arriving

    for position in range(4):

        @pl.when((slot < homes) & (order[position] == chosen))
        def _():
            tokens_ref[...] = own[position][...]

    for source in range(slot + 1):

        @pl.when(homes + source == slot)
        def _():
            tokens_ref[...] = incoming[source][...]

    @pl.when(filled)
    def _():
        tokens = tokens_ref[...].astype(F32)
        normed = layer_norm(tokens, gain[...], bias[...])
        context = []
        for c in range(0, E, 2 * width):
            cols = slice(c, c + 2 * width)
            q = ((matmul(normed, in_proj[:, cols]) + in_bias[cols][None]) * QSCALE).astype(BF16)
            cols = slice(E + c, E + c + 2 * width)
            k = (matmul(normed, in_proj[:, cols]) + in_bias[cols][None]).astype(BF16)
            cols = slice(2 * E + c, 2 * E + c + 2 * width)
            v = (matmul(normed, in_proj[:, cols]) + in_bias[cols][None]).astype(BF16)
            for a in (0, width):
                context.append(attend(q[:, a : a + width], k[:, a : a + width], v[:, a : a + width]))
        value = matmul(jnp.concatenate(context, axis=1), out_proj[...]) + out_bias[...] + tokens
        result[...] = value.astype(BF16)

    @pl.when(jnp.logical_not(filled))
    def _():
        result[...] = jnp.zeros((WIN * WIN, E), BF16)

    copy = pltpu.make_async_copy(result, out.at[0, slot], sem)
    copy.start()
    copy.wait()


def top_first(route, first, second, third, fourth, one, *rest):
    top_kernel(0, route, (first, second, third, fourth), (one,), *rest)


def top_second(route, first, second, third, fourth, one, two, *rest):
    top_kernel(1, route, (first, second, third, fourth), (one, two), *rest)


def in_smem():
    return pl.BlockSpec(memory_space=pltpu.SMEM)


def in_vmem():
    return pl.BlockSpec(memory_space=pltpu.VMEM)


def in_hbm():
    return pl.BlockSpec(memory_space=pltpu.HBM)


def shifted(block, axis, distance):
    count = lax.axis_size(axis)
    return lax.ppermute(block, axis, [((i - distance) % count, i) for i in range(count)])


def shape(*sizes):
    return jax.ShapeDtypeStruct(sizes, BF16)


def params(mib):
    return pltpu.CompilerParams(vmem_limit_bytes=mib * 2**20)


def cost(us):
    return pl.CostEstimate(flops=us * 10**9, bytes_accessed=4_000_000, transcendentals=0)


def shards(
    image,
    third_norm_gain,
    third_norm_bias,
    third_in_proj,
    third_in_bias,
    third_out_proj,
    third_out_bias,
    window_keep,
    merge_gain,
    merge_bias,
    merge_weight,
    fourth_norm_gain,
    fourth_norm_bias,
    fourth_in_proj,
    fourth_in_bias,
    fourth_out_proj,
    fourth_out_bias,
    window_route,
):
    low, high = 3 * WIN, 5 * WIN

    def row_parts(rows):
        early = jnp.concatenate([rows[:, :low], rows[:, high:]], axis=1)
        return early.reshape(-1, D), rows[:, low:high].reshape(-1, D)

    keep_above = shifted(window_keep, "narrow", 1)
    send_down, send_down_rest = row_parts(image[3 * SHIFT :])
    send_up, send_up_rest = row_parts(image[:SHIFT])
    above = shifted(send_down, "narrow", 1)
    below = shifted(send_up, "narrow", -1)
    third = (
        third_norm_gain[None],
        third_norm_bias[None],
        third_in_proj,
        third_in_bias,
        third_out_proj,
        third_out_bias[None],
    )
    inner = pl.pallas_call(
        inner_kernel,
        out_shape=shape(7, WIN * WIN, D),
        in_specs=[in_smem()] + [in_vmem()] * 7,
        out_specs=in_vmem(),
        compiler_params=params(24),
        cost_estimate=cost(18),
        name="inner_windows",
    )(window_keep, image, *third)

    above, below, send_down_rest, send_up_rest = lax.optimization_barrier(
        (above, below, send_down_rest, send_up_rest)
    )
    own_left, own_right = pl.pallas_call(
        strip_kernel,
        out_shape=(shape(24, WIN, D), shape(25, WIN, D)),
        in_specs=[in_smem()] * 2 + [in_vmem()] * 3,
        out_specs=(in_vmem(),) * 2,
        compiler_params=params(12),
        cost_estimate=cost(1),
        name="pack_columns",
    )(window_keep, keep_above, image, above, below)
    above, below, own_left, own_right = lax.optimization_barrier((above, below, own_left, own_right))
    above_rest = shifted(send_down_rest, "narrow", 1)
    below_rest = shifted(send_up_rest, "narrow", -1)
    far_left = shifted(own_right, "wide", 1)
    far_right = shifted(own_left, "wide", -1)
    work = [
        pltpu.VMEM((256, D), BF16),
        pltpu.VMEM((512, D), BF16),
        pltpu.VMEM((512, D), BF16),
        pltpu.VMEM((256, D), BF16),
    ]
    outer_halves = pl.pallas_call(
        half_outer_kernel,
        out_shape=shape(4, 2, 128, D),
        in_specs=[in_smem()] * 3 + [in_vmem()] * 9,
        out_specs=in_vmem(),
        scratch_shapes=work,
        compiler_params=params(24),
        cost_estimate=cost(14),
        name="half_windows_outer",
    )(window_keep, keep_above, window_route, image, above, below, *third)
    inner_halves = pl.pallas_call(
        half_inner_kernel,
        out_shape=shape(3, 2, 128, D),
        in_specs=[in_smem()] * 3 + [in_vmem()] * 11,
        out_specs=in_vmem(),
        scratch_shapes=work + [pltpu.VMEM((2, 512, D), BF16)],
        compiler_params=params(24),
        cost_estimate=cost(10),
        name="half_windows_inner",
    )(window_keep, keep_above, window_route, image, above, below, above_rest, below_rest, *third)
    merging = (merge_gain[None], merge_bias[None], merge_weight)
    scratch = [
        pltpu.VMEM((4, 32, 128, 128), F32),
        pltpu.VMEM((2, WIN, WIN, E), BF16),
        pltpu.SemaphoreType.DMA((2,)),
    ]
    half_work = work
    work = [
        pltpu.VMEM((512, D), BF16),
        pltpu.VMEM((1536, D), BF16),
        pltpu.VMEM((1536, D), BF16),
        pltpu.VMEM((512, D), BF16),
    ]
    attended = (inner, outer_halves, inner_halves)
    merged, first, second, edges = pl.pallas_call(
        edge_kernel,
        out_shape=(shape(16, 64, E), shape(WIN * WIN, E), shape(WIN * WIN, E), shape(512, D)),
        in_specs=[in_smem()] * 3 + [in_vmem()] * 16,
        out_specs=(in_hbm(),) + (in_vmem(),) * 3,
        scratch_shapes=scratch[:2] + work + scratch[2:],
        compiler_params=params(30),
        cost_estimate=cost(12),
        name="edge_windows",
    )(window_keep, keep_above, window_route, own_left, own_right, far_left, far_right, *attended, *third, *merging)
    incoming_first = shifted(first, "wide", 1)
    incoming_second = shifted(second, "wide", 1)
    merged, left_first, left_second = pl.pallas_call(
        rest_kernel,
        out_shape=(shape(16, 64, E), shape(WIN * WIN, E), shape(WIN * WIN, E)),
        in_specs=[in_smem()] * 3 + [in_hbm()] + [in_vmem()] * 18,
        out_specs=(in_hbm(), in_vmem(), in_vmem()),
        scratch_shapes=scratch + half_work + [pltpu.VMEM((2, 1024, D), BF16), pltpu.VMEM((2, 2, 128, D), BF16)],
        input_output_aliases={3: 0},
        compiler_params=params(24),
        cost_estimate=cost(12),
        name="rest_merging",
    )(
        window_keep,
        keep_above,
        window_route,
        merged,
        image,
        above,
        below,
        above_rest,
        below_rest,
        *attended,
        edges,
        *third,
        *merging,
    )
    own = (first, second, left_first, left_second)
    top = (
        fourth_norm_gain[None],
        fourth_norm_bias[None],
        fourth_in_proj,
        fourth_in_bias,
        fourth_out_proj,
        fourth_out_bias[None],
    )
    scratch = [
        pltpu.VMEM((WIN * WIN, E), BF16),
        pltpu.VMEM((WIN * WIN, E), BF16),
        pltpu.SemaphoreType.DMA,
    ]
    slots = pl.pallas_call(
        top_first,
        out_shape=shape(1, 2, WIN * WIN, E),
        in_specs=[in_smem()] + [in_vmem()] * 11,
        out_specs=in_hbm(),
        scratch_shapes=scratch,
        compiler_params=params(24),
        cost_estimate=cost(8),
        name="top_first",
    )(window_route, *own, incoming_first, *top)
    slots = pl.pallas_call(
        top_second,
        out_shape=shape(1, 2, WIN * WIN, E),
        in_specs=[in_smem()] + [in_vmem()] * 12 + [in_hbm()],
        out_specs=in_hbm(),
        scratch_shapes=scratch,
        input_output_aliases={13: 0},
        compiler_params=params(24),
        cost_estimate=cost(8),
        name="top_second",
    )(window_route, *own, incoming_first, incoming_second, *top, slots)
    return merged, slots


def solution(mesh):
    placed = (
        P("narrow", "wide", None),
        P(),
        P(),
        P(),
        P(),
        P(),
        P(),
        P("narrow", "wide"),
        P(),
        P(),
        P(),
        P(),
        P(),
        P(),
        P(),
        P(),
        P(),
        P("narrow", None),
    )
    return jax.shard_map(
        shards,
        mesh=mesh,
        in_specs=placed,
        out_specs=(P("narrow", "wide", None), P("narrow", "wide", None, None)),
        check_vma=False,
    )
```

```python
import jax
import jax.numpy as jnp
from jax import lax
from jax.experimental import pallas as pl
from jax.experimental.pallas import tpu as pltpu
from jax.sharding import PartitionSpec as P

D = 512
HEADS_D = 16
E = 1024
HEADS_E = 32
WIN = 16
SHIFT = 8
HEAD = 32
PACK = 4
EPSILON = 1e-05
LOG2E = 1.4426950408889634
QSCALE = HEAD ** (-0.5) * LOG2E
BF16 = jnp.bfloat16
F32 = jnp.float32


def matmul(a, b):
    return jnp.dot(a, b, preferred_element_type=F32)


def layer_norm(values, gain, bias):
    center = jnp.mean(values, axis=-1, keepdims=True)
    offsets = values - center
    spread = jnp.mean(offsets * offsets, axis=-1, keepdims=True)
    return (offsets * lax.rsqrt(spread + EPSILON) * gain + bias).astype(BF16)


def attend(q, k, v):
    count = q.shape[0]
    lane = lax.broadcasted_iota(jnp.int32, (count, PACK * HEAD), 1)
    stacked = jnp.concatenate(
        [jnp.where((lane >= HEAD * h) & (lane < HEAD * h + HEAD), q, 0) for h in range(PACK)], axis=0
    )
    scores = lax.dot_general(stacked, k, (((1,), (1,)), ((), ())), preferred_element_type=F32)
    weights = jnp.exp2(scores - jnp.max(scores, axis=1, keepdims=True)).astype(BF16)
    sums = matmul(weights, jnp.concatenate([v, jnp.ones_like(v)], axis=1))
    total = sums[:count]
    lane = lax.broadcasted_iota(jnp.int32, total.shape, 1) % (PACK * HEAD)
    for h in range(1, PACK):
        total = jnp.where(lane >= HEAD * h, sums[count * h : count * (h + 1)], total)
    return (total[:, : PACK * HEAD] / total[:, PACK * HEAD :]).astype(BF16)


def attention_three(tokens, count, refs):
    gain, bias, in_proj, in_bias, out_proj, out_bias = refs
    normed = layer_norm(tokens, gain[...], bias[...])
    q = ((matmul(normed[:count], in_proj[:, :D]) + in_bias[:D][None]) * QSCALE).astype(BF16)
    k = (matmul(normed, in_proj[:, D : 2 * D]) + in_bias[D : 2 * D][None]).astype(BF16)
    v = (matmul(normed, in_proj[:, 2 * D :]) + in_bias[2 * D : 3 * D][None]).astype(BF16)
    width = PACK * HEAD
    context = jnp.concatenate(
        [attend(q[:, c : c + width], k[:, c : c + width], v[:, c : c + width]) for c in range(0, D, width)],
        axis=1,
    )
    return (matmul(context, out_proj[...]) + out_bias[...] + tokens[:count]).astype(BF16)


def column(j):
    return pl.multiple_of(j * WIN, WIN)


def merge_order(route, first):
    wide = lax.axis_index("wide")
    moves = [(route[0, 4 * wide + j] == 2).astype(jnp.int32) for j in range(4)]
    total = moves[0] + moves[1] + moves[2] + moves[3]
    chosen = [0, 0]
    moved, stayed = 0, 0
    for j in range(4):
        position = jnp.where(moves[j] == 1, moved, total + stayed)
        for slot in range(2):
            chosen[slot] = jnp.where(position == first + slot, j, chosen[slot])
        moved = moved + moves[j]
        stayed = stayed + 1 - moves[j]
    return chosen


def needed_first(route, j):
    first = merge_order(route, 0)
    return (j % 2 == 1) | (j == 2 * first[0]) | (j == 2 * first[1])


def strip_kernel(keep, keep_above, image, above, below, left, right):
    for side, out in enumerate((left, right)):
        base, start = (0, 7 * WIN)[side], SHIFT * side
        for pair in range(24):
            rows = []
            for r in (2 * pair, 2 * pair + 1):
                if r < SHIFT:
                    block = above[96 * r + (0, 80)[side] : 96 * r + (16, 96)[side]]
                elif r < 5 * SHIFT:
                    block = image[r - SHIFT, base : base + WIN]
                else:
                    q = r - 5 * SHIFT
                    block = below[96 * q + (0, 80)[side] : 96 * q + (16, 96)[side]]
                rows.append(block.astype(F32)[start : start + SHIFT])
            out[pair] = jnp.concatenate(rows, axis=0).astype(BF16)
    lanes = lax.broadcasted_iota(jnp.int32, (WIN, D), 1)
    flags = jnp.where(lanes == 0, keep_above[1, 7].astype(F32), 0.0)
    for a in range(2):
        flags = jnp.where(lanes == a + 1, keep[a, 7].astype(F32), flags)
    right[24] = flags.astype(BF16)


def inner_kernel(keep, image, gain, bias, in_proj, in_bias, out_proj, out_bias, out):
    refs = (gain, bias, in_proj, in_bias, out_proj, out_bias)

    @pl.loop(0, 7)
    def _(j):
        both = image[SHIFT : SHIFT + WIN, pl.ds(column(j), 2 * WIN), :].astype(F32)
        tokens = both[:, SHIFT : SHIFT + WIN, :].reshape(WIN * WIN, D)

        @pl.when(keep[0, j] == 1)
        def _():
            out[j] = attention_three(tokens, WIN * WIN, refs)

        @pl.when(keep[0, j] != 1)
        def _():
            out[j] = tokens.astype(BF16)


def flag_at(flags, lane):
    lanes = lax.broadcasted_iota(jnp.int32, (WIN, 128), 1)
    return jnp.max(jnp.where(lanes == lane, flags[:, :128].astype(F32), 0.0)) > 0.5


def project(normed, queries, in_proj, in_bias, q_ref, k_ref, v_ref):
    q = (matmul(queries, in_proj[:, :D]) + in_bias[:D][None]) * QSCALE
    q_ref[...] = q.astype(BF16)
    k_ref[...] = (matmul(normed, in_proj[:, D : 2 * D]) + in_bias[D : 2 * D][None]).astype(BF16)
    v_ref[...] = (matmul(normed, in_proj[:, 2 * D :]) + in_bias[2 * D : 3 * D][None]).astype(BF16)


def attend_window(first, count, window, q_ref, k_ref, v_ref, context):
    width = PACK * HEAD
    mine = pl.ds(pl.multiple_of(first, count), count)
    keys = pl.ds(pl.multiple_of(WIN * WIN * window, WIN * WIN), WIN * WIN)
    for c in range(0, D, width):
        cols = slice(c, c + width)
        context[mine, cols] = attend(q_ref[mine, cols], k_ref[keys, cols], v_ref[keys, cols])


def attend_windows(kept, first, count, window, q_ref, k_ref, v_ref, context):
    @pl.loop(0, len(kept))
    def _(i):
        wanted = 0
        for step, flag in enumerate(kept):
            wanted = jnp.where(i == step, flag.astype(jnp.int32), wanted)

        @pl.when(wanted == 1)
        def _():
            attend_window(first + count * i, count, window + i, q_ref, k_ref, v_ref, context)


def half_pair(keep, image, j, far, top_kept, refs, out, step, scratch):
    gain, bias, in_proj, in_bias, out_proj, out_bias = refs
    narrow, rows = lax.axis_index("narrow"), lax.axis_size("narrow")
    q_ref, k_ref, v_ref, context = scratch
    tokens = []
    for side in range(2):
        row = 3 * SHIFT * side
        own = image[row : row + SHIFT, pl.ds(column(j), 2 * WIN), :].astype(F32)
        own = own[:, SHIFT : SHIFT + WIN].reshape(-1, D)
        tokens.append((own, jnp.where(narrow == (0, rows - 1)[side], own, far(side))))
    kept = [top_kept, keep[1, j] == 1]

    @pl.when(kept[0] | kept[1])
    def _():
        normed = [[layer_norm(part, gain[...], bias[...]) for part in pair] for pair in tokens]
        queries = jnp.concatenate([normed[0][0], normed[1][0]], axis=0)
        project(jnp.concatenate(normed[0] + normed[1], axis=0), queries, in_proj, in_bias, q_ref, k_ref, v_ref)

    attend_windows(kept, 0, 128, 0, q_ref, k_ref, v_ref, context)

    @pl.when(kept[0] | kept[1])
    def _():
        result = matmul(context[...], out_proj[...]) + out_bias[...]
        for side in range(2):
            own = tokens[side][0]
            new = own + result[128 * side : 128 * side + 128]
            out[step, side] = jnp.where(kept[side], new, own).astype(BF16)

    @pl.when(jnp.logical_not(kept[0] | kept[1]))
    def _():
        for side in range(2):
            out[step, side] = tokens[side][0].astype(BF16)


def gather_rows(ref, pitch, start):
    rows = [ref[pl.ds(pitch * r + start, 2 * WIN), :].astype(F32)[SHIFT : SHIFT + WIN] for r in range(SHIFT)]
    return jnp.concatenate(rows, axis=0)


def half_outer_kernel(
    keep, keep_above, route, image, above, below, gain, bias, in_proj, in_bias, out_proj, out_bias, out, *scratch
):
    refs = (gain, bias, in_proj, in_bias, out_proj, out_bias)

    @pl.loop(0, 4)
    def _(step):
        late = (step >= 2).astype(jnp.int32)
        j = step + 3 * late
        start = pl.multiple_of((step + late) * WIN, WIN)
        far = lambda side: gather_rows((above, below)[side], 96, start)

        @pl.when(needed_first(route, j))
        def _():
            half_pair(keep, image, j, far, keep_above[1, j] == 1, refs, out, step, scratch)


def half_inner_kernel(
    keep, keep_above, route, image, above, below, above_rest, below_rest, gain, bias, in_proj, in_bias, out_proj, out_bias, out, *scratch
):
    refs = (gain, bias, in_proj, in_bias, out_proj, out_bias)
    rows = scratch[4]
    for side in range(2):
        early, late = (above, below)[side], (above_rest, below_rest)[side]
        for r in range(SHIFT):
            rows[side, 64 * r : 64 * r + 16] = early[96 * r + 32 : 96 * r + 48]
            rows[side, 64 * r + 16 : 64 * r + 48] = late[32 * r : 32 * r + 32]
            rows[side, 64 * r + 48 : 64 * r + 64] = early[96 * r + 48 : 96 * r + 64]

    @pl.loop(0, 3)
    def _(step):
        j = step + 2
        far = lambda side: gather_rows(rows.at[side], 64, column(step))

        @pl.when(needed_first(route, j))
        def _():
            half_pair(keep, image, j, far, keep_above[1, j] == 1, refs, out, step, scratch[:4])


def store(layer, rows, cols, values):
    for c in range(4):
        layer[c, rows, cols, :] = values[:, :, 128 * c : 128 * c + 128]


def lay_out(layer, inner, outer_halves, inner_halves):
    @pl.loop(0, 7)
    def _(j):
        cols = pl.ds(pl.multiple_of(j * WIN + SHIFT, SHIFT), WIN)
        store(layer, slice(SHIFT, SHIFT + WIN), cols, inner[j].astype(F32).reshape(WIN, WIN, D))

    for ref, columns in ((outer_halves, (0, 1, 5, 6)), (inner_halves, (2, 3, 4))):
        for step, j in enumerate(columns):
            cols = slice(j * WIN + SHIFT, j * WIN + SHIFT + WIN)
            for side in range(2):
                rows = slice(3 * SHIFT * side, 3 * SHIFT * side + SHIFT)
                store(layer, rows, cols, ref[step, side].astype(F32).reshape(SHIFT, WIN, D))


def lay_out_edges(layer, edges):
    for side in range(2):
        col = slice(15 * SHIFT * side, 15 * SHIFT * side + SHIFT)
        values = edges[128 * side : 128 * side + 128].astype(F32)
        store(layer, slice(SHIFT, SHIFT + WIN), col, values.reshape(WIN, SHIFT, D))
        for down in range(2):
            row = slice(3 * SHIFT * down, 3 * SHIFT * down + SHIFT)
            first = 256 + 64 * (2 * down + side)
            store(layer, row, col, edges[first : first + 64].astype(F32).reshape(SHIFT, SHIFT, D))


def merge_two(route, start, layer, gain, bias, weight, merged, results, sem, outs):
    chosen = merge_order(route, start)
    blocks = []
    for group in chosen:
        parts = []
        for odd_col in range(2):
            cols = pl.ds(group * 32 + odd_col, WIN, stride=2)
            for odd_row in range(2):
                for c in range(4):
                    parts.append(
                        jnp.concatenate([layer[c, 2 * r + odd_row, cols, :] for r in range(WIN)], axis=0)
                    )
        blocks.append(layer_norm(jnp.concatenate(parts, axis=1), gain[...], bias[...]))
    result = matmul(jnp.concatenate(blocks, axis=0), weight[...]).astype(BF16)
    copies = []
    for slot, group in enumerate(chosen):
        part = result[256 * slot : 256 * slot + 256]
        if outs is not None:
            outs[slot][...] = part
        results[slot] = part.reshape(WIN, WIN, E)
        copy = pltpu.make_async_copy(results.at[slot], merged.at[:, pl.ds(column(group), WIN), :], sem.at[slot])
        copy.start()
        copies.append(copy)
    for copy in copies:
        copy.wait()


def edge_kernel(
    keep,
    keep_above,
    route,
    own_left,
    own_right,
    far_left,
    far_right,
    inner,
    outer_halves,
    inner_halves,
    gain,
    bias,
    in_proj,
    in_bias,
    out_proj,
    out_bias,
    merge_gain,
    merge_bias,
    merge_weight,
    merged,
    first,
    second,
    edges,
    layer,
    results,
    q_ref,
    k_ref,
    v_ref,
    context,
    sem,
):
    narrow, rows = lax.axis_index("narrow"), lax.axis_size("narrow")
    wide, groups = lax.axis_index("wide"), lax.axis_size("wide")
    flags = far_left[24]

    def strip(ref, low, high):
        return ref[low // 2 : high // 2].astype(F32).reshape(-1, D)

    windows = []
    for side in range(2):
        near, far = (own_left, own_right)[side], (far_left, far_right)[side]
        edge_col = wide == (0, groups - 1)[side]
        own = strip(near, 16, 32)
        beside = jnp.where(edge_col, own, strip(far, 16, 32))
        kept = flag_at(flags, 1) if side == 0 else keep[0, 7] == 1
        windows.append((kept, own, [own, beside]))
    for down in range(2):
        for side in range(2):
            near, far = (own_left, own_right)[side], (far_left, far_right)[side]
            edge_col = wide == (0, groups - 1)[side]
            edge_row = narrow == (0, rows - 1)[down]
            mine, beyond = ((8, 0), (32, 40))[down]
            own = strip(near, mine, mine + SHIFT)
            across = jnp.where(edge_row, own, strip(near, beyond, beyond + SHIFT))
            beside = jnp.where(edge_col, own, strip(far, mine, mine + SHIFT))
            corner = strip(far, beyond, beyond + SHIFT)
            corner = jnp.where(edge_col, across, jnp.where(edge_row, beside, corner))
            if side == 0:
                kept = flag_at(flags, 2 * down)
            elif down == 0:
                kept = keep_above[1, 7] == 1
            else:
                kept = keep[1, 7] == 1
            windows.append((kept, own, [own, across, beside, corner]))
    normed = [[layer_norm(part, gain[...], bias[...]) for part in parts] for _, _, parts in windows]
    queries = jnp.concatenate([parts[0] for parts in normed], axis=0)
    normed = jnp.concatenate([part for parts in normed for part in parts], axis=0)
    project(normed, queries, in_proj, in_bias, q_ref, k_ref, v_ref)
    kept = [flag for flag, _, _ in windows]
    attend_windows(kept[:2], 0, 128, 0, q_ref, k_ref, v_ref, context)
    attend_windows(kept[2:], 256, 64, 2, q_ref, k_ref, v_ref, context)
    result = matmul(context[...], out_proj[...]) + out_bias[...]
    place = 0
    for kept, own, _ in windows:
        mine = slice(place, place + own.shape[0])
        edges[mine] = jnp.where(kept, own + result[mine], own).astype(BF16)
        place += own.shape[0]
    lay_out(layer, inner, outer_halves, inner_halves)
    lay_out_edges(layer, edges)
    merge_two(route, 0, layer, merge_gain, merge_bias, merge_weight, merged, results, sem, (first, second))


def rest_kernel(
    keep,
    keep_above,
    route,
    earlier,
    image,
    above,
    below,
    above_rest,
    below_rest,
    inner,
    outer_halves,
    inner_halves,
    edges,
    gain,
    bias,
    in_proj,
    in_bias,
    out_proj,
    out_bias,
    merge_gain,
    merge_bias,
    merge_weight,
    merged,
    third,
    fourth,
    layer,
    results,
    sem,
    q_ref,
    k_ref,
    v_ref,
    context,
    rows,
    out,
):
    refs = (gain, bias, in_proj, in_bias, out_proj, out_bias)
    for side in range(2):
        early, late = (above, below)[side], (above_rest, below_rest)[side]
        for r in range(SHIFT):
            rows[side, 128 * r : 128 * r + 48] = early[96 * r : 96 * r + 48]
            rows[side, 128 * r + 48 : 128 * r + 80] = late[32 * r : 32 * r + 32]
            rows[side, 128 * r + 80 : 128 * r + 128] = early[96 * r + 48 : 96 * r + 96]
    lay_out(layer, inner, outer_halves, inner_halves)
    lay_out_edges(layer, edges)
    left = merge_order(route, 2)

    @pl.loop(0, 2)
    def _(step):
        j = 2 * jnp.where(step == 0, left[0], left[1])
        far = lambda side: gather_rows(rows.at[side], 128, column(j))
        half_pair(
            keep, image, j, far, keep_above[1, j] == 1, refs, out, step, (q_ref, k_ref, v_ref, context)
        )
        cols = pl.ds(pl.multiple_of(j * WIN + SHIFT, SHIFT), WIN)
        for side in range(2):
            where = slice(3 * SHIFT * side, 3 * SHIFT * side + SHIFT)
            store(layer, where, cols, out[step, side].astype(F32).reshape(SHIFT, WIN, D))

    merge_two(route, 2, layer, merge_gain, merge_bias, merge_weight, merged, results, sem, (third, fourth))


def top_kernel(slot, route, own, incoming, gain, bias, in_proj, in_bias, out_proj, out_bias, *rest):
    out, tokens_ref, result, sem = rest[-4:]
    wide, groups = lax.axis_index("wide"), lax.axis_size("wide")
    before = jnp.where(wide == 0, groups - 1, wide - 1)
    homes = 0
    arriving = 0
    chosen = 0
    for j in range(4):
        stays = route[0, 4 * wide + j] == 1
        chosen = jnp.where(stays & (homes == slot), j, chosen)
        homes = homes + stays.astype(jnp.int32)
        arriving = arriving + (route[0, 4 * before + j] == 2).astype(jnp.int32)
    order = merge_order(route, 0) + merge_order(route, 2)
    width = PACK * HEAD
    filled = slot < homes + arriving

    for position in range(4):

        @pl.when((slot < homes) & (order[position] == chosen))
        def _():
            tokens_ref[...] = own[position][...]

    for source in range(slot + 1):

        @pl.when(homes + source == slot)
        def _():
            tokens_ref[...] = incoming[source][...]

    @pl.when(filled)
    def _():
        tokens = tokens_ref[...].astype(F32)
        normed = layer_norm(tokens, gain[...], bias[...])
        context = []
        for c in range(0, E, 2 * width):
            cols = slice(c, c + 2 * width)
            q = ((matmul(normed, in_proj[:, cols]) + in_bias[cols][None]) * QSCALE).astype(BF16)
            cols = slice(E + c, E + c + 2 * width)
            k = (matmul(normed, in_proj[:, cols]) + in_bias[cols][None]).astype(BF16)
            cols = slice(2 * E + c, 2 * E + c + 2 * width)
            v = (matmul(normed, in_proj[:, cols]) + in_bias[cols][None]).astype(BF16)
            for a in (0, width):
                context.append(attend(q[:, a : a + width], k[:, a : a + width], v[:, a : a + width]))
        value = matmul(jnp.concatenate(context, axis=1), out_proj[...]) + out_bias[...] + tokens
        result[...] = value.astype(BF16)

    @pl.when(jnp.logical_not(filled))
    def _():
        result[...] = jnp.zeros((WIN * WIN, E), BF16)

    copy = pltpu.make_async_copy(result, out.at[0, slot], sem)
    copy.start()
    copy.wait()


def top_first(route, first, second, third, fourth, one, *rest):
    top_kernel(0, route, (first, second, third, fourth), (one,), *rest)


def top_second(route, first, second, third, fourth, one, two, *rest):
    top_kernel(1, route, (first, second, third, fourth), (one, two), *rest)


def in_smem():
    return pl.BlockSpec(memory_space=pltpu.SMEM)


def in_vmem():
    return pl.BlockSpec(memory_space=pltpu.VMEM)


def in_hbm():
    return pl.BlockSpec(memory_space=pltpu.HBM)


def shifted(block, axis, distance):
    count = lax.axis_size(axis)
    return lax.ppermute(block, axis, [((i - distance) % count, i) for i in range(count)])


def shape(*sizes):
    return jax.ShapeDtypeStruct(sizes, BF16)


def params(mib):
    return pltpu.CompilerParams(vmem_limit_bytes=mib * 2**20)


def cost(us):
    return pl.CostEstimate(flops=us * 10**9, bytes_accessed=4_000_000, transcendentals=0)


def shards(
    image,
    third_norm_gain,
    third_norm_bias,
    third_in_proj,
    third_in_bias,
    third_out_proj,
    third_out_bias,
    window_keep,
    merge_gain,
    merge_bias,
    merge_weight,
    fourth_norm_gain,
    fourth_norm_bias,
    fourth_in_proj,
    fourth_in_bias,
    fourth_out_proj,
    fourth_out_bias,
    window_route,
):
    low, high = 3 * WIN, 5 * WIN

    def row_parts(rows):
        early = jnp.concatenate([rows[:, :low], rows[:, high:]], axis=1)
        return early.reshape(-1, D), rows[:, low:high].reshape(-1, D)

    keep_above = shifted(window_keep, "narrow", 1)
    send_down, send_down_rest = row_parts(image[3 * SHIFT :])
    send_up, send_up_rest = row_parts(image[:SHIFT])
    above = shifted(send_down, "narrow", 1)
    below = shifted(send_up, "narrow", -1)
    third = (
        third_norm_gain[None],
        third_norm_bias[None],
        third_in_proj,
        third_in_bias,
        third_out_proj,
        third_out_bias[None],
    )
    inner = pl.pallas_call(
        inner_kernel,
        out_shape=shape(7, WIN * WIN, D),
        in_specs=[in_smem()] + [in_vmem()] * 7,
        out_specs=in_vmem(),
        compiler_params=params(24),
        cost_estimate=cost(18),
        name="inner_windows",
    )(window_keep, image, *third)

    above, below, send_down_rest, send_up_rest = lax.optimization_barrier(
        (above, below, send_down_rest, send_up_rest)
    )
    own_left, own_right = pl.pallas_call(
        strip_kernel,
        out_shape=(shape(24, WIN, D), shape(25, WIN, D)),
        in_specs=[in_smem()] * 2 + [in_vmem()] * 3,
        out_specs=(in_vmem(),) * 2,
        compiler_params=params(12),
        cost_estimate=cost(1),
        name="pack_columns",
    )(window_keep, keep_above, image, above, below)
    above, below, own_left, own_right = lax.optimization_barrier((above, below, own_left, own_right))
    above_rest = shifted(send_down_rest, "narrow", 1)
    below_rest = shifted(send_up_rest, "narrow", -1)
    far_left = shifted(own_right, "wide", 1)
    far_right = shifted(own_left, "wide", -1)
    work = [
        pltpu.VMEM((256, D), BF16),
        pltpu.VMEM((512, D), BF16),
        pltpu.VMEM((512, D), BF16),
        pltpu.VMEM((256, D), BF16),
    ]
    outer_halves = pl.pallas_call(
        half_outer_kernel,
        out_shape=shape(4, 2, 128, D),
        in_specs=[in_smem()] * 3 + [in_vmem()] * 9,
        out_specs=in_vmem(),
        scratch_shapes=work,
        compiler_params=params(24),
        cost_estimate=cost(14),
        name="half_windows_outer",
    )(window_keep, keep_above, window_route, image, above, below, *third)
    inner_halves = pl.pallas_call(
        half_inner_kernel,
        out_shape=shape(3, 2, 128, D),
        in_specs=[in_smem()] * 3 + [in_vmem()] * 11,
        out_specs=in_vmem(),
        scratch_shapes=work + [pltpu.VMEM((2, 512, D), BF16)],
        compiler_params=params(24),
        cost_estimate=cost(10),
        name="half_windows_inner",
    )(window_keep, keep_above, window_route, image, above, below, above_rest, below_rest, *third)
    merging = (merge_gain[None], merge_bias[None], merge_weight)
    scratch = [
        pltpu.VMEM((4, 32, 128, 128), F32),
        pltpu.VMEM((2, WIN, WIN, E), BF16),
        pltpu.SemaphoreType.DMA((2,)),
    ]
    half_work = work
    work = [
        pltpu.VMEM((512, D), BF16),
        pltpu.VMEM((1536, D), BF16),
        pltpu.VMEM((1536, D), BF16),
        pltpu.VMEM((512, D), BF16),
    ]
    attended = (inner, outer_halves, inner_halves)
    merged, first, second, edges = pl.pallas_call(
        edge_kernel,
        out_shape=(shape(16, 64, E), shape(WIN * WIN, E), shape(WIN * WIN, E), shape(512, D)),
        in_specs=[in_smem()] * 3 + [in_vmem()] * 16,
        out_specs=(in_hbm(),) + (in_vmem(),) * 3,
        scratch_shapes=scratch[:2] + work + scratch[2:],
        compiler_params=params(30),
        cost_estimate=cost(12),
        name="edge_windows",
    )(window_keep, keep_above, window_route, own_left, own_right, far_left, far_right, *attended, *third, *merging)
    incoming_first = shifted(first, "wide", 1)
    incoming_second = shifted(second, "wide", 1)
    merged, left_first, left_second = pl.pallas_call(
        rest_kernel,
        out_shape=(shape(16, 64, E), shape(WIN * WIN, E), shape(WIN * WIN, E)),
        in_specs=[in_smem()] * 3 + [in_hbm()] + [in_vmem()] * 18,
        out_specs=(in_hbm(), in_vmem(), in_vmem()),
        scratch_shapes=scratch + half_work + [pltpu.VMEM((2, 1024, D), BF16), pltpu.VMEM((2, 2, 128, D), BF16)],
        input_output_aliases={3: 0},
        compiler_params=params(24),
        cost_estimate=cost(12),
        name="rest_merging",
    )(
        window_keep,
        keep_above,
        window_route,
        merged,
        image,
        above,
        below,
        above_rest,
        below_rest,
        *attended,
        edges,
        *third,
        *merging,
    )
    own = (first, second, left_first, left_second)
    top = (
        fourth_norm_gain[None],
        fourth_norm_bias[None],
        fourth_in_proj,
        fourth_in_bias,
        fourth_out_proj,
        fourth_out_bias[None],
    )
    scratch = [
        pltpu.VMEM((WIN * WIN, E), BF16),
        pltpu.VMEM((WIN * WIN, E), BF16),
        pltpu.SemaphoreType.DMA,
    ]
    slots = pl.pallas_call(
        top_first,
        out_shape=shape(1, 2, WIN * WIN, E),
        in_specs=[in_smem()] + [in_vmem()] * 11,
        out_specs=in_hbm(),
        scratch_shapes=scratch,
        compiler_params=params(24),
        cost_estimate=cost(8),
        name="top_first",
    )(window_route, *own, incoming_first, *top)
    slots = pl.pallas_call(
        top_second,
        out_shape=shape(1, 2, WIN * WIN, E),
        in_specs=[in_smem()] + [in_vmem()] * 12 + [in_hbm()],
        out_specs=in_hbm(),
        scratch_shapes=scratch,
        input_output_aliases={13: 0},
        compiler_params=params(24),
        cost_estimate=cost(8),
        name="top_second",
    )(window_route, *own, incoming_first, incoming_second, *top, slots)
    return merged, slots


def solution(mesh):
    placed = (
        P("narrow", "wide", None),
        P(),
        P(),
        P(),
        P(),
        P(),
        P(),
        P("narrow", "wide"),
        P(),
        P(),
        P(),
        P(),
        P(),
        P(),
        P(),
        P(),
        P(),
        P("narrow", None),
    )
    return jax.shard_map(
        shards,
        mesh=mesh,
        in_specs=placed,
        out_specs=(P("narrow", "wide", None), P("narrow", "wide", None, None)),
        check_vma=False,
    )
```
